32 devices in a mesh: qa: 2 (over y), qb: 16 (over z, x, core).
Axes of the slice: x: 2, y: 2, z: 4, core: 2. Of those that a mesh axis runs over, the one named last changes fastest.
Arguments:
- state: float32 [2, 2, 16, 65536], P(None, 'qa', 'qb'), may hold values from -6 to 6
- adjoint: float32 [2, 2, 16, 65536], P(None, 'qa', 'qb'), may hold values from -6 to 6
- gates: float32 [8, 2, 128, 128], replicated, may hold values from -1 to 1, as said below
Outputs:
- state_out: float32 [2, 2, 16, 65536], P(None, 'qa', 'qb')
- adjoint_out: float32 [2, 2, 16, 65536], P(None, 'qa', 'qb')
- gate_grads: float32 [8, 2, 128, 128], replicated
The draws below stay inside these ranges and needn't reach their ends.
Inputs may be any that keep to these rules, and one draw needn't show every extreme that they name: gates[k, 0] + i gates[k, 1] is a unitary 128 x 128 matrix for every k.
All inputs are finite; a program needn't handle non-finite values.
Results may differ from the reference program's by a relative error of at most 0.0001.
Values sent between devices are 32-bit elements; how exact they have to be, the bound alone decides.
No kernel may reach another device: no remote copies, remote signals or barrier semaphores. Data moves between devices by JAX's collectives and lax.ppermute only.
A program may use at most 64 MiB of HBM per device.

```python
import math
import jax
import jax.numpy as jnp
from jax import lax

GATE_DIM = 128
AMP_DEV = 65536
GATES = 8
N_QA = 2
N_QB = 16


precise = lax.Precision.HIGHEST


def complex_dot(left_real, left_imag, right_real, right_imag):
    out_real = jnp.dot(left_real, right_real, precision=precise) - jnp.dot(left_imag, right_imag, precision=precise)
    out_imag = jnp.dot(left_real, right_imag, precision=precise) + jnp.dot(left_imag, right_real, precision=precise)
    return (out_real, out_imag)


def one_unitary(subkey):
    phases = jax.random.uniform(subkey, (3, GATE_DIM), jnp.float32, -math.pi, math.pi)
    indices = jnp.arange(GATE_DIM, dtype=jnp.int32)
    product = indices[:, None] * indices[None, :] % GATE_DIM
    angles = product.astype(jnp.float32) * (-2.0 * math.pi / GATE_DIM)
    norming = 1.0 / math.sqrt(GATE_DIM)
    dft_real = jnp.cos(angles) * norming
    dft_imag = jnp.sin(angles) * norming
    cosines = jnp.cos(phases)
    sines = jnp.sin(phases)
    mat_real = dft_real * cosines[2][None, :] - dft_imag * sines[2][None, :]
    mat_imag = dft_real * sines[2][None, :] + dft_imag * cosines[2][None, :]
    rot_real = cosines[1][:, None] * mat_real - sines[1][:, None] * mat_imag
    rot_imag = cosines[1][:, None] * mat_imag + sines[1][:, None] * mat_real
    mat_real, mat_imag = complex_dot(dft_real, dft_imag, rot_real, rot_imag)
    fin_real = cosines[0][:, None] * mat_real - sines[0][:, None] * mat_imag
    fin_imag = cosines[0][:, None] * mat_imag + sines[0][:, None] * mat_real
    return jnp.stack([fin_real, fin_imag])


def draw_gates(key, part):
    subkeys = jax.random.split(jax.random.fold_in(key, 17), GATES)
    return jax.vmap(one_unitary)(subkeys).astype(jnp.float32)


def level_of(rng, shape, shards, low, top_value):
    gain, own = 1.0, jax.random.fold_in(rng, 6)
    for position, shards_of in shards:
        draws = jnp.exp(jax.random.uniform(jax.random.fold_in(own, position), (shards_of,), jnp.float32, low / len(shards), top_value / len(shards)))
        gain = gain * jnp.repeat(draws, shape[position] // shards_of).reshape([-1 if axis == position else 1 for axis in range(len(shape))])
    return gain


def noise(rng, extent, width, reach, pieces=(), kind=jnp.bfloat16):
    gain = level_of(rng, extent, pieces, -0.22, 0.18) if pieces else 1.0
    result = jax.random.normal(rng, extent, jnp.float32) * width * gain
    return jnp.minimum(jnp.maximum(result, -reach), reach).astype(kind)


def setup_inputs(seed: int = 0) -> dict:
    splits = jax.random.split(jax.random.key(seed), 4)
    state = noise(splits[0], (2, N_QA, N_QB, AMP_DEV), 1.0, 6.0, ((1, 2), (2, 16)), jnp.float32)
    adjoint = noise(splits[1], (2, N_QA, N_QB, AMP_DEV), 1.0, 6.0, ((1, 2), (2, 16)), jnp.float32)
    gates = draw_gates(jax.random.fold_in(splits[3], 71), 0)
    return dict(state=state, adjoint=adjoint, gates=gates)


precise = lax.Precision.HIGHEST


def undo_high(real_part, imag_part, gate_real, gate_imag):
    shape = real_part.shape
    gate_size = gate_real.shape[0]
    folded = (shape[0] * shape[1], gate_size, shape[2] // gate_size)
    fold_real = real_part.reshape(folded)
    fold_imag = imag_part.reshape(folded)

    def mixing(matrix, field):
        return jnp.einsum('hg,phm->pgm', matrix, field, precision=precise)

    new_real = mixing(gate_real, fold_real) + mixing(gate_imag, fold_imag)
    new_imag = mixing(gate_real, fold_imag) - mixing(gate_imag, fold_real)
    return new_real.reshape(shape), new_imag.reshape(shape)


def undo_low(real_part, imag_part, gate_real, gate_imag):
    shape = real_part.shape
    gate_size = gate_real.shape[0]
    fold_real = real_part.reshape(-1, gate_size)
    fold_imag = imag_part.reshape(-1, gate_size)

    def mixing(field, matrix):
        return jnp.einsum('rh,hg->rg', field, matrix, precision=precise)

    new_real = mixing(fold_real, gate_real) + mixing(fold_imag, gate_imag)
    new_imag = mixing(fold_imag, gate_real) - mixing(fold_real, gate_imag)
    return new_real.reshape(shape), new_imag.reshape(shape)


def pair_high(adjoint_real, adjoint_imag, new_real, new_imag, gate_size):
    shape = adjoint_real.shape
    folded = (shape[0] * shape[1], gate_size, shape[2] // gate_size)

    def inner(left, right):
        return jnp.einsum('pgm,phm->gh', left.reshape(folded), right.reshape(folded), precision=precise)

    grad_real = inner(adjoint_real, new_real) + inner(adjoint_imag, new_imag)
    grad_imag = inner(adjoint_imag, new_real) - inner(adjoint_real, new_imag)
    return jnp.stack([grad_real, grad_imag])


def pair_low(adjoint_real, adjoint_imag, new_real, new_imag, gate_size):
    def inner(left, right):
        return jnp.einsum('rg,rh->gh', left.reshape(-1, gate_size), right.reshape(-1, gate_size), precision=precise)

    grad_real = inner(adjoint_real, new_real) + inner(adjoint_imag, new_imag)
    grad_imag = inner(adjoint_imag, new_real) - inner(adjoint_real, new_imag)
    return jnp.stack([grad_real, grad_imag])


def swap_first(field):
    shape = field.shape
    return field.reshape(shape[0], shape[1], shape[0], shape[2] // shape[0]).transpose(2, 1, 0, 3).reshape(shape)


def swap_second(field):
    shape = field.shape
    return field.reshape(shape[0], shape[1], shape[1], shape[2] // shape[1]).transpose(0, 2, 1, 3).reshape(shape)


def reference(state, adjoint, gates):
    state_real, state_imag = state[0], state[1]
    adjoint_real, adjoint_imag = adjoint[0], adjoint[1]
    gate_size = gates.shape[-1]
    scaling = float(N_QA * N_QB * AMP_DEV // GATE_DIM) ** -0.5
    collected = []
    for index in range(GATES):
        gate_real = gates[index, 0]
        gate_imag = gates[index, 1]
        if index % 2 == 0:
            new_real, new_imag = undo_high(state_real, state_imag, gate_real, gate_imag)
            collected.append(scaling * pair_high(adjoint_real, adjoint_imag, new_real, new_imag, gate_size))
            adjoint_real, adjoint_imag = undo_high(adjoint_real, adjoint_imag, gate_real, gate_imag)
        else:
            new_real, new_imag = undo_low(state_real, state_imag, gate_real, gate_imag)
            collected.append(scaling * pair_low(adjoint_real, adjoint_imag, new_real, new_imag, gate_size))
            adjoint_real, adjoint_imag = undo_low(adjoint_real, adjoint_imag, gate_real, gate_imag)
        state_real, state_imag = new_real, new_imag
        if index % 2 == 1:
            if (index // 2) % 2 == 0:
                permute = swap_first
            else:
                permute = swap_second
            state_real = permute(state_real)
            state_imag = permute(state_imag)
            adjoint_real = permute(adjoint_real)
            adjoint_imag = permute(adjoint_imag)
    state_out = jnp.stack([state_real, state_imag])
    adjoint_out = jnp.stack([adjoint_real, adjoint_imag])
    return state_out, adjoint_out, jnp.stack(collected)
```

```python
import jax
import jax.numpy as jnp
from jax import lax
from jax.sharding import PartitionSpec as P

precise = lax.Precision.HIGH
AXES = ("qa", "qb")


def mul(left, right):
    dot = lambda i, j: jnp.matmul(left[i], right[j], precision=lax.Precision.HIGHEST)
    return jnp.stack([dot(0, 0) - dot(1, 1), dot(0, 1) + dot(1, 0)])


def mul_adjoint(left, right):
    dot = lambda i, j: lax.dot_general(
        left[i], right[j], (((0,), (0,)), ((), ())), precision=lax.Precision.HIGHEST
    )
    return jnp.stack([dot(0, 0) + dot(1, 1), dot(0, 1) - dot(1, 0)])


def embed(gate):
    real, imag = gate[0], gate[1]
    return jnp.concatenate(
        [jnp.concatenate([real, -imag], 1), jnp.concatenate([imag, real], 1)], 0
    )


def undo(fields, gate):
    kinds, parts, size, rest = fields.shape
    flat = fields.reshape(kinds, parts * size, rest)
    done = jnp.einsum("kg,fkn->fgn", embed(gate), flat, precision=precise)
    return done.reshape(fields.shape)


def pair(fields):
    kinds, parts, size, rest = fields.shape
    flat = fields.reshape(kinds, parts * size, rest)
    both = jnp.einsum("gn,hn->gh", flat[1], flat[0], precision=precise)
    both = both.reshape(parts, size, parts, size)
    return jnp.stack([both[0, :, 0] + both[1, :, 1], both[1, :, 0] - both[0, :, 1]])


def contract(left, right, left_dim, right_dim):
    return lax.dot_general(
        left,
        right,
        (((left_dim,), (right_dim,)), ((), ())),
        precision=lax.Precision.HIGHEST,
        preferred_element_type=jnp.float32,
    )


def undo_high(field, gate):
    new_real = contract(gate[0], field[0], 0, 0) + contract(gate[1], field[1], 0, 0)
    new_imag = contract(gate[0], field[1], 0, 0) - contract(gate[1], field[0], 0, 0)
    return jnp.stack([new_real, new_imag])


def undo_low(field, gate):
    new_real = contract(field[0], gate[0], 1, 0) + contract(field[1], gate[1], 1, 0)
    new_imag = contract(field[1], gate[0], 1, 0) - contract(field[0], gate[1], 1, 0)
    return jnp.stack([new_real, new_imag])


def pair_high(adjoint_field, new_field):
    grad_real = contract(adjoint_field[0], new_field[0], 1, 1) + contract(
        adjoint_field[1], new_field[1], 1, 1
    )
    grad_imag = contract(adjoint_field[1], new_field[0], 1, 1) - contract(
        adjoint_field[0], new_field[1], 1, 1
    )
    return jnp.stack([grad_real, grad_imag])


def pair_low(adjoint_field, new_field):
    grad_real = contract(adjoint_field[0], new_field[0], 0, 0) + contract(
        adjoint_field[1], new_field[1], 0, 0
    )
    grad_imag = contract(adjoint_field[1], new_field[0], 0, 0) - contract(
        adjoint_field[0], new_field[1], 0, 0
    )
    return jnp.stack([grad_real, grad_imag])


def stepwise(state, adjoint, gates):
    gate_size = gates.shape[-1]
    local_count = state.shape[-1]
    scaling = float(lax.axis_size("qa") * lax.axis_size("qb") * local_count // gate_size) ** (-0.5)
    state_now = state.reshape(2, local_count)
    adjoint_now = adjoint.reshape(2, local_count)
    collected = []

    def record(term):
        return lax.psum(term, ("qa", "qb"))

    for section in range(gates.shape[0] // 2):
        high_gate = gates[2 * section]
        low_gate = gates[2 * section + 1]
        upright = (2, gate_size, local_count // gate_size)
        state_high = state_now.reshape(upright)
        adjoint_high = adjoint_now.reshape(upright)
        state_new = undo_high(state_high, high_gate)
        collected.append(record(scaling * pair_high(adjoint_high, state_new)))
        adjoint_new = undo_high(adjoint_high, high_gate)
        flat = (2, local_count // gate_size, gate_size)
        state_low = state_new.reshape(flat)
        adjoint_low = adjoint_new.reshape(flat)
        groups = lax.axis_size("qa") if section % 2 == 0 else lax.axis_size("qb")
        state_done = undo_low(state_low, low_gate)
        collected.append(record(scaling * pair_low(adjoint_low, state_done)))
        adjoint_done = undo_low(adjoint_low, low_gate)
        split = (2, groups, local_count // groups)
        outgoing = (state_done.reshape(split), adjoint_done.reshape(split))
        if section % 2 == 0:
            arrived = (
                lax.all_to_all(outgoing[0], "qa", split_axis=1, concat_axis=1, tiled=True),
                lax.all_to_all(outgoing[1], "qa", split_axis=1, concat_axis=1, tiled=True),
            )
        else:
            arrived = (
                lax.all_to_all(outgoing[0], "qb", split_axis=1, concat_axis=1, tiled=True),
                lax.all_to_all(outgoing[1], "qb", split_axis=1, concat_axis=1, tiled=True),
            )
        state_now = arrived[0].reshape(2, local_count)
        adjoint_now = arrived[1].reshape(2, local_count)
    gradients = jnp.stack(collected)
    return (state_now.reshape(state.shape), adjoint_now.reshape(adjoint.shape), gradients)


def shards(state, adjoint, gates):
    size = gates.shape[-1]
    count = state.shape[-1]
    na, nb = lax.axis_size("qa"), lax.axis_size("qb")
    total = na * nb
    scaling = float(total * count // size) ** (-0.5)
    rest = count // size
    kept = rest // total
    inner, tail = nb // na, size // nb
    if inner * kept != size:
        return stepwise(state, adjoint, gates)

    fields = jnp.stack([state.reshape(2, count), adjoint.reshape(2, count)])
    chain = [gates[1]]
    for index in range(3, gates.shape[0], 2):
        chain.append(mul(chain[-1], gates[index]))

    low = fields.reshape(2, 2, rest, size).transpose(0, 1, 3, 2)
    sum_low = pair(low)
    low = undo(low, chain[-1])
    high = low.transpose(0, 1, 3, 2).reshape(2, 2, size, rest)
    sum_0 = pair(high)
    high = undo(high, gates[0])

    out = high.reshape(2, 2, size, total, kept).transpose(3, 0, 1, 4, 2)
    got = lax.all_to_all(out, AXES, split_axis=0, concat_axis=0, tiled=True)
    got = got.reshape(na, na, inner, 2, 2, kept, na, inner, tail)
    now = jnp.einsum("aBbfpsHht->fpahtHBbs", got)
    dims = now.shape
    now = now.reshape(2, 2, size, -1)
    sum_2 = pair(now)
    now = undo(now, gates[2]).reshape(dims)
    now = jnp.einsum("fpahtHBbs->fpBbtaHhs", now)
    dims = now.shape
    now = now.reshape(2, 2, size, -1)
    sum_4 = pair(now)
    now = undo(now, gates[4]).reshape(dims)
    now = jnp.einsum("fpBbtaHhs->fpHbtBahs", now)
    dims = now.shape
    now = now.reshape(2, 2, size, -1)
    sum_6 = pair(now)
    now = undo(now, gates[6]).reshape(dims)
    out = jnp.einsum("fpHbtBahs->BHbfpahts", now).reshape(total, -1, size)
    got = lax.all_to_all(out, AXES, split_axis=0, concat_axis=0, tiled=True)
    got = got.reshape(total, 2, 2, na, inner, tail, kept)
    done = jnp.einsum("dfpahts->fpahtds", got).reshape(2, 2, 1, 1, count)

    sums = lax.psum(jnp.stack([sum_low, sum_0, sum_2, sum_4, sum_6]), AXES) * scaling
    grads = []
    for index in range(gates.shape[0]):
        if index % 2 == 0:
            grads.append(mul(sums[1 + index // 2], gates[index]))
        elif index == 1:
            grads.append(mul(sums[0], chain[0]))
        else:
            place = index // 2
            grads.append(mul_adjoint(chain[place - 1], mul(sums[0], chain[place])))
    return done[0], done[1], jnp.stack(grads)


def solution(mesh):
    in_specs = (P(None, "qa", "qb", None), P(None, "qa", "qb", None), P())
    out_specs = (P(None, "qa", "qb", None), P(None, "qa", "qb", None), P())
    return jax.shard_map(shards, mesh=mesh, in_specs=in_specs, out_specs=out_specs, check_vma=False)
```

```python
import functools

import jax
import jax.numpy as jnp
from jax import lax
from jax.experimental import pallas as pl
from jax.experimental.pallas import tpu as pltpu
from jax.sharding import PartitionSpec as P

AXES = ("qa", "qb")
NN = (((1,), (0,)), ((), ()))
NT = (((1,), (1,)), ((), ()))
TN = (((0,), (0,)), ((), ()))


def contract(left, right, left_dim, right_dim):
    return lax.dot_general(
        left,
        right,
        (((left_dim,), (right_dim,)), ((), ())),
        precision=lax.Precision.HIGHEST,
        preferred_element_type=jnp.float32,
    )


def undo_high(field, gate):
    new_real = contract(gate[0], field[0], 0, 0) + contract(gate[1], field[1], 0, 0)
    new_imag = contract(gate[0], field[1], 0, 0) - contract(gate[1], field[0], 0, 0)
    return jnp.stack([new_real, new_imag])


def undo_low(field, gate):
    new_real = contract(field[0], gate[0], 1, 0) + contract(field[1], gate[1], 1, 0)
    new_imag = contract(field[1], gate[0], 1, 0) - contract(field[0], gate[1], 1, 0)
    return jnp.stack([new_real, new_imag])


def pair_high(adjoint_field, new_field):
    grad_real = contract(adjoint_field[0], new_field[0], 1, 1) + contract(
        adjoint_field[1], new_field[1], 1, 1
    )
    grad_imag = contract(adjoint_field[1], new_field[0], 1, 1) - contract(
        adjoint_field[0], new_field[1], 1, 1
    )
    return jnp.stack([grad_real, grad_imag])


def pair_low(adjoint_field, new_field):
    grad_real = contract(adjoint_field[0], new_field[0], 0, 0) + contract(
        adjoint_field[1], new_field[1], 0, 0
    )
    grad_imag = contract(adjoint_field[1], new_field[0], 0, 0) - contract(
        adjoint_field[0], new_field[1], 0, 0
    )
    return jnp.stack([grad_real, grad_imag])


def stepwise(state, adjoint, gates):
    gate_size = gates.shape[-1]
    local_count = state.shape[-1]
    scaling = float(lax.axis_size("qa") * lax.axis_size("qb") * local_count // gate_size) ** (-0.5)
    state_now = state.reshape(2, local_count)
    adjoint_now = adjoint.reshape(2, local_count)
    collected = []

    def record(term):
        return lax.psum(term, ("qa", "qb"))

    for section in range(gates.shape[0] // 2):
        high_gate = gates[2 * section]
        low_gate = gates[2 * section + 1]
        upright = (2, gate_size, local_count // gate_size)
        state_high = state_now.reshape(upright)
        adjoint_high = adjoint_now.reshape(upright)
        state_new = undo_high(state_high, high_gate)
        collected.append(record(scaling * pair_high(adjoint_high, state_new)))
        adjoint_new = undo_high(adjoint_high, high_gate)
        flat = (2, local_count // gate_size, gate_size)
        state_low = state_new.reshape(flat)
        adjoint_low = adjoint_new.reshape(flat)
        groups = lax.axis_size("qa") if section % 2 == 0 else lax.axis_size("qb")
        state_done = undo_low(state_low, low_gate)
        collected.append(record(scaling * pair_low(adjoint_low, state_done)))
        adjoint_done = undo_low(adjoint_low, low_gate)
        split = (2, groups, local_count // groups)
        outgoing = (state_done.reshape(split), adjoint_done.reshape(split))
        if section % 2 == 0:
            arrived = (
                lax.all_to_all(outgoing[0], "qa", split_axis=1, concat_axis=1, tiled=True),
                lax.all_to_all(outgoing[1], "qa", split_axis=1, concat_axis=1, tiled=True),
            )
        else:
            arrived = (
                lax.all_to_all(outgoing[0], "qb", split_axis=1, concat_axis=1, tiled=True),
                lax.all_to_all(outgoing[1], "qb", split_axis=1, concat_axis=1, tiled=True),
            )
        state_now = arrived[0].reshape(2, local_count)
        adjoint_now = arrived[1].reshape(2, local_count)
    gradients = jnp.stack(collected)
    return (state_now.reshape(state.shape), adjoint_now.reshape(adjoint.shape), gradients)


def split(x):
    high = x.astype(jnp.bfloat16)
    return high, (x - high.astype(jnp.float32)).astype(jnp.bfloat16)


def dot(left, right, dims):
    part = lambda i, j: lax.dot_general(left[i], right[j], dims, preferred_element_type=jnp.float32)
    return (part(0, 1) + part(1, 0)) + part(0, 0)


def each(operation, *arrays):
    return tuple(operation(*parts) for parts in zip(*arrays))


def wide(arrays):
    return jnp.concatenate(arrays, 1)


def tall(arrays):
    return jnp.concatenate(arrays, 0)


def multiply(left, right):
    size = left[0].shape[0]
    both = dot(split(tall(left)), split(wide(right)), NN)
    return (
        both[:size, :size] - both[size:, size:],
        both[:size, size:] + both[size:, :size],
    )


def multiply_adjoint(left, right):
    size = left[0].shape[0]
    both = dot(split(tall((left[0].T, left[1].T))), split(wide(right)), NN)
    return (
        both[:size, :size] + both[size:, size:],
        both[:size, size:] - both[size:, :size],
    )


def undoing(gate):
    real, imag = gate[0].T, gate[1].T
    return split(tall((wide((real, imag)), wide((-imag, real)))))


def paired(both):
    size = both.shape[0] // 2
    return tall((both[:size, :size] + both[size:, size:], both[size:, :size] - both[:size, size:]))


def exchange(parts, width):
    parts = list(parts)
    lanes = parts[0].shape[-1]
    lane = lax.broadcasted_iota(jnp.int32, parts[0].shape, 1)
    step = 1
    while step < len(parts):
        shift = step * width
        lower = (lane // shift) % 2 == 0
        for index in range(len(parts)):
            if index & step == 0:
                one, two = parts[index], parts[index + step]
                parts[index] = jnp.where(lower, one, pltpu.roll(two, shift, 1))
                parts[index + step] = jnp.where(lower, pltpu.roll(one, lanes - shift, 1), two)
        step *= 2
    return parts


def first_kernel(state_ref, adjoint_ref, gates_ref, out_ref, chain_ref):
    size = gates_ref.shape[-1]
    mid = state_ref.shape[1] // size
    total = out_ref.shape[0]
    kept = mid * size // total
    blocks = size // kept
    gate = lambda index: (gates_ref[index, 0], gates_ref[index, 1])

    two = multiply(gate(1), gate(3))
    three = multiply(two, gate(5))
    four = multiply(two, multiply(gate(5), gate(7)))
    for place, product in enumerate((two, three, four)):
        chain_ref[place, 0] = product[0]
        chain_ref[place, 1] = product[1]
    undo_low = undoing(four)
    undo_high = undoing(gate(0))

    fields = [
        [
            [split(ref[part, pl.ds(j, size, stride=mid), :]) for part in range(2)]
            for j in range(mid)
        ]
        for ref in (state_ref, adjoint_ref)
    ]
    by_low = [each(lambda *a: tall(a), *[each(lambda *b: wide(b), *row) for row in field]) for field in fields]
    sums = [paired(dot(by_low[1], by_low[0], TN))]
    by_high = [
        each(lambda *a: tall(a), *[each(lambda *b: wide(b), *[row[part] for row in field]) for part in range(2)])
        for field in fields
    ]
    sums.append(paired(dot(by_high[1], by_high[0], NT)))
    done = [dot(undo_high, field, NN) for field in by_high]
    for j in range(mid):
        here = slice(j * size, (j + 1) * size)
        rows = tall([wide((field[:size, here], field[size:, here])) for field in done])
        sent = dot(undo_low, split(rows), NT)
        for block in range(blocks):
            for f in range(2):
                for part in range(2):
                    start = part * size + block * kept
                    out_ref[j * blocks + block, pl.ds((f * 2 + part) * kept, kept), :] = sent[
                        start : start + kept, f * size : (f + 1) * size
                    ]
    base = 4 * kept
    share = 2 * size // total
    for device in range(total):
        for place, term in enumerate(sums):
            out_ref[device, pl.ds(base + place * share, share), :] = term[
                device * share : (device + 1) * share
            ]


def second_kernel(na, got_ref, gates_ref, out_ref):
    size = gates_ref.shape[-1]
    total = got_ref.shape[0]
    nb = total // na
    inner = nb // na
    tail = size // nb
    kept = size // inner
    share = 2 * size // total
    gate = lambda index: (gates_ref[index, 0], gates_ref[index, 1])

    fields = []
    for f in range(2):
        parts = []
        for part in range(2):
            start = (f * 2 + part) * kept
            rows = [got_ref[pl.ds(a * nb, nb), pl.ds(start, kept), :].reshape(nb * kept, size) for a in range(na)]
            parts.append(tall(exchange(rows, size // na)))
        fields.append(split(wide(parts)))
    sums = [paired(dot(fields[1], fields[0], TN))]
    undo = undoing(gate(2))
    after = []
    for f in range(2):
        done = dot(undo, fields[f], NT)
        after.append(done)
    lists = []
    for h in range(inner):
        pieces = []
        for f in range(2):
            for block in range(na * na):
                cut = after[f][:, block * size : (block + 1) * size]
                pieces.append(cut.reshape(2 * na, inner, tail, size)[:, h].reshape(2 * na * tail, size))
        lists.append(tall(pieces))
    turned = exchange(lists, kept)
    turned = [item.reshape(2, na, na, 2, na, tail, size) for item in turned]

    fields = []
    for f in range(2):
        columns = []
        for top in range(na):
            for a in range(na):
                rows = [
                    turned[b][f, top, B, part, a]
                    for part in range(2)
                    for B in range(na)
                    for b in range(inner)
                ]
                columns.append(tall(rows))
        fields.append(split(wide(columns)))
    sums.append(paired(dot(fields[1], fields[0], NT)))
    undo = undoing(gate(4))
    after = [dot(undo, field, NN) for field in fields]

    span = inner * tail
    fields = []
    for f in range(2):
        columns = []
        for a in range(na):
            for B in range(na):
                rows = []
                for part in range(2):
                    for top in range(na):
                        row = (part * na + B) * span
                        column = (top * na + a) * size
                        rows.append(after[f][row : row + span, column : column + size])
                columns.append(tall(rows))
        fields.append(split(wide(columns)))
    sums.append(paired(dot(fields[1], fields[0], NT)))
    undo = undoing(gate(6))
    for f in range(2):
        done = dot(undo, fields[f], NN)
        for part in range(2):
            for a in range(na):
                for B in range(na):
                    column = (a * na + B) * size
                    for top in range(na):
                        for b in range(inner):
                            row = ((part * na + top) * inner + b) * tail
                            out_ref[
                                (B * na + top) * inner + b,
                                pl.ds(((f * 2 + part) * na + a) * tail, tail),
                                :,
                            ] = done[row : row + tail, column : column + size]

    base = 4 * kept
    for device in range(total):
        for place, term in enumerate(sums):
            out_ref[device, pl.ds(base + place * share, share), :] = term[
                device * share : (device + 1) * share
            ]
    early = 2 * share
    summed = jnp.sum(got_ref[:, pl.ds(base, early), :], 0)
    for device in range(total):
        out_ref[device, pl.ds(base + 3 * share, early), :] = summed


def third_kernel(na, nb, got_ref, state_ref, adjoint_ref, late_ref):
    total, _, size = got_ref.shape
    rest = state_ref.shape[1]
    mid = rest // size
    inner = nb // na
    tail = size // nb
    kept = size // inner
    blocks = total // mid
    share = 2 * size // total
    for j in range(mid):
        lists = [
            got_ref[j * blocks + block, pl.ds(0, 4 * kept), :] for block in range(blocks)
        ]
        turned = exchange(lists, kept)
        for h in range(inner):
            for f, ref in enumerate((state_ref, adjoint_ref)):
                for part in range(2):
                    for a in range(na):
                        row = ((f * 2 + part) * na + a) * tail
                        ref[part, pl.ds(((a * inner + h) * tail) * mid + j, tail, stride=mid), :] = turned[h][
                            row : row + tail
                        ]
    late_ref[...] = jnp.sum(got_ref[:, pl.ds(4 * kept, 3 * share), :], 0)


def fourth_kernel(scaling, early_ref, late_ref, gates_ref, chain_ref, out_ref):
    size = gates_ref.shape[-1]
    total = early_ref.shape[0]
    share = 2 * size // total
    gate = lambda index: (gates_ref[index, 0], gates_ref[index, 1])

    def sums(ref, place):
        rows = ref[:, pl.ds(place * share, share), :].reshape(2 * size, size) * scaling
        return rows[:size], rows[size:]

    low = sums(early_ref, 0)
    chain = [gate(1)] + [(chain_ref[place, 0], chain_ref[place, 1]) for place in range(3)]
    for index in range(8):
        if index % 2:
            grad = multiply(low, chain[index // 2])
            if index > 1:
                grad = multiply_adjoint(chain[index // 2 - 1], grad)
        elif index == 0:
            grad = multiply(sums(early_ref, 1), gate(0))
        else:
            grad = multiply(sums(late_ref, index // 2 - 1), gate(index))
        out_ref[index, 0] = grad[0]
        out_ref[index, 1] = grad[1]


def shards(state, adjoint, gates):
    size = gates.shape[-1]
    count = state.shape[-1]
    na, nb = lax.axis_size("qa"), lax.axis_size("qb")
    total = na * nb
    scaling = float(total * count // size) ** (-0.5)
    rest = count // size
    kept = rest // total
    inner, tail = nb // na, size // nb
    share = 2 * size // total
    if gates.shape[0] != 8 or inner * kept != size or tail != 8 or share != 8:
        return stepwise(state, adjoint, gates)

    params = pltpu.CompilerParams(vmem_limit_bytes=48 * 2**20)
    shape = lambda *dims: jax.ShapeDtypeStruct(dims, jnp.float32)
    flat = (2, rest, size)
    out, chain = pl.pallas_call(
        first_kernel,
        out_shape=(shape(total, 4 * kept + 2 * share, size), shape(3, 2, size, size)),
        compiler_params=params,
        name="first",
    )(state.reshape(flat), adjoint.reshape(flat), gates)
    got = lax.all_to_all(out, AXES, split_axis=0, concat_axis=0, tiled=True)
    out = pl.pallas_call(
        functools.partial(second_kernel, na),
        out_shape=shape(total, 4 * kept + 5 * share, size),
        compiler_params=params,
        name="second",
    )(got, gates)
    got = lax.all_to_all(out, AXES, split_axis=0, concat_axis=0, tiled=True)
    state_out, adjoint_out, late = pl.pallas_call(
        functools.partial(third_kernel, na, nb),
        out_shape=(shape(*flat), shape(*flat), shape(3 * share, size)),
        compiler_params=params,
        name="third",
    )(got)
    late = jnp.broadcast_to(late, (total, *late.shape))
    late = lax.all_to_all(late, AXES, split_axis=0, concat_axis=0, tiled=True)
    grads = pl.pallas_call(
        functools.partial(fourth_kernel, scaling),
        out_shape=shape(*gates.shape),
        compiler_params=params,
        name="fourth",
    )(got[:, 4 * kept + 3 * share :], late, gates, chain)
    return state_out.reshape(state.shape), adjoint_out.reshape(adjoint.shape), grads


def solution(mesh):
    in_specs = (P(None, "qa", "qb", None), P(None, "qa", "qb", None), P())
    out_specs = (P(None, "qa", "qb", None), P(None, "qa", "qb", None), P())
    return jax.shard_map(shards, mesh=mesh, in_specs=in_specs, out_specs=out_specs, check_vma=False)
```

```python
import functools

import jax
import jax.numpy as jnp
from jax import lax
from jax.experimental import pallas as pl
from jax.experimental.pallas import tpu as pltpu
from jax.sharding import PartitionSpec as P

AXES = ("qa", "qb")
NN = (((1,), (0,)), ((), ()))
NT = (((1,), (1,)), ((), ()))
TN = (((0,), (0,)), ((), ()))


def contract(left, right, left_dim, right_dim):
    return lax.dot_general(
        left,
        right,
        (((left_dim,), (right_dim,)), ((), ())),
        precision=lax.Precision.HIGHEST,
        preferred_element_type=jnp.float32,
    )


def undo_high(field, gate):
    new_real = contract(gate[0], field[0], 0, 0) + contract(gate[1], field[1], 0, 0)
    new_imag = contract(gate[0], field[1], 0, 0) - contract(gate[1], field[0], 0, 0)
    return jnp.stack([new_real, new_imag])


def undo_low(field, gate):
    new_real = contract(field[0], gate[0], 1, 0) + contract(field[1], gate[1], 1, 0)
    new_imag = contract(field[1], gate[0], 1, 0) - contract(field[0], gate[1], 1, 0)
    return jnp.stack([new_real, new_imag])


def pair_high(adjoint_field, new_field):
    grad_real = contract(adjoint_field[0], new_field[0], 1, 1) + contract(
        adjoint_field[1], new_field[1], 1, 1
    )
    grad_imag = contract(adjoint_field[1], new_field[0], 1, 1) - contract(
        adjoint_field[0], new_field[1], 1, 1
    )
    return jnp.stack([grad_real, grad_imag])


def pair_low(adjoint_field, new_field):
    grad_real = contract(adjoint_field[0], new_field[0], 0, 0) + contract(
        adjoint_field[1], new_field[1], 0, 0
    )
    grad_imag = contract(adjoint_field[1], new_field[0], 0, 0) - contract(
        adjoint_field[0], new_field[1], 0, 0
    )
    return jnp.stack([grad_real, grad_imag])


def stepwise(state, adjoint, gates):
    gate_size = gates.shape[-1]
    local_count = state.shape[-1]
    scaling = float(lax.axis_size("qa") * lax.axis_size("qb") * local_count // gate_size) ** (-0.5)
    state_now = state.reshape(2, local_count)
    adjoint_now = adjoint.reshape(2, local_count)
    collected = []

    def record(term):
        return lax.psum(term, ("qa", "qb"))

    for section in range(gates.shape[0] // 2):
        high_gate = gates[2 * section]
        low_gate = gates[2 * section + 1]
        upright = (2, gate_size, local_count // gate_size)
        state_high = state_now.reshape(upright)
        adjoint_high = adjoint_now.reshape(upright)
        state_new = undo_high(state_high, high_gate)
        collected.append(record(scaling * pair_high(adjoint_high, state_new)))
        adjoint_new = undo_high(adjoint_high, high_gate)
        flat = (2, local_count // gate_size, gate_size)
        state_low = state_new.reshape(flat)
        adjoint_low = adjoint_new.reshape(flat)
        groups = lax.axis_size("qa") if section % 2 == 0 else lax.axis_size("qb")
        state_done = undo_low(state_low, low_gate)
        collected.append(record(scaling * pair_low(adjoint_low, state_done)))
        adjoint_done = undo_low(adjoint_low, low_gate)
        split = (2, groups, local_count // groups)
        outgoing = (state_done.reshape(split), adjoint_done.reshape(split))
        if section % 2 == 0:
            arrived = (
                lax.all_to_all(outgoing[0], "qa", split_axis=1, concat_axis=1, tiled=True),
                lax.all_to_all(outgoing[1], "qa", split_axis=1, concat_axis=1, tiled=True),
            )
        else:
            arrived = (
                lax.all_to_all(outgoing[0], "qb", split_axis=1, concat_axis=1, tiled=True),
                lax.all_to_all(outgoing[1], "qb", split_axis=1, concat_axis=1, tiled=True),
            )
        state_now = arrived[0].reshape(2, local_count)
        adjoint_now = arrived[1].reshape(2, local_count)
    gradients = jnp.stack(collected)
    return (state_now.reshape(state.shape), adjoint_now.reshape(adjoint.shape), gradients)


def split(x):
    high = x.astype(jnp.bfloat16)
    return high, (x - high.astype(jnp.float32)).astype(jnp.bfloat16)


def dot(left, right, dims):
    part = lambda i, j: lax.dot_general(left[i], right[j], dims, preferred_element_type=jnp.float32)
    return (part(0, 1) + part(1, 0)) + part(0, 0)


def each(operation, *arrays):
    return tuple(operation(*parts) for parts in zip(*arrays))


def wide(arrays):
    return jnp.concatenate(arrays, 1)


def tall(arrays):
    return jnp.concatenate(arrays, 0)


def multiply(left, right):
    size = left[0].shape[0]
    both = dot(split(tall(left)), split(wide(right)), NN)
    return (
        both[:size, :size] - both[size:, size:],
        both[:size, size:] + both[size:, :size],
    )


def multiply_adjoint(left, right):
    size = left[0].shape[0]
    both = dot(split(tall((left[0].T, left[1].T))), split(wide(right)), NN)
    return (
        both[:size, :size] + both[size:, size:],
        both[:size, size:] - both[size:, :size],
    )


def undoing(gate):
    real, imag = gate[0].T, gate[1].T
    return split(tall((wide((real, imag)), wide((-imag, real)))))


def paired(both):
    size = both.shape[0] // 2
    return tall((both[:size, :size] + both[size:, size:], both[size:, :size] - both[:size, size:]))


def exchange(parts, width):
    parts = list(parts)
    lanes = parts[0].shape[-1]
    lane = lax.broadcasted_iota(jnp.int32, parts[0].shape, 1)
    step = 1
    while step < len(parts):
        shift = step * width
        lower = (lane // shift) % 2 == 0
        for index in range(len(parts)):
            if index & step == 0:
                one, two = parts[index], parts[index + step]
                parts[index] = jnp.where(lower, one, pltpu.roll(two, shift, 1))
                parts[index + step] = jnp.where(lower, pltpu.roll(one, lanes - shift, 1), two)
        step *= 2
    return parts


def share_out(sums, place_ref, refs, all_ref):
    for index, term in enumerate(sums):
        all_ref[index] = term
    rows = all_ref.shape[1] // len(refs)
    for mask, ref in enumerate(refs):
        start = pl.multiple_of(lax.bitwise_xor(place_ref[0], mask) * rows, rows)
        for index in range(len(sums)):
            ref[pl.ds(index * rows, rows), :] = all_ref[index, pl.ds(start, rows), :]


def collect(place_ref, refs, all_ref):
    rows = all_ref.shape[1] // len(refs)
    for mask, ref in enumerate(refs):
        start = pl.multiple_of(lax.bitwise_xor(place_ref[0], mask) * rows, rows)
        for index in range(all_ref.shape[0]):
            all_ref[index, pl.ds(start, rows), :] = ref[pl.ds(index * rows, rows), :]


def first_kernel(place_ref, state_ref, adjoint_ref, gates_ref, out_ref, *refs):
    size = gates_ref.shape[-1]
    mid = state_ref.shape[1] // size
    total = out_ref.shape[0]
    kept = mid * size // total
    blocks = size // kept
    gate = lambda index: (gates_ref[index, 0], gates_ref[index, 1])

    four = multiply(multiply(gate(1), gate(3)), multiply(gate(5), gate(7)))
    undo_low = undoing(four)
    undo_high = undoing(gate(0))

    fields = [
        [
            [split(ref[part, pl.ds(j, size, stride=mid), :]) for part in range(2)]
            for j in range(mid)
        ]
        for ref in (state_ref, adjoint_ref)
    ]
    by_low = [each(lambda *a: tall(a), *[each(lambda *b: wide(b), *row) for row in field]) for field in fields]
    sums = [paired(dot(by_low[1], by_low[0], TN))]
    by_high = [
        each(lambda *a: tall(a), *[each(lambda *b: wide(b), *[row[part] for row in field]) for part in range(2)])
        for field in fields
    ]
    sums.append(paired(dot(by_high[1], by_high[0], NT)))
    done = [dot(undo_high, field, NN) for field in by_high]
    for j in range(mid):
        here = slice(j * size, (j + 1) * size)
        rows = tall([wide((field[:size, here], field[size:, here])) for field in done])
        sent = dot(undo_low, split(rows), NT)
        for block in range(blocks):
            for f in range(2):
                for part in range(2):
                    start = part * size + block * kept
                    out_ref[j * blocks + block, pl.ds((f * 2 + part) * kept, kept), :] = sent[
                        start : start + kept, f * size : (f + 1) * size
                    ]
    share_out(sums, place_ref, refs[:-1], refs[-1])


def second_kernel(na, place_ref, got_ref, gates_ref, out_ref, *refs):
    size = gates_ref.shape[-1]
    total = got_ref.shape[0]
    nb = total // na
    inner = nb // na
    tail = size // nb
    kept = size // inner
    gate = lambda index: (gates_ref[index, 0], gates_ref[index, 1])

    fields = []
    for f in range(2):
        parts = []
        for part in range(2):
            start = (f * 2 + part) * kept
            rows = [got_ref[pl.ds(a * nb, nb), pl.ds(start, kept), :].reshape(nb * kept, size) for a in range(na)]
            parts.append(tall(exchange(rows, size // na)))
        fields.append(split(wide(parts)))
    sums = [paired(dot(fields[1], fields[0], TN))]
    undo = undoing(gate(2))
    after = []
    for f in range(2):
        done = dot(undo, fields[f], NT)
        after.append(done)
    lists = []
    for h in range(inner):
        pieces = []
        for f in range(2):
            for block in range(na * na):
                cut = after[f][:, block * size : (block + 1) * size]
                pieces.append(cut.reshape(2 * na, inner, tail, size)[:, h].reshape(2 * na * tail, size))
        lists.append(tall(pieces))
    turned = exchange(lists, kept)
    turned = [item.reshape(2, na, na, 2, na, tail, size) for item in turned]

    fields = []
    for f in range(2):
        columns = []
        for top in range(na):
            for a in range(na):
                rows = [
                    turned[b][f, top, B, part, a]
                    for part in range(2)
                    for B in range(na)
                    for b in range(inner)
                ]
                columns.append(tall(rows))
        fields.append(split(wide(columns)))
    sums.append(paired(dot(fields[1], fields[0], NT)))
    undo = undoing(gate(4))
    after = [dot(undo, field, NN) for field in fields]

    span = inner * tail
    fields = []
    for f in range(2):
        columns = []
        for a in range(na):
            for B in range(na):
                rows = []
                for part in range(2):
                    for top in range(na):
                        row = (part * na + B) * span
                        column = (top * na + a) * size
                        rows.append(after[f][row : row + span, column : column + size])
                columns.append(tall(rows))
        fields.append(split(wide(columns)))
    sums.append(paired(dot(fields[1], fields[0], NT)))
    undo = undoing(gate(6))
    for f in range(2):
        done = dot(undo, fields[f], NN)
        for part in range(2):
            for a in range(na):
                for B in range(na):
                    column = (a * na + B) * size
                    for top in range(na):
                        for b in range(inner):
                            row = ((part * na + top) * inner + b) * tail
                            out_ref[
                                (B * na + top) * inner + b,
                                pl.ds(((f * 2 + part) * na + a) * tail, tail),
                                :,
                            ] = done[row : row + tail, column : column + size]

    share_out(sums, place_ref, refs[:-1], refs[-1])


def third_kernel(na, nb, got_ref, state_ref, adjoint_ref):
    total, _, size = got_ref.shape
    rest = state_ref.shape[1]
    mid = rest // size
    inner = nb // na
    tail = size // nb
    kept = size // inner
    blocks = total // mid
    for j in range(mid):
        lists = [
            got_ref[j * blocks + block, pl.ds(0, 4 * kept), :] for block in range(blocks)
        ]
        turned = exchange(lists, kept)
        for h in range(inner):
            for f, ref in enumerate((state_ref, adjoint_ref)):
                for part in range(2):
                    for a in range(na):
                        row = ((f * 2 + part) * na + a) * tail
                        ref[part, pl.ds(((a * inner + h) * tail) * mid + j, tail, stride=mid), :] = turned[h][
                            row : row + tail
                        ]


def early_kernel(scaling, place_ref, gates_ref, *refs):
    *refs, out_ref, all_ref = refs
    size = gates_ref.shape[-1]
    gate = lambda index: (gates_ref[index, 0], gates_ref[index, 1])
    collect(place_ref, refs, all_ref)
    sums = lambda place: (all_ref[place, :size] * scaling, all_ref[place, size:] * scaling)
    grads = {0: multiply(sums(1), gate(0))}
    low = sums(0)
    for index in range(1, gates_ref.shape[0], 2):
        grads[index] = multiply(low, gate(index))
        low = multiply_adjoint(gate(index), grads[index])
    for index, grad in grads.items():
        out_ref[index, 0] = grad[0]
        out_ref[index, 1] = grad[1]


def late_kernel(scaling, place_ref, gates_ref, *refs):
    *refs, _, out_ref, all_ref, grad_ref, sem = refs
    size = gates_ref.shape[-1]
    collect(place_ref, refs, all_ref)
    copies = []
    for place in range(all_ref.shape[0]):
        index = 2 * place + 2
        sums = (all_ref[place, :size] * scaling, all_ref[place, size:] * scaling)
        grad = multiply(sums, (gates_ref[index, 0], gates_ref[index, 1]))
        grad_ref[place, 0] = grad[0]
        grad_ref[place, 1] = grad[1]
        copies.append(pltpu.make_async_copy(grad_ref.at[place], out_ref.at[index], sem.at[place]))
        copies[-1].start()
    for copy in copies:
        copy.wait()


def from_mask(value, mask, total):
    return lax.ppermute(value, AXES, [(device, device ^ mask) for device in range(total)])


def tree(terms):
    while len(terms) > 1:
        terms = [one + two for one, two in zip(terms[::2], terms[1::2])]
    return terms[0]


def reduce_all(chunks, near, far, total):
    own = tree([chunks[0]] + [from_mask(chunk, mask, total) for chunk, mask in zip(chunks[1:], near[1:])])
    own = tree([own] + [from_mask(own, mask, total) for mask in far[1:]])
    return [own] + [from_mask(own, mask, total) for mask in near[1:]]


def shards(state, adjoint, gates):
    size = gates.shape[-1]
    count = state.shape[-1]
    na, nb = lax.axis_size("qa"), lax.axis_size("qb")
    total = na * nb
    scaling = float(total * count // size) ** (-0.5)
    rest = count // size
    kept = rest // total
    inner, tail = nb // na, size // nb
    if gates.shape[0] != 8 or inner * kept != size or tail != 8:
        return stepwise(state, adjoint, gates)

    low = 1 << ((nb.bit_length() - 1) // 2)
    near = [a * nb + b for a in range(na) for b in range(low)]
    far = [b * low for b in range(nb // low)]
    place = (lax.axis_index("qa") * low + lax.bitwise_and(lax.axis_index("qb"), low - 1)).astype(jnp.int32).reshape(1)

    shape = lambda *dims: jax.ShapeDtypeStruct(dims, jnp.float32)
    flat = (2, rest, size)
    rows = 2 * size // len(near)
    smem = pl.BlockSpec(memory_space=pltpu.SMEM)
    vmem = pl.BlockSpec(memory_space=pltpu.VMEM)
    anywhere = pl.BlockSpec(memory_space=pl.ANY)

    def call(kernel, name, out_shape, scratch=(), **options):
        return pl.pallas_call(
            kernel,
            out_shape=out_shape,
            scratch_shapes=scratch,
            compiler_params=pltpu.CompilerParams(vmem_limit_bytes=48 * 2**20),
            name=name,
            **options,
        )

    out, *chunks = call(
        first_kernel,
        "first",
        [shape(total, 4 * kept, size)] + [shape(2 * rows, size) for _ in near],
        [pltpu.VMEM((2, 2 * size, size), jnp.float32)],
        in_specs=[smem, vmem, vmem, vmem],
    )(place, state.reshape(flat), adjoint.reshape(flat), gates)
    got = lax.all_to_all(out, AXES, split_axis=0, concat_axis=0, tiled=True)
    chunks = reduce_all(chunks, near, far, total)
    early = call(
        functools.partial(early_kernel, scaling),
        "early",
        shape(*gates.shape),
        [pltpu.VMEM((2, 2 * size, size), jnp.float32)],
        in_specs=[smem] + [vmem] * (1 + len(chunks)),
    )(place, gates, *chunks)
    out, *chunks = call(
        functools.partial(second_kernel, na),
        "second",
        [shape(total, 4 * kept, size)] + [shape(3 * rows, size) for _ in near],
        [pltpu.VMEM((3, 2 * size, size), jnp.float32)],
        in_specs=[smem, vmem, vmem],
    )(place, got, gates)
    got = lax.all_to_all(out, AXES, split_axis=0, concat_axis=0, tiled=True)
    chunks = reduce_all(chunks, near, far, total)
    state_out, adjoint_out = call(
        functools.partial(third_kernel, na, nb), "third", (shape(*flat), shape(*flat))
    )(got)
    grads = call(
        functools.partial(late_kernel, scaling),
        "late",
        shape(*gates.shape),
        [
            pltpu.VMEM((3, 2 * size, size), jnp.float32),
            pltpu.VMEM((3, 2, size, size), jnp.float32),
            pltpu.SemaphoreType.DMA((3,)),
        ],
        in_specs=[smem] + [vmem] * (1 + len(chunks)) + [anywhere],
        out_specs=anywhere,
        input_output_aliases={2 + len(chunks): 0},
    )(place, gates, *chunks, early)
    return state_out.reshape(state.shape), adjoint_out.reshape(adjoint.shape), grads


def solution(mesh):
    in_specs = (P(None, "qa", "qb", None), P(None, "qa", "qb", None), P())
    out_specs = (P(None, "qa", "qb", None), P(None, "qa", "qb", None), P())
    return jax.shard_map(shards, mesh=mesh, in_specs=in_specs, out_specs=out_specs, check_vma=False)
```

```python
import functools

import jax
import jax.numpy as jnp
from jax import lax
from jax.experimental import pallas as pl
from jax.experimental.pallas import tpu as pltpu
from jax.sharding import PartitionSpec as P

AXES = ("qa", "qb")
NN = (((1,), (0,)), ((), ()))
NT = (((1,), (1,)), ((), ()))
TN = (((0,), (0,)), ((), ()))


def contract(left, right, left_dim, right_dim):
    return lax.dot_general(
        left,
        right,
        (((left_dim,), (right_dim,)), ((), ())),
        precision=lax.Precision.HIGHEST,
        preferred_element_type=jnp.float32,
    )


def undo_high(field, gate):
    new_real = contract(gate[0], field[0], 0, 0) + contract(gate[1], field[1], 0, 0)
    new_imag = contract(gate[0], field[1], 0, 0) - contract(gate[1], field[0], 0, 0)
    return jnp.stack([new_real, new_imag])


def undo_low(field, gate):
    new_real = contract(field[0], gate[0], 1, 0) + contract(field[1], gate[1], 1, 0)
    new_imag = contract(field[1], gate[0], 1, 0) - contract(field[0], gate[1], 1, 0)
    return jnp.stack([new_real, new_imag])


def pair_high(adjoint_field, new_field):
    grad_real = contract(adjoint_field[0], new_field[0], 1, 1) + contract(
        adjoint_field[1], new_field[1], 1, 1
    )
    grad_imag = contract(adjoint_field[1], new_field[0], 1, 1) - contract(
        adjoint_field[0], new_field[1], 1, 1
    )
    return jnp.stack([grad_real, grad_imag])


def pair_low(adjoint_field, new_field):
    grad_real = contract(adjoint_field[0], new_field[0], 0, 0) + contract(
        adjoint_field[1], new_field[1], 0, 0
    )
    grad_imag = contract(adjoint_field[1], new_field[0], 0, 0) - contract(
        adjoint_field[0], new_field[1], 0, 0
    )
    return jnp.stack([grad_real, grad_imag])


def stepwise(state, adjoint, gates):
    gate_size = gates.shape[-1]
    local_count = state.shape[-1]
    scaling = float(lax.axis_size("qa") * lax.axis_size("qb") * local_count // gate_size) ** (-0.5)
    state_now = state.reshape(2, local_count)
    adjoint_now = adjoint.reshape(2, local_count)
    collected = []

    def record(term):
        return lax.psum(term, ("qa", "qb"))

    for section in range(gates.shape[0] // 2):
        high_gate = gates[2 * section]
        low_gate = gates[2 * section + 1]
        upright = (2, gate_size, local_count // gate_size)
        state_high = state_now.reshape(upright)
        adjoint_high = adjoint_now.reshape(upright)
        state_new = undo_high(state_high, high_gate)
        collected.append(record(scaling * pair_high(adjoint_high, state_new)))
        adjoint_new = undo_high(adjoint_high, high_gate)
        flat = (2, local_count // gate_size, gate_size)
        state_low = state_new.reshape(flat)
        adjoint_low = adjoint_new.reshape(flat)
        groups = lax.axis_size("qa") if section % 2 == 0 else lax.axis_size("qb")
        state_done = undo_low(state_low, low_gate)
        collected.append(record(scaling * pair_low(adjoint_low, state_done)))
        adjoint_done = undo_low(adjoint_low, low_gate)
        split = (2, groups, local_count // groups)
        outgoing = (state_done.reshape(split), adjoint_done.reshape(split))
        if section % 2 == 0:
            arrived = (
                lax.all_to_all(outgoing[0], "qa", split_axis=1, concat_axis=1, tiled=True),
                lax.all_to_all(outgoing[1], "qa", split_axis=1, concat_axis=1, tiled=True),
            )
        else:
            arrived = (
                lax.all_to_all(outgoing[0], "qb", split_axis=1, concat_axis=1, tiled=True),
                lax.all_to_all(outgoing[1], "qb", split_axis=1, concat_axis=1, tiled=True),
            )
        state_now = arrived[0].reshape(2, local_count)
        adjoint_now = arrived[1].reshape(2, local_count)
    gradients = jnp.stack(collected)
    return (state_now.reshape(state.shape), adjoint_now.reshape(adjoint.shape), gradients)


def split(x):
    high = x.astype(jnp.bfloat16)
    return high, (x - high.astype(jnp.float32)).astype(jnp.bfloat16)


def dot(left, right, dims):
    part = lambda i, j: lax.dot_general(left[i], right[j], dims, preferred_element_type=jnp.float32)
    return (part(0, 1) + part(1, 0)) + part(0, 0)


def each(operation, *arrays):
    return tuple(operation(*parts) for parts in zip(*arrays))


def wide(arrays):
    return jnp.concatenate(arrays, 1)


def tall(arrays):
    return jnp.concatenate(arrays, 0)


def multiply(left, right):
    size = left[0].shape[0]
    both = dot(split(tall(left)), split(wide(right)), NN)
    return (
        both[:size, :size] - both[size:, size:],
        both[:size, size:] + both[size:, :size],
    )


def multiply_adjoint(left, right):
    size = left[0].shape[0]
    both = dot(split(tall((left[0].T, left[1].T))), split(wide(right)), NN)
    return (
        both[:size, :size] + both[size:, size:],
        both[:size, size:] - both[size:, :size],
    )


def undoing(gate):
    real, imag = gate[0].T, gate[1].T
    return split(tall((wide((real, imag)), wide((-imag, real)))))


def paired(both):
    size = both.shape[0] // 2
    return tall((both[:size, :size] + both[size:, size:], both[size:, :size] - both[:size, size:]))


def exchange(parts, width):
    parts = list(parts)
    lanes = parts[0].shape[-1]
    lane = lax.broadcasted_iota(jnp.int32, parts[0].shape, 1)
    step = 1
    while step < len(parts):
        shift = step * width
        lower = (lane // shift) % 2 == 0
        for index in range(len(parts)):
            if index & step == 0:
                one, two = parts[index], parts[index + step]
                parts[index] = jnp.where(lower, one, pltpu.roll(two, shift, 1))
                parts[index + step] = jnp.where(lower, pltpu.roll(one, lanes - shift, 1), two)
        step *= 2
    return parts


def share_out(sums, place_ref, refs, all_ref):
    for index, term in enumerate(sums):
        all_ref[index] = term
    count, rows = refs[0].shape[0], refs[0].shape[1] // len(sums)
    for other, ref in enumerate(refs):
        half = lax.bitwise_xor(place_ref[0], other)
        for mask in range(count):
            chunk = half * count + lax.bitwise_xor(place_ref[1], mask)
            start = pl.multiple_of(chunk * rows, rows)
            for index in range(len(sums)):
                ref[mask, pl.ds(index * rows, rows), :] = all_ref[index, pl.ds(start, rows), :]


def collect(place_ref, refs, all_ref):
    sums, count, rows = all_ref.shape[0], refs[0].shape[0], refs[0].shape[1] // all_ref.shape[0]
    for other, ref in enumerate(refs):
        half = lax.bitwise_xor(place_ref[0], other)
        for mask in range(count):
            chunk = half * count + lax.bitwise_xor(place_ref[1], mask)
            start = pl.multiple_of(chunk * rows, rows)
            for index in range(sums):
                all_ref[index, pl.ds(start, rows), :] = ref[mask, pl.ds(index * rows, rows), :]


def first_kernel(state_ref, adjoint_ref, gates_ref, out_ref, sums_ref):
    size = gates_ref.shape[-1]
    mid = state_ref.shape[1] // size
    total = out_ref.shape[0]
    kept = mid * size // total
    blocks = size // kept
    gate = lambda index: (gates_ref[index, 0], gates_ref[index, 1])

    four = multiply(multiply(gate(1), gate(3)), multiply(gate(5), gate(7)))
    undo_low = undoing(four)
    undo_high = undoing(gate(0))

    fields = [
        [
            [split(ref[part, pl.ds(j, size, stride=mid), :]) for part in range(2)]
            for j in range(mid)
        ]
        for ref in (state_ref, adjoint_ref)
    ]
    by_low = [each(lambda *a: tall(a), *[each(lambda *b: wide(b), *row) for row in field]) for field in fields]
    sums = [paired(dot(by_low[1], by_low[0], TN))]
    by_high = [
        each(lambda *a: tall(a), *[each(lambda *b: wide(b), *[row[part] for row in field]) for part in range(2)])
        for field in fields
    ]
    sums.append(paired(dot(by_high[1], by_high[0], NT)))
    done = [dot(undo_high, field, NN) for field in by_high]
    for j in range(mid):
        here = slice(j * size, (j + 1) * size)
        rows = tall([wide((field[:size, here], field[size:, here])) for field in done])
        sent = dot(undo_low, split(rows), NT)
        for block in range(blocks):
            for f in range(2):
                for part in range(2):
                    start = part * size + block * kept
                    out_ref[j * blocks + block, pl.ds((f * 2 + part) * kept, kept), :] = sent[
                        start : start + kept, f * size : (f + 1) * size
                    ]
    for place, term in enumerate(sums):
        sums_ref[place] = term


def second_kernel(na, place_ref, got_ref, gates_ref, early_ref, out_ref, own_ref, other_ref, all_ref):
    size = gates_ref.shape[-1]
    total = got_ref.shape[0]
    nb = total // na
    inner = nb // na
    tail = size // nb
    kept = size // inner
    gate = lambda index: (gates_ref[index, 0], gates_ref[index, 1])

    fields = []
    for f in range(2):
        parts = []
        for part in range(2):
            start = (f * 2 + part) * kept
            rows = [got_ref[pl.ds(a * nb, nb), pl.ds(start, kept), :].reshape(nb * kept, size) for a in range(na)]
            parts.append(tall(exchange(rows, size // na)))
        fields.append(split(wide(parts)))
    sums = [paired(dot(fields[1], fields[0], TN))]
    undo = undoing(gate(2))
    after = []
    for f in range(2):
        done = dot(undo, fields[f], NT)
        after.append(done)
    lists = []
    for h in range(inner):
        pieces = []
        for f in range(2):
            for block in range(na * na):
                cut = after[f][:, block * size : (block + 1) * size]
                pieces.append(cut.reshape(2 * na, inner, tail, size)[:, h].reshape(2 * na * tail, size))
        lists.append(tall(pieces))
    turned = exchange(lists, kept)
    turned = [item.reshape(2, na, na, 2, na, tail, size) for item in turned]

    fields = []
    for f in range(2):
        columns = []
        for top in range(na):
            for a in range(na):
                rows = [
                    turned[b][f, top, B, part, a]
                    for part in range(2)
                    for B in range(na)
                    for b in range(inner)
                ]
                columns.append(tall(rows))
        fields.append(split(wide(columns)))
    sums.append(paired(dot(fields[1], fields[0], NT)))
    undo = undoing(gate(4))
    after = [dot(undo, field, NN) for field in fields]

    span = inner * tail
    fields = []
    for f in range(2):
        columns = []
        for a in range(na):
            for B in range(na):
                rows = []
                for part in range(2):
                    for top in range(na):
                        row = (part * na + B) * span
                        column = (top * na + a) * size
                        rows.append(after[f][row : row + span, column : column + size])
                columns.append(tall(rows))
        fields.append(split(wide(columns)))
    sums.append(paired(dot(fields[1], fields[0], NT)))
    undo = undoing(gate(6))
    for f in range(2):
        done = dot(undo, fields[f], NN)
        for part in range(2):
            for a in range(na):
                for B in range(na):
                    column = (a * na + B) * size
                    for top in range(na):
                        for b in range(inner):
                            row = ((part * na + top) * inner + b) * tail
                            out_ref[
                                (B * na + top) * inner + b,
                                pl.ds(((f * 2 + part) * na + a) * tail, tail),
                                :,
                            ] = done[row : row + tail, column : column + size]

    early = [early_ref[place] for place in range(early_ref.shape[0])]
    share_out(early + sums, place_ref, (own_ref, other_ref), all_ref)


def third_kernel(na, nb, got_ref, state_ref, adjoint_ref):
    total, _, size = got_ref.shape
    rest = state_ref.shape[1]
    mid = rest // size
    inner = nb // na
    tail = size // nb
    kept = size // inner
    blocks = total // mid
    for j in range(mid):
        lists = [
            got_ref[j * blocks + block, pl.ds(0, 4 * kept), :] for block in range(blocks)
        ]
        turned = exchange(lists, kept)
        for h in range(inner):
            for f, ref in enumerate((state_ref, adjoint_ref)):
                for part in range(2):
                    for a in range(na):
                        row = ((f * 2 + part) * na + a) * tail
                        ref[part, pl.ds(((a * inner + h) * tail) * mid + j, tail, stride=mid), :] = turned[h][
                            row : row + tail
                        ]


def gradient_kernel(scaling, place_ref, gates_ref, own_ref, other_ref, out_ref, all_ref):
    size = gates_ref.shape[-1]
    gate = lambda index: (gates_ref[index, 0], gates_ref[index, 1])
    collect(place_ref, (own_ref, other_ref), all_ref)
    sums = lambda place: (all_ref[place, :size] * scaling, all_ref[place, size:] * scaling)
    low = sums(0)
    for index in range(gates_ref.shape[0]):
        if index % 2:
            grad = multiply(low, gate(index))
            low = multiply_adjoint(gate(index), grad)
        else:
            grad = multiply(sums(1 + index // 2), gate(index))
        out_ref[index, 0] = grad[0]
        out_ref[index, 1] = grad[1]


def from_mask(value, mask, total):
    return lax.ppermute(value, AXES, [(device, device ^ mask) for device in range(total)])


def tree(terms):
    while len(terms) > 1:
        terms = [one + two for one, two in zip(terms[::2], terms[1::2])]
    return terms[0]


def reduce_all(own, other, pair, near, far, total):
    half = own + from_mask(other, pair, total)
    mine = tree([half[0]] + [from_mask(half[place], mask, total) for place, mask in enumerate(near) if place])
    for mask in far:
        mine = mine + from_mask(mine, mask, total)
    half = jnp.stack([mine] + [from_mask(mine, mask, total) for mask in near[1:]])
    return half, from_mask(half, pair, total)


def shards(state, adjoint, gates):
    size = gates.shape[-1]
    count = state.shape[-1]
    na, nb = lax.axis_size("qa"), lax.axis_size("qb")
    total = na * nb
    scaling = float(total * count // size) ** (-0.5)
    rest = count // size
    kept = rest // total
    inner, tail = nb // na, size // nb
    if gates.shape[0] != 8 or inner * kept != size or tail != 8:
        return stepwise(state, adjoint, gates)

    low = 1 << ((nb.bit_length() - 1) // 2)
    near = [a * nb + b for a in range(na) for b in range(0, low, 2)]
    far = [1 << bit for bit in range(low.bit_length() - 1, nb.bit_length() - 1)]
    along = lax.axis_index("qb")
    half = lax.bitwise_and(along, 1)
    within = lax.axis_index("qa") * (low // 2) + lax.shift_right_logical(lax.bitwise_and(along, low - 1), 1)
    place = jnp.stack([half, within]).astype(jnp.int32)

    shape = lambda *dims: jax.ShapeDtypeStruct(dims, jnp.float32)
    flat = (2, rest, size)
    chunks = shape(len(near), 5 * size // len(near), size)
    smem = pl.BlockSpec(memory_space=pltpu.SMEM)
    vmem = pl.BlockSpec(memory_space=pltpu.VMEM)

    def call(kernel, name, out_shape, scratch=(), **options):
        return pl.pallas_call(
            kernel,
            out_shape=out_shape,
            scratch_shapes=scratch,
            compiler_params=pltpu.CompilerParams(vmem_limit_bytes=48 * 2**20),
            name=name,
            **options,
        )

    out, early = call(
        first_kernel,
        "first",
        (shape(total, 4 * kept, size), shape(2, 2 * size, size)),
    )(state.reshape(flat), adjoint.reshape(flat), gates)
    got = lax.all_to_all(out, AXES, split_axis=0, concat_axis=0, tiled=True)
    out, own, other = call(
        functools.partial(second_kernel, na),
        "second",
        (shape(total, 4 * kept, size), chunks, chunks),
        [pltpu.VMEM((5, 2 * size, size), jnp.float32)],
        in_specs=[smem, vmem, vmem, vmem],
    )(place, got, gates, early)
    got = lax.all_to_all(out, AXES, split_axis=0, concat_axis=0, tiled=True)
    own, other = reduce_all(own, other, 1, near, far, total)
    grads = call(
        functools.partial(gradient_kernel, scaling),
        "gradient",
        shape(*gates.shape),
        [pltpu.VMEM((5, 2 * size, size), jnp.float32)],
        in_specs=[smem, vmem, vmem, vmem],
    )(place, gates, own, other)
    state_out, adjoint_out = call(
        functools.partial(third_kernel, na, nb), "third", (shape(*flat), shape(*flat))
    )(got)
    return state_out.reshape(state.shape), adjoint_out.reshape(adjoint.shape), grads


def solution(mesh):
    in_specs = (P(None, "qa", "qb", None), P(None, "qa", "qb", None), P())
    out_specs = (P(None, "qa", "qb", None), P(None, "qa", "qb", None), P())
    return jax.shard_map(shards, mesh=mesh, in_specs=in_specs, out_specs=out_specs, check_vma=False)
```

```python
import functools

import jax
import jax.numpy as jnp
from jax import lax
from jax.experimental import pallas as pl
from jax.experimental.pallas import tpu as pltpu
from jax.sharding import PartitionSpec as P

AXES = ("qa", "qb")
NN = (((1,), (0,)), ((), ()))
NT = (((1,), (1,)), ((), ()))
TN = (((0,), (0,)), ((), ()))


def contract(left, right, left_dim, right_dim):
    return lax.dot_general(
        left,
        right,
        (((left_dim,), (right_dim,)), ((), ())),
        precision=lax.Precision.HIGHEST,
        preferred_element_type=jnp.float32,
    )


def undo_high(field, gate):
    new_real = contract(gate[0], field[0], 0, 0) + contract(gate[1], field[1], 0, 0)
    new_imag = contract(gate[0], field[1], 0, 0) - contract(gate[1], field[0], 0, 0)
    return jnp.stack([new_real, new_imag])


def undo_low(field, gate):
    new_real = contract(field[0], gate[0], 1, 0) + contract(field[1], gate[1], 1, 0)
    new_imag = contract(field[1], gate[0], 1, 0) - contract(field[0], gate[1], 1, 0)
    return jnp.stack([new_real, new_imag])


def pair_high(adjoint_field, new_field):
    grad_real = contract(adjoint_field[0], new_field[0], 1, 1) + contract(
        adjoint_field[1], new_field[1], 1, 1
    )
    grad_imag = contract(adjoint_field[1], new_field[0], 1, 1) - contract(
        adjoint_field[0], new_field[1], 1, 1
    )
    return jnp.stack([grad_real, grad_imag])


def pair_low(adjoint_field, new_field):
    grad_real = contract(adjoint_field[0], new_field[0], 0, 0) + contract(
        adjoint_field[1], new_field[1], 0, 0
    )
    grad_imag = contract(adjoint_field[1], new_field[0], 0, 0) - contract(
        adjoint_field[0], new_field[1], 0, 0
    )
    return jnp.stack([grad_real, grad_imag])


def stepwise(state, adjoint, gates):
    gate_size = gates.shape[-1]
    local_count = state.shape[-1]
    scaling = float(lax.axis_size("qa") * lax.axis_size("qb") * local_count // gate_size) ** (-0.5)
    state_now = state.reshape(2, local_count)
    adjoint_now = adjoint.reshape(2, local_count)
    collected = []

    def record(term):
        return lax.psum(term, ("qa", "qb"))

    for section in range(gates.shape[0] // 2):
        high_gate = gates[2 * section]
        low_gate = gates[2 * section + 1]
        upright = (2, gate_size, local_count // gate_size)
        state_high = state_now.reshape(upright)
        adjoint_high = adjoint_now.reshape(upright)
        state_new = undo_high(state_high, high_gate)
        collected.append(record(scaling * pair_high(adjoint_high, state_new)))
        adjoint_new = undo_high(adjoint_high, high_gate)
        flat = (2, local_count // gate_size, gate_size)
        state_low = state_new.reshape(flat)
        adjoint_low = adjoint_new.reshape(flat)
        groups = lax.axis_size("qa") if section % 2 == 0 else lax.axis_size("qb")
        state_done = undo_low(state_low, low_gate)
        collected.append(record(scaling * pair_low(adjoint_low, state_done)))
        adjoint_done = undo_low(adjoint_low, low_gate)
        split = (2, groups, local_count // groups)
        outgoing = (state_done.reshape(split), adjoint_done.reshape(split))
        if section % 2 == 0:
            arrived = (
                lax.all_to_all(outgoing[0], "qa", split_axis=1, concat_axis=1, tiled=True),
                lax.all_to_all(outgoing[1], "qa", split_axis=1, concat_axis=1, tiled=True),
            )
        else:
            arrived = (
                lax.all_to_all(outgoing[0], "qb", split_axis=1, concat_axis=1, tiled=True),
                lax.all_to_all(outgoing[1], "qb", split_axis=1, concat_axis=1, tiled=True),
            )
        state_now = arrived[0].reshape(2, local_count)
        adjoint_now = arrived[1].reshape(2, local_count)
    gradients = jnp.stack(collected)
    return (state_now.reshape(state.shape), adjoint_now.reshape(adjoint.shape), gradients)


def split(x):
    high = x.astype(jnp.bfloat16)
    return high, (x - high.astype(jnp.float32)).astype(jnp.bfloat16)


def dot(left, right, dims):
    part = lambda i, j: lax.dot_general(left[i], right[j], dims, preferred_element_type=jnp.float32)
    return (part(0, 1) + part(1, 0)) + part(0, 0)


def each(operation, *arrays):
    return tuple(operation(*parts) for parts in zip(*arrays))


def wide(arrays):
    return jnp.concatenate(arrays, 1)


def tall(arrays):
    return jnp.concatenate(arrays, 0)


def multiply(left, right):
    size = left[0].shape[0]
    both = dot(split(tall(left)), split(wide(right)), NN)
    return (
        both[:size, :size] - both[size:, size:],
        both[:size, size:] + both[size:, :size],
    )


def multiply_adjoint(left, right):
    size = left[0].shape[0]
    both = dot(split(tall((left[0].T, left[1].T))), split(wide(right)), NN)
    return (
        both[:size, :size] + both[size:, size:],
        both[:size, size:] - both[size:, :size],
    )


def undoing(gate):
    real, imag = gate[0].T, gate[1].T
    return split(tall((wide((real, imag)), wide((-imag, real)))))


def paired(both):
    size = both.shape[0] // 2
    return tall((both[:size, :size] + both[size:, size:], both[size:, :size] - both[:size, size:]))


def exchange(parts, width):
    parts = list(parts)
    lanes = parts[0].shape[-1]
    lane = lax.broadcasted_iota(jnp.int32, parts[0].shape, 1)
    step = 1
    while step < len(parts):
        shift = step * width
        lower = (lane // shift) % 2 == 0
        for index in range(len(parts)):
            if index & step == 0:
                one, two = parts[index], parts[index + step]
                parts[index] = jnp.where(lower, one, pltpu.roll(two, shift, 1))
                parts[index + step] = jnp.where(lower, pltpu.roll(one, lanes - shift, 1), two)
        step *= 2
    return parts


def share_out(sums, place_ref, refs, all_ref):
    for index, term in enumerate(sums):
        all_ref[index] = term
    count, rows = refs[0].shape[0], refs[0].shape[1] // len(sums)
    for other, ref in enumerate(refs):
        half = lax.bitwise_xor(place_ref[0], other)
        for mask in range(count):
            chunk = half * count + lax.bitwise_xor(place_ref[1], mask)
            start = pl.multiple_of(chunk * rows, rows)
            for index in range(len(sums)):
                ref[mask, pl.ds(index * rows, rows), :] = all_ref[index, pl.ds(start, rows), :]


def collect(place_ref, refs, all_ref):
    sums, count, rows = all_ref.shape[0], refs[0].shape[0], refs[0].shape[1] // all_ref.shape[0]
    for other, ref in enumerate(refs):
        half = lax.bitwise_xor(place_ref[0], other)
        for mask in range(count):
            chunk = half * count + lax.bitwise_xor(place_ref[1], mask)
            start = pl.multiple_of(chunk * rows, rows)
            for index in range(sums):
                all_ref[index, pl.ds(start, rows), :] = ref[mask, pl.ds(index * rows, rows), :]


def first_kernel(place_ref, state_ref, adjoint_ref, gates_ref, out_ref, own_ref, other_ref, all_ref):
    size = gates_ref.shape[-1]
    mid = state_ref.shape[1] // size
    total = out_ref.shape[0]
    kept = mid * size // total
    blocks = size // kept
    gate = lambda index: (gates_ref[index, 0], gates_ref[index, 1])

    four = multiply(multiply(gate(1), gate(3)), multiply(gate(5), gate(7)))
    undo_low = undoing(four)
    undo_high = undoing(gate(0))

    fields = [
        [
            [split(ref[part, pl.ds(j, size, stride=mid), :]) for part in range(2)]
            for j in range(mid)
        ]
        for ref in (state_ref, adjoint_ref)
    ]
    by_low = [each(lambda *a: tall(a), *[each(lambda *b: wide(b), *row) for row in field]) for field in fields]
    sums = [paired(dot(by_low[1], by_low[0], TN))]
    by_high = [
        each(lambda *a: tall(a), *[each(lambda *b: wide(b), *[row[part] for row in field]) for part in range(2)])
        for field in fields
    ]
    sums.append(paired(dot(by_high[1], by_high[0], NT)))
    done = [dot(undo_high, field, NN) for field in by_high]
    for j in range(mid):
        here = slice(j * size, (j + 1) * size)
        rows = tall([wide((field[:size, here], field[size:, here])) for field in done])
        sent = dot(undo_low, split(rows), NT)
        for block in range(blocks):
            for f in range(2):
                for part in range(2):
                    start = part * size + block * kept
                    out_ref[j * blocks + block, pl.ds((f * 2 + part) * kept, kept), :] = sent[
                        start : start + kept, f * size : (f + 1) * size
                    ]
    share_out(sums, place_ref, (own_ref, other_ref), all_ref)


def second_kernel(na, place_ref, got_ref, gates_ref, _, out_ref, own_ref, other_ref, all_ref):
    size = gates_ref.shape[-1]
    total = got_ref.shape[0]
    nb = total // na
    inner = nb // na
    tail = size // nb
    kept = size // inner
    gate = lambda index: (gates_ref[index, 0], gates_ref[index, 1])

    fields = []
    for f in range(2):
        parts = []
        for part in range(2):
            start = (f * 2 + part) * kept
            rows = [got_ref[pl.ds(a * nb, nb), pl.ds(start, kept), :].reshape(nb * kept, size) for a in range(na)]
            parts.append(tall(exchange(rows, size // na)))
        fields.append(split(wide(parts)))
    sums = [paired(dot(fields[1], fields[0], TN))]
    undo = undoing(gate(2))
    after = []
    for f in range(2):
        done = dot(undo, fields[f], NT)
        after.append(done)
    lists = []
    for h in range(inner):
        pieces = []
        for f in range(2):
            for block in range(na * na):
                cut = after[f][:, block * size : (block + 1) * size]
                pieces.append(cut.reshape(2 * na, inner, tail, size)[:, h].reshape(2 * na * tail, size))
        lists.append(tall(pieces))
    turned = exchange(lists, kept)
    turned = [item.reshape(2, na, na, 2, na, tail, size) for item in turned]

    fields = []
    for f in range(2):
        columns = []
        for top in range(na):
            for a in range(na):
                rows = [
                    turned[b][f, top, B, part, a]
                    for part in range(2)
                    for B in range(na)
                    for b in range(inner)
                ]
                columns.append(tall(rows))
        fields.append(split(wide(columns)))
    sums.append(paired(dot(fields[1], fields[0], NT)))
    undo = undoing(gate(4))
    after = [dot(undo, field, NN) for field in fields]

    span = inner * tail
    fields = []
    for f in range(2):
        columns = []
        for a in range(na):
            for B in range(na):
                rows = []
                for part in range(2):
                    for top in range(na):
                        row = (part * na + B) * span
                        column = (top * na + a) * size
                        rows.append(after[f][row : row + span, column : column + size])
                columns.append(tall(rows))
        fields.append(split(wide(columns)))
    sums.append(paired(dot(fields[1], fields[0], NT)))
    undo = undoing(gate(6))
    for f in range(2):
        done = dot(undo, fields[f], NN)
        for part in range(2):
            for a in range(na):
                for B in range(na):
                    column = (a * na + B) * size
                    for top in range(na):
                        for b in range(inner):
                            row = ((part * na + top) * inner + b) * tail
                            out_ref[
                                (B * na + top) * inner + b,
                                pl.ds(((f * 2 + part) * na + a) * tail, tail),
                                :,
                            ] = done[row : row + tail, column : column + size]

    share_out(sums, place_ref, (own_ref, other_ref), all_ref)


def third_kernel(na, nb, got_ref, state_ref, adjoint_ref):
    total, _, size = got_ref.shape
    rest = state_ref.shape[1]
    mid = rest // size
    inner = nb // na
    tail = size // nb
    kept = size // inner
    blocks = total // mid
    for j in range(mid):
        lists = [
            got_ref[j * blocks + block, pl.ds(0, 4 * kept), :] for block in range(blocks)
        ]
        turned = exchange(lists, kept)
        for h in range(inner):
            for f, ref in enumerate((state_ref, adjoint_ref)):
                for part in range(2):
                    for a in range(na):
                        row = ((f * 2 + part) * na + a) * tail
                        ref[part, pl.ds(((a * inner + h) * tail) * mid + j, tail, stride=mid), :] = turned[h][
                            row : row + tail
                        ]


def write(grads, out_ref, grad_ref, sem):
    copies = []
    for place, (index, grad) in enumerate(grads):
        grad_ref[place, 0] = grad[0]
        grad_ref[place, 1] = grad[1]
        copies.append(pltpu.make_async_copy(grad_ref.at[place], out_ref.at[index], sem.at[place]))
        copies[-1].start()
    for copy in copies:
        copy.wait()


def early_kernel(scaling, place_ref, gates_ref, own_ref, other_ref, out_ref, all_ref, grad_ref, sem):
    size = gates_ref.shape[-1]
    gate = lambda index: (gates_ref[index, 0], gates_ref[index, 1])
    collect(place_ref, (own_ref, other_ref), all_ref)
    sums = lambda place: (all_ref[place, :size] * scaling, all_ref[place, size:] * scaling)
    grads = [(0, multiply(sums(1), gate(0)))]
    low = sums(0)
    for index in range(1, gates_ref.shape[0], 2):
        grads.append((index, multiply(low, gate(index))))
        low = multiply_adjoint(gate(index), grads[-1][1])
    write(grads, out_ref, grad_ref, sem)


def late_kernel(scaling, place_ref, gates_ref, own_ref, other_ref, _, out_ref, all_ref, grad_ref, sem):
    size = gates_ref.shape[-1]
    collect(place_ref, (own_ref, other_ref), all_ref)
    grads = []
    for place in range(all_ref.shape[0]):
        index = 2 * place + 2
        sums = (all_ref[place, :size] * scaling, all_ref[place, size:] * scaling)
        grads.append((index, multiply(sums, (gates_ref[index, 0], gates_ref[index, 1]))))
    write(grads, out_ref, grad_ref, sem)


def from_mask(value, mask, total):
    return lax.ppermute(value, AXES, [(device, device ^ mask) for device in range(total)])


def tree(terms):
    while len(terms) > 1:
        terms = [one + two for one, two in zip(terms[::2], terms[1::2])]
    return terms[0]


def reduce_all(own, other, pair, near, far, total):
    half = own + from_mask(other, pair, total)
    mine = tree([half[0]] + [from_mask(half[place], mask, total) for place, mask in enumerate(near) if place])
    for mask in far:
        mine = mine + from_mask(mine, mask, total)
    half = jnp.stack([mine] + [from_mask(mine, mask, total) for mask in near[1:]])
    return half, from_mask(half, pair, total)


def shards(state, adjoint, gates):
    size = gates.shape[-1]
    count = state.shape[-1]
    na, nb = lax.axis_size("qa"), lax.axis_size("qb")
    total = na * nb
    scaling = float(total * count // size) ** (-0.5)
    rest = count // size
    kept = rest // total
    inner, tail = nb // na, size // nb
    if gates.shape[0] != 8 or inner * kept != size or tail != 8:
        return stepwise(state, adjoint, gates)

    low = 1 << ((nb.bit_length() - 1) // 2)
    near = [a * nb + b for a in range(na) for b in range(0, low, 2)]
    far = [1 << bit for bit in range(low.bit_length() - 1, nb.bit_length() - 1)]
    along = lax.axis_index("qb")
    half = lax.bitwise_and(along, 1)
    within = lax.axis_index("qa") * (low // 2) + lax.shift_right_logical(lax.bitwise_and(along, low - 1), 1)
    place = jnp.stack([half, within]).astype(jnp.int32)

    shape = lambda *dims: jax.ShapeDtypeStruct(dims, jnp.float32)
    flat = (2, rest, size)
    chunks = lambda sums: shape(len(near), sums * size // len(near), size)
    buffers = lambda sums, grads: [
        pltpu.VMEM((sums, 2 * size, size), jnp.float32),
        pltpu.VMEM((grads, 2, size, size), jnp.float32),
        pltpu.SemaphoreType.DMA((grads,)),
    ]
    smem = pl.BlockSpec(memory_space=pltpu.SMEM)
    vmem = pl.BlockSpec(memory_space=pltpu.VMEM)
    anywhere = pl.BlockSpec(memory_space=pl.ANY)

    def call(kernel, name, out_shape, scratch=(), **options):
        return pl.pallas_call(
            kernel,
            out_shape=out_shape,
            scratch_shapes=scratch,
            compiler_params=pltpu.CompilerParams(vmem_limit_bytes=48 * 2**20),
            name=name,
            **options,
        )

    out, own, other = call(
        first_kernel,
        "first",
        (shape(total, 4 * kept, size), chunks(2), chunks(2)),
        buffers(2, 1)[:1],
        in_specs=[smem, vmem, vmem, vmem],
    )(place, state.reshape(flat), adjoint.reshape(flat), gates)
    got = lax.all_to_all(out, AXES, split_axis=0, concat_axis=0, tiled=True)
    early = reduce_all(own, other, 1, near, far, total)
    out, own, other = call(
        functools.partial(second_kernel, na),
        "second",
        (shape(total, 4 * kept, size), chunks(3), chunks(3)),
        buffers(3, 1)[:1],
        in_specs=[smem, vmem, vmem, anywhere],
    )(place, got, gates, early[1])
    got = lax.all_to_all(out, AXES, split_axis=0, concat_axis=0, tiled=True)
    late = reduce_all(own, other, 1, near, far, total)
    grads = call(
        functools.partial(early_kernel, scaling),
        "early",
        shape(*gates.shape),
        buffers(2, 5),
        in_specs=[smem, vmem, vmem, vmem],
        out_specs=anywhere,
    )(place, gates, *early)
    grads = call(
        functools.partial(late_kernel, scaling),
        "late",
        shape(*gates.shape),
        buffers(3, 3),
        in_specs=[smem, vmem, vmem, vmem, anywhere],
        out_specs=anywhere,
        input_output_aliases={4: 0},
    )(place, gates, *late, grads)
    state_out, adjoint_out = call(
        functools.partial(third_kernel, na, nb), "third", (shape(*flat), shape(*flat))
    )(got)
    return state_out.reshape(state.shape), adjoint_out.reshape(adjoint.shape), grads


def solution(mesh):
    in_specs = (P(None, "qa", "qb", None), P(None, "qa", "qb", None), P())
    out_specs = (P(None, "qa", "qb", None), P(None, "qa", "qb", None), P())
    return jax.shard_map(shards, mesh=mesh, in_specs=in_specs, out_specs=out_specs, check_vma=False)
```

```python
import functools

import jax
import jax.numpy as jnp
from jax import lax
from jax.experimental import pallas as pl
from jax.experimental.pallas import tpu as pltpu
from jax.sharding import PartitionSpec as P

AXES = ("qa", "qb")
NN = (((1,), (0,)), ((), ()))
NT = (((1,), (1,)), ((), ()))
TN = (((0,), (0,)), ((), ()))


def contract(left, right, left_dim, right_dim):
    return lax.dot_general(
        left,
        right,
        (((left_dim,), (right_dim,)), ((), ())),
        precision=lax.Precision.HIGHEST,
        preferred_element_type=jnp.float32,
    )


def undo_high(field, gate):
    new_real = contract(gate[0], field[0], 0, 0) + contract(gate[1], field[1], 0, 0)
    new_imag = contract(gate[0], field[1], 0, 0) - contract(gate[1], field[0], 0, 0)
    return jnp.stack([new_real, new_imag])


def undo_low(field, gate):
    new_real = contract(field[0], gate[0], 1, 0) + contract(field[1], gate[1], 1, 0)
    new_imag = contract(field[1], gate[0], 1, 0) - contract(field[0], gate[1], 1, 0)
    return jnp.stack([new_real, new_imag])


def pair_high(adjoint_field, new_field):
    grad_real = contract(adjoint_field[0], new_field[0], 1, 1) + contract(
        adjoint_field[1], new_field[1], 1, 1
    )
    grad_imag = contract(adjoint_field[1], new_field[0], 1, 1) - contract(
        adjoint_field[0], new_field[1], 1, 1
    )
    return jnp.stack([grad_real, grad_imag])


def pair_low(adjoint_field, new_field):
    grad_real = contract(adjoint_field[0], new_field[0], 0, 0) + contract(
        adjoint_field[1], new_field[1], 0, 0
    )
    grad_imag = contract(adjoint_field[1], new_field[0], 0, 0) - contract(
        adjoint_field[0], new_field[1], 0, 0
    )
    return jnp.stack([grad_real, grad_imag])


def stepwise(state, adjoint, gates):
    gate_size = gates.shape[-1]
    local_count = state.shape[-1]
    scaling = float(lax.axis_size("qa") * lax.axis_size("qb") * local_count // gate_size) ** (-0.5)
    state_now = state.reshape(2, local_count)
    adjoint_now = adjoint.reshape(2, local_count)
    collected = []

    def record(term):
        return lax.psum(term, ("qa", "qb"))

    for section in range(gates.shape[0] // 2):
        high_gate = gates[2 * section]
        low_gate = gates[2 * section + 1]
        upright = (2, gate_size, local_count // gate_size)
        state_high = state_now.reshape(upright)
        adjoint_high = adjoint_now.reshape(upright)
        state_new = undo_high(state_high, high_gate)
        collected.append(record(scaling * pair_high(adjoint_high, state_new)))
        adjoint_new = undo_high(adjoint_high, high_gate)
        flat = (2, local_count // gate_size, gate_size)
        state_low = state_new.reshape(flat)
        adjoint_low = adjoint_new.reshape(flat)
        groups = lax.axis_size("qa") if section % 2 == 0 else lax.axis_size("qb")
        state_done = undo_low(state_low, low_gate)
        collected.append(record(scaling * pair_low(adjoint_low, state_done)))
        adjoint_done = undo_low(adjoint_low, low_gate)
        split = (2, groups, local_count // groups)
        outgoing = (state_done.reshape(split), adjoint_done.reshape(split))
        if section % 2 == 0:
            arrived = (
                lax.all_to_all(outgoing[0], "qa", split_axis=1, concat_axis=1, tiled=True),
                lax.all_to_all(outgoing[1], "qa", split_axis=1, concat_axis=1, tiled=True),
            )
        else:
            arrived = (
                lax.all_to_all(outgoing[0], "qb", split_axis=1, concat_axis=1, tiled=True),
                lax.all_to_all(outgoing[1], "qb", split_axis=1, concat_axis=1, tiled=True),
            )
        state_now = arrived[0].reshape(2, local_count)
        adjoint_now = arrived[1].reshape(2, local_count)
    gradients = jnp.stack(collected)
    return (state_now.reshape(state.shape), adjoint_now.reshape(adjoint.shape), gradients)


def split(x):
    high = x.astype(jnp.bfloat16)
    return high, (x - high.astype(jnp.float32)).astype(jnp.bfloat16)


def dot(left, right, dims):
    part = lambda i, j: lax.dot_general(left[i], right[j], dims, preferred_element_type=jnp.float32)
    return (part(0, 1) + part(1, 0)) + part(0, 0)


def each(operation, *arrays):
    return tuple(operation(*parts) for parts in zip(*arrays))


def wide(arrays):
    return jnp.concatenate(arrays, 1)


def tall(arrays):
    return jnp.concatenate(arrays, 0)


def multiply(left, right):
    size = left[0].shape[0]
    both = dot(split(tall(left)), split(wide(right)), NN)
    return (
        both[:size, :size] - both[size:, size:],
        both[:size, size:] + both[size:, :size],
    )


def multiply_adjoint(left, right):
    size = left[0].shape[0]
    both = dot(split(tall((left[0].T, left[1].T))), split(wide(right)), NN)
    return (
        both[:size, :size] + both[size:, size:],
        both[:size, size:] - both[size:, :size],
    )


def undoing(gate):
    real, imag = gate[0].T, gate[1].T
    return split(tall((wide((real, imag)), wide((-imag, real)))))


def paired(both):
    size = both.shape[0] // 2
    return tall((both[:size, :size] + both[size:, size:], both[size:, :size] - both[:size, size:]))


def exchange(parts, width):
    parts = list(parts)
    lanes = parts[0].shape[-1]
    lane = lax.broadcasted_iota(jnp.int32, parts[0].shape, 1)
    step = 1
    while step < len(parts):
        shift = step * width
        lower = (lane // shift) % 2 == 0
        for index in range(len(parts)):
            if index & step == 0:
                one, two = parts[index], parts[index + step]
                parts[index] = jnp.where(lower, one, pltpu.roll(two, shift, 1))
                parts[index + step] = jnp.where(lower, pltpu.roll(one, lanes - shift, 1), two)
        step *= 2
    return parts


def share_out(sums, place_ref, refs, all_ref):
    for index, term in enumerate(sums):
        all_ref[index] = term
    rows = all_ref.shape[1] // len(refs)
    for mask, ref in enumerate(refs):
        start = pl.multiple_of(lax.bitwise_xor(place_ref[0], mask) * rows, rows)
        for index in range(len(sums)):
            ref[pl.ds(index * rows, rows), :] = all_ref[index, pl.ds(start, rows), :]


def collect(place_ref, refs, all_ref):
    rows = all_ref.shape[1] // len(refs)
    for mask, ref in enumerate(refs):
        start = pl.multiple_of(lax.bitwise_xor(place_ref[0], mask) * rows, rows)
        for index in range(all_ref.shape[0]):
            all_ref[index, pl.ds(start, rows), :] = ref[pl.ds(index * rows, rows), :]


def first_kernel(place_ref, state_ref, adjoint_ref, gates_ref, out_ref, *refs):
    size = gates_ref.shape[-1]
    mid = state_ref.shape[1] // size
    total = out_ref.shape[0]
    kept = mid * size // total
    blocks = size // kept
    gate = lambda index: (gates_ref[index, 0], gates_ref[index, 1])

    four = multiply(multiply(gate(1), gate(3)), multiply(gate(5), gate(7)))
    undo_low = undoing(four)
    undo_high = undoing(gate(0))

    fields = [
        [
            [split(ref[part, pl.ds(j, size, stride=mid), :]) for part in range(2)]
            for j in range(mid)
        ]
        for ref in (state_ref, adjoint_ref)
    ]
    by_low = [each(lambda *a: tall(a), *[each(lambda *b: wide(b), *row) for row in field]) for field in fields]
    sums = [paired(dot(by_low[1], by_low[0], TN))]
    by_high = [
        each(lambda *a: tall(a), *[each(lambda *b: wide(b), *[row[part] for row in field]) for part in range(2)])
        for field in fields
    ]
    sums.append(paired(dot(by_high[1], by_high[0], NT)))
    done = [dot(undo_high, field, NN) for field in by_high]
    for j in range(mid):
        here = slice(j * size, (j + 1) * size)
        rows = tall([wide((field[:size, here], field[size:, here])) for field in done])
        sent = dot(undo_low, split(rows), NT)
        for block in range(blocks):
            for f in range(2):
                for part in range(2):
                    start = part * size + block * kept
                    out_ref[j * blocks + block, pl.ds((f * 2 + part) * kept, kept), :] = sent[
                        start : start + kept, f * size : (f + 1) * size
                    ]
    share_out(sums, place_ref, refs[:-1], refs[-1])


def second_kernel(na, unread, place_ref, got_ref, gates_ref, *refs):
    out_ref, *refs = refs[unread:]
    size = gates_ref.shape[-1]
    total = got_ref.shape[0]
    nb = total // na
    inner = nb // na
    tail = size // nb
    kept = size // inner
    gate = lambda index: (gates_ref[index, 0], gates_ref[index, 1])

    fields = []
    for f in range(2):
        parts = []
        for part in range(2):
            start = (f * 2 + part) * kept
            rows = [got_ref[pl.ds(a * nb, nb), pl.ds(start, kept), :].reshape(nb * kept, size) for a in range(na)]
            parts.append(tall(exchange(rows, size // na)))
        fields.append(split(wide(parts)))
    sums = [paired(dot(fields[1], fields[0], TN))]
    undo = undoing(gate(2))
    after = []
    for f in range(2):
        done = dot(undo, fields[f], NT)
        after.append(done)
    lists = []
    for h in range(inner):
        pieces = []
        for f in range(2):
            for block in range(na * na):
                cut = after[f][:, block * size : (block + 1) * size]
                pieces.append(cut.reshape(2 * na, inner, tail, size)[:, h].reshape(2 * na * tail, size))
        lists.append(tall(pieces))
    turned = exchange(lists, kept)
    turned = [item.reshape(2, na, na, 2, na, tail, size) for item in turned]

    fields = []
    for f in range(2):
        columns = []
        for top in range(na):
            for a in range(na):
                rows = [
                    turned[b][f, top, B, part, a]
                    for part in range(2)
                    for B in range(na)
                    for b in range(inner)
                ]
                columns.append(tall(rows))
        fields.append(split(wide(columns)))
    sums.append(paired(dot(fields[1], fields[0], NT)))
    undo = undoing(gate(4))
    after = [dot(undo, field, NN) for field in fields]

    span = inner * tail
    fields = []
    for f in range(2):
        columns = []
        for a in range(na):
            for B in range(na):
                rows = []
                for part in range(2):
                    for top in range(na):
                        row = (part * na + B) * span
                        column = (top * na + a) * size
                        rows.append(after[f][row : row + span, column : column + size])
                columns.append(tall(rows))
        fields.append(split(wide(columns)))
    sums.append(paired(dot(fields[1], fields[0], NT)))
    undo = undoing(gate(6))
    for f in range(2):
        done = dot(undo, fields[f], NN)
        for part in range(2):
            for a in range(na):
                for B in range(na):
                    column = (a * na + B) * size
                    for top in range(na):
                        for b in range(inner):
                            row = ((part * na + top) * inner + b) * tail
                            out_ref[
                                (B * na + top) * inner + b,
                                pl.ds(((f * 2 + part) * na + a) * tail, tail),
                                :,
                            ] = done[row : row + tail, column : column + size]

    share_out(sums, place_ref, refs[:-1], refs[-1])


def third_kernel(na, nb, got_ref, state_ref, adjoint_ref):
    total, _, size = got_ref.shape
    rest = state_ref.shape[1]
    mid = rest // size
    inner = nb // na
    tail = size // nb
    kept = size // inner
    blocks = total // mid
    for j in range(mid):
        lists = [
            got_ref[j * blocks + block, pl.ds(0, 4 * kept), :] for block in range(blocks)
        ]
        turned = exchange(lists, kept)
        for h in range(inner):
            for f, ref in enumerate((state_ref, adjoint_ref)):
                for part in range(2):
                    for a in range(na):
                        row = ((f * 2 + part) * na + a) * tail
                        ref[part, pl.ds(((a * inner + h) * tail) * mid + j, tail, stride=mid), :] = turned[h][
                            row : row + tail
                        ]


def write(grads, out_ref, grad_ref, sem):
    copies = []
    for place, (index, grad) in enumerate(grads):
        grad_ref[place, 0] = grad[0]
        grad_ref[place, 1] = grad[1]
        copies.append(pltpu.make_async_copy(grad_ref.at[place], out_ref.at[index], sem.at[place]))
        copies[-1].start()
    for copy in copies:
        copy.wait()


def early_kernel(scaling, place_ref, gates_ref, *refs):
    *refs, out_ref, all_ref, grad_ref, sem = refs
    size = gates_ref.shape[-1]
    gate = lambda index: (gates_ref[index, 0], gates_ref[index, 1])
    collect(place_ref, refs, all_ref)
    sums = lambda place: (all_ref[place, :size] * scaling, all_ref[place, size:] * scaling)
    grads = [(0, multiply(sums(1), gate(0)))]
    low = sums(0)
    for index in range(1, gates_ref.shape[0], 2):
        grads.append((index, multiply(low, gate(index))))
        low = multiply_adjoint(gate(index), grads[-1][1])
    write(grads, out_ref, grad_ref, sem)


def late_kernel(scaling, place_ref, gates_ref, *refs):
    *refs, _, out_ref, all_ref, grad_ref, sem = refs
    size = gates_ref.shape[-1]
    collect(place_ref, refs, all_ref)
    grads = []
    for place in range(all_ref.shape[0]):
        index = 2 * place + 2
        sums = (all_ref[place, :size] * scaling, all_ref[place, size:] * scaling)
        grads.append((index, multiply(sums, (gates_ref[index, 0], gates_ref[index, 1]))))
    write(grads, out_ref, grad_ref, sem)


def from_mask(value, mask, total):
    return lax.ppermute(value, AXES, [(device, device ^ mask) for device in range(total)])


def tree(terms):
    while len(terms) > 1:
        terms = [one + two for one, two in zip(terms[::2], terms[1::2])]
    return terms[0]


def reduce_all(chunks, near, far, total):
    own = tree([chunks[0]] + [from_mask(chunk, mask, total) for chunk, mask in zip(chunks[1:], near[1:])])
    own = tree([own] + [from_mask(own, mask, total) for mask in far[1:]])
    return [own] + [from_mask(own, mask, total) for mask in near[1:]]


def shards(state, adjoint, gates):
    size = gates.shape[-1]
    count = state.shape[-1]
    na, nb = lax.axis_size("qa"), lax.axis_size("qb")
    total = na * nb
    scaling = float(total * count // size) ** (-0.5)
    rest = count // size
    kept = rest // total
    inner, tail = nb // na, size // nb
    if gates.shape[0] != 8 or inner * kept != size or tail != 8:
        return stepwise(state, adjoint, gates)

    low = 1 << ((nb.bit_length() - 1) // 2)
    near = [a * nb + b for a in range(na) for b in range(low)]
    far = [b * low for b in range(nb // low)]
    place = lax.axis_index("qa") * low + lax.bitwise_and(lax.axis_index("qb"), low - 1)
    place = place.astype(jnp.int32).reshape(1)

    shape = lambda *dims: jax.ShapeDtypeStruct(dims, jnp.float32)
    flat = (2, rest, size)
    chunks = lambda sums: [shape(2 * sums * size // len(near), size) for _ in near]
    buffers = lambda sums, grads: [
        pltpu.VMEM((sums, 2 * size, size), jnp.float32),
        pltpu.VMEM((grads, 2, size, size), jnp.float32),
        pltpu.SemaphoreType.DMA((grads,)),
    ]
    smem = pl.BlockSpec(memory_space=pltpu.SMEM)
    vmem = pl.BlockSpec(memory_space=pltpu.VMEM)
    anywhere = pl.BlockSpec(memory_space=pl.ANY)

    def call(kernel, name, out_shape, scratch=(), **options):
        return pl.pallas_call(
            kernel,
            out_shape=out_shape,
            scratch_shapes=scratch,
            compiler_params=pltpu.CompilerParams(vmem_limit_bytes=48 * 2**20),
            name=name,
            **options,
        )

    out, *chunk = call(
        first_kernel,
        "first",
        [shape(total, 4 * kept, size)] + chunks(2),
        buffers(2, 1)[:1],
        in_specs=[smem, vmem, vmem, vmem],
    )(place, state.reshape(flat), adjoint.reshape(flat), gates)
    got = lax.all_to_all(out, AXES, split_axis=0, concat_axis=0, tiled=True)
    early = reduce_all(chunk, near, far, total)
    out, *chunk = call(
        functools.partial(second_kernel, na, len(near)),
        "second",
        [shape(total, 4 * kept, size)] + chunks(3),
        buffers(3, 1)[:1],
        in_specs=[smem, vmem, vmem] + [anywhere] * len(near),
    )(place, got, gates, *early)
    got = lax.all_to_all(out, AXES, split_axis=0, concat_axis=0, tiled=True)
    late = reduce_all(chunk, near, far, total)
    grads = call(
        functools.partial(early_kernel, scaling),
        "early",
        shape(*gates.shape),
        buffers(2, 5),
        in_specs=[smem] + [vmem] * (1 + len(near)),
        out_specs=anywhere,
    )(place, gates, *early)
    grads = call(
        functools.partial(late_kernel, scaling),
        "late",
        shape(*gates.shape),
        buffers(3, 3),
        in_specs=[smem] + [vmem] * (1 + len(near)) + [anywhere],
        out_specs=anywhere,
        input_output_aliases={2 + len(near): 0},
    )(place, gates, *late, grads)
    state_out, adjoint_out = call(
        functools.partial(third_kernel, na, nb), "third", (shape(*flat), shape(*flat))
    )(got)
    return state_out.reshape(state.shape), adjoint_out.reshape(adjoint.shape), grads


def solution(mesh):
    in_specs = (P(None, "qa", "qb", None), P(None, "qa", "qb", None), P())
    out_specs = (P(None, "qa", "qb", None), P(None, "qa", "qb", None), P())
    return jax.shard_map(shards, mesh=mesh, in_specs=in_specs, out_specs=out_specs, check_vma=False)
```

```python
import functools

import jax
import jax.numpy as jnp
from jax import lax
from jax.experimental import pallas as pl
from jax.experimental.pallas import tpu as pltpu
from jax.sharding import PartitionSpec as P

AXES = ("qa", "qb")
NN = (((1,), (0,)), ((), ()))
NT = (((1,), (1,)), ((), ()))
TN = (((0,), (0,)), ((), ()))


def contract(left, right, left_dim, right_dim):
    return lax.dot_general(
        left,
        right,
        (((left_dim,), (right_dim,)), ((), ())),
        precision=lax.Precision.HIGHEST,
        preferred_element_type=jnp.float32,
    )


def undo_high(field, gate):
    new_real = contract(gate[0], field[0], 0, 0) + contract(gate[1], field[1], 0, 0)
    new_imag = contract(gate[0], field[1], 0, 0) - contract(gate[1], field[0], 0, 0)
    return jnp.stack([new_real, new_imag])


def undo_low(field, gate):
    new_real = contract(field[0], gate[0], 1, 0) + contract(field[1], gate[1], 1, 0)
    new_imag = contract(field[1], gate[0], 1, 0) - contract(field[0], gate[1], 1, 0)
    return jnp.stack([new_real, new_imag])


def pair_high(adjoint_field, new_field):
    grad_real = contract(adjoint_field[0], new_field[0], 1, 1) + contract(
        adjoint_field[1], new_field[1], 1, 1
    )
    grad_imag = contract(adjoint_field[1], new_field[0], 1, 1) - contract(
        adjoint_field[0], new_field[1], 1, 1
    )
    return jnp.stack([grad_real, grad_imag])


def pair_low(adjoint_field, new_field):
    grad_real = contract(adjoint_field[0], new_field[0], 0, 0) + contract(
        adjoint_field[1], new_field[1], 0, 0
    )
    grad_imag = contract(adjoint_field[1], new_field[0], 0, 0) - contract(
        adjoint_field[0], new_field[1], 0, 0
    )
    return jnp.stack([grad_real, grad_imag])


def stepwise(state, adjoint, gates):
    gate_size = gates.shape[-1]
    local_count = state.shape[-1]
    scaling = float(lax.axis_size("qa") * lax.axis_size("qb") * local_count // gate_size) ** (-0.5)
    state_now = state.reshape(2, local_count)
    adjoint_now = adjoint.reshape(2, local_count)
    collected = []

    def record(term):
        return lax.psum(term, ("qa", "qb"))

    for section in range(gates.shape[0] // 2):
        high_gate = gates[2 * section]
        low_gate = gates[2 * section + 1]
        upright = (2, gate_size, local_count // gate_size)
        state_high = state_now.reshape(upright)
        adjoint_high = adjoint_now.reshape(upright)
        state_new = undo_high(state_high, high_gate)
        collected.append(record(scaling * pair_high(adjoint_high, state_new)))
        adjoint_new = undo_high(adjoint_high, high_gate)
        flat = (2, local_count // gate_size, gate_size)
        state_low = state_new.reshape(flat)
        adjoint_low = adjoint_new.reshape(flat)
        groups = lax.axis_size("qa") if section % 2 == 0 else lax.axis_size("qb")
        state_done = undo_low(state_low, low_gate)
        collected.append(record(scaling * pair_low(adjoint_low, state_done)))
        adjoint_done = undo_low(adjoint_low, low_gate)
        split = (2, groups, local_count // groups)
        outgoing = (state_done.reshape(split), adjoint_done.reshape(split))
        if section % 2 == 0:
            arrived = (
                lax.all_to_all(outgoing[0], "qa", split_axis=1, concat_axis=1, tiled=True),
                lax.all_to_all(outgoing[1], "qa", split_axis=1, concat_axis=1, tiled=True),
            )
        else:
            arrived = (
                lax.all_to_all(outgoing[0], "qb", split_axis=1, concat_axis=1, tiled=True),
                lax.all_to_all(outgoing[1], "qb", split_axis=1, concat_axis=1, tiled=True),
            )
        state_now = arrived[0].reshape(2, local_count)
        adjoint_now = arrived[1].reshape(2, local_count)
    gradients = jnp.stack(collected)
    return (state_now.reshape(state.shape), adjoint_now.reshape(adjoint.shape), gradients)


def split(x):
    high = x.astype(jnp.bfloat16)
    return high, (x - high.astype(jnp.float32)).astype(jnp.bfloat16)


def dot(left, right, dims):
    part = lambda i, j: lax.dot_general(left[i], right[j], dims, preferred_element_type=jnp.float32)
    return (part(0, 1) + part(1, 0)) + part(0, 0)


def each(operation, *arrays):
    return tuple(operation(*parts) for parts in zip(*arrays))


def wide(arrays):
    return jnp.concatenate(arrays, 1)


def tall(arrays):
    return jnp.concatenate(arrays, 0)


def multiply(left, right):
    size = left[0].shape[0]
    both = dot(split(tall(left)), split(wide(right)), NN)
    return (
        both[:size, :size] - both[size:, size:],
        both[:size, size:] + both[size:, :size],
    )


def multiply_adjoint(left, right):
    size = left[0].shape[0]
    both = dot(split(tall((left[0].T, left[1].T))), split(wide(right)), NN)
    return (
        both[:size, :size] + both[size:, size:],
        both[:size, size:] - both[size:, :size],
    )


def undoing(gate):
    real, imag = gate[0].T, gate[1].T
    return split(tall((wide((real, imag)), wide((-imag, real)))))


def paired(both):
    size = both.shape[0] // 2
    return tall((both[:size, :size] + both[size:, size:], both[size:, :size] - both[:size, size:]))


def exchange(parts, width):
    parts = list(parts)
    lanes = parts[0].shape[-1]
    lane = lax.broadcasted_iota(jnp.int32, parts[0].shape, 1)
    step = 1
    while step < len(parts):
        shift = step * width
        lower = (lane // shift) % 2 == 0
        for index in range(len(parts)):
            if index & step == 0:
                one, two = parts[index], parts[index + step]
                parts[index] = jnp.where(lower, one, pltpu.roll(two, shift, 1))
                parts[index + step] = jnp.where(lower, pltpu.roll(one, lanes - shift, 1), two)
        step *= 2
    return parts


def place_of(low):
    along = lax.axis_index("qb")
    within = lax.shift_right_logical(lax.bitwise_and(along, low - 1), 1)
    return lax.bitwise_and(along, 1), lax.axis_index("qa") * (low // 2) + within


def share_out(sums, low, refs, all_ref):
    for index, term in enumerate(sums):
        all_ref[index] = term
    half, within = place_of(low)
    count, rows = refs[0].shape[0], refs[0].shape[1] // len(sums)
    for other, ref in enumerate(refs):
        for mask in range(count):
            chunk = lax.bitwise_xor(half, other) * count + lax.bitwise_xor(within, mask)
            start = pl.multiple_of(chunk * rows, rows)
            for index in range(len(sums)):
                ref[mask, pl.ds(index * rows, rows), :] = all_ref[index, pl.ds(start, rows), :]


def collect(low, refs, all_ref):
    half, within = place_of(low)
    sums, count, rows = all_ref.shape[0], refs[0].shape[0], refs[0].shape[1] // all_ref.shape[0]
    for other, ref in enumerate(refs):
        for mask in range(count):
            chunk = lax.bitwise_xor(half, other) * count + lax.bitwise_xor(within, mask)
            start = pl.multiple_of(chunk * rows, rows)
            for index in range(sums):
                all_ref[index, pl.ds(start, rows), :] = ref[mask, pl.ds(index * rows, rows), :]


def first_kernel(
    state_hbm, adjoint_hbm, gates_hbm, out_hbm, sums_ref, state_ref, adjoint_ref, gates_ref, out_ref, sem, out_sem
):
    pairs = ((gates_hbm, gates_ref), (state_hbm, state_ref), (adjoint_hbm, adjoint_ref))
    copies = [pltpu.make_async_copy(*pair, sem.at[place]) for place, pair in enumerate(pairs)]
    for copy in copies:
        copy.start()
    size = gates_ref.shape[-1]
    mid = state_ref.shape[1] // size
    total = out_ref.shape[0]
    kept = mid * size // total
    blocks = size // kept
    gate = lambda index: (gates_ref[index, 0], gates_ref[index, 1])

    copies[0].wait()
    four = multiply(multiply(gate(1), gate(3)), multiply(gate(5), gate(7)))
    undo_low = undoing(four)
    undo_high = undoing(gate(0))

    for copy in copies[1:]:
        copy.wait()
    fields = [
        [
            [split(ref[part, pl.ds(j, size, stride=mid), :]) for part in range(2)]
            for j in range(mid)
        ]
        for ref in (state_ref, adjoint_ref)
    ]
    by_low = [each(lambda *a: tall(a), *[each(lambda *b: wide(b), *row) for row in field]) for field in fields]
    by_high = [
        each(lambda *a: tall(a), *[each(lambda *b: wide(b), *[row[part] for row in field]) for part in range(2)])
        for field in fields
    ]
    done = [dot(undo_high, field, NN) for field in by_high]
    copies = []
    for j in range(mid):
        here = slice(j * size, (j + 1) * size)
        rows = tall([wide((field[:size, here], field[size:, here])) for field in done])
        sent = dot(undo_low, split(rows), NT)
        for block in range(blocks):
            for f in range(2):
                for part in range(2):
                    start = part * size + block * kept
                    out_ref[j * blocks + block, pl.ds((f * 2 + part) * kept, kept), :] = sent[
                        start : start + kept, f * size : (f + 1) * size
                    ]
        mine = pl.ds(j * blocks, blocks)
        copies.append(pltpu.make_async_copy(out_ref.at[mine], out_hbm.at[mine], out_sem.at[j]))
        copies[-1].start()
    sums_ref[0] = paired(dot(by_low[1], by_low[0], TN))
    sums_ref[1] = paired(dot(by_high[1], by_high[0], NT))
    for copy in copies:
        copy.wait()


def second_kernel(na, low, got_ref, gates_ref, early_ref, out_hbm, own_ref, other_ref, all_ref, out_ref, sem):
    size = gates_ref.shape[-1]
    total = got_ref.shape[0]
    nb = total // na
    inner = nb // na
    tail = size // nb
    kept = size // inner
    gate = lambda index: (gates_ref[index, 0], gates_ref[index, 1])

    fields = []
    for f in range(2):
        parts = []
        for part in range(2):
            start = (f * 2 + part) * kept
            rows = [got_ref[pl.ds(a * nb, nb), pl.ds(start, kept), :].reshape(nb * kept, size) for a in range(na)]
            parts.append(tall(exchange(rows, size // na)))
        fields.append(split(wide(parts)))
    sums = [paired(dot(fields[1], fields[0], TN))]
    undo = undoing(gate(2))
    after = []
    for f in range(2):
        done = dot(undo, fields[f], NT)
        after.append(done)
    lists = []
    for h in range(inner):
        pieces = []
        for f in range(2):
            for block in range(na * na):
                cut = after[f][:, block * size : (block + 1) * size]
                pieces.append(cut.reshape(2 * na, inner, tail, size)[:, h].reshape(2 * na * tail, size))
        lists.append(tall(pieces))
    turned = exchange(lists, kept)
    turned = [item.reshape(2, na, na, 2, na, tail, size) for item in turned]

    fields = []
    for f in range(2):
        columns = []
        for top in range(na):
            for a in range(na):
                rows = [
                    turned[b][f, top, B, part, a]
                    for part in range(2)
                    for B in range(na)
                    for b in range(inner)
                ]
                columns.append(tall(rows))
        fields.append(split(wide(columns)))
    sums.append(paired(dot(fields[1], fields[0], NT)))
    undo = undoing(gate(4))
    after = [dot(undo, field, NN) for field in fields]

    span = inner * tail
    fields = []
    for f in range(2):
        columns = []
        for a in range(na):
            for B in range(na):
                rows = []
                for part in range(2):
                    for top in range(na):
                        row = (part * na + B) * span
                        column = (top * na + a) * size
                        rows.append(after[f][row : row + span, column : column + size])
                columns.append(tall(rows))
        fields.append(split(wide(columns)))
    undo = undoing(gate(6))
    copies = []
    for f in range(2):
        done = dot(undo, fields[f], NN)
        for part in range(2):
            for a in range(na):
                for B in range(na):
                    column = (a * na + B) * size
                    for top in range(na):
                        for b in range(inner):
                            row = ((part * na + top) * inner + b) * tail
                            out_ref[
                                (B * na + top) * inner + b,
                                pl.ds(((f * 2 + part) * na + a) * tail, tail),
                                :,
                            ] = done[row : row + tail, column : column + size]
        mine = (slice(None), pl.ds(f * 2 * kept, 2 * kept))
        copies.append(pltpu.make_async_copy(out_ref.at[mine], out_hbm.at[mine], sem.at[f]))
        copies[-1].start()
    sums.append(paired(dot(fields[1], fields[0], NT)))

    early = [early_ref[place] for place in range(early_ref.shape[0])]
    share_out(early + sums, low, (own_ref, other_ref), all_ref)
    for copy in copies:
        copy.wait()


def third_kernel(na, nb, got_ref, gates_ref, state_ref, adjoint_ref, chain_ref):
    total, _, size = got_ref.shape
    rest = state_ref.shape[1]
    mid = rest // size
    inner = nb // na
    tail = size // nb
    kept = size // inner
    blocks = total // mid
    for j in range(mid):
        lists = [
            got_ref[j * blocks + block, pl.ds(0, 4 * kept), :] for block in range(blocks)
        ]
        turned = exchange(lists, kept)
        for h in range(inner):
            for f, ref in enumerate((state_ref, adjoint_ref)):
                for part in range(2):
                    for a in range(na):
                        row = ((f * 2 + part) * na + a) * tail
                        ref[part, pl.ds(((a * inner + h) * tail) * mid + j, tail, stride=mid), :] = turned[h][
                            row : row + tail
                        ]
    gate = lambda index: (gates_ref[index, 0], gates_ref[index, 1])
    two = multiply(gate(1), gate(3))
    three = multiply(two, gate(5))
    four = multiply(two, multiply(gate(5), gate(7)))
    for place, product in enumerate((two, three, four)):
        chain_ref[place, 0] = product[0]
        chain_ref[place, 1] = product[1]


def gradient_kernel(scaling, low, gates_ref, chain_ref, own_ref, other_ref, out_hbm, all_ref, out_ref, sem):
    size = gates_ref.shape[-1]
    gate = lambda index: (gates_ref[index, 0], gates_ref[index, 1])
    collect(low, (own_ref, other_ref), all_ref)
    sums = lambda place: (all_ref[place, :size] * scaling, all_ref[place, size:] * scaling)
    chain = [gate(1)] + [(chain_ref[place, 0], chain_ref[place, 1]) for place in range(3)]
    copies = []
    for index in range(gates_ref.shape[0]):
        if index % 2 == 0:
            grad = multiply(sums(1 + index // 2), gate(index))
        else:
            grad = multiply(sums(0), chain[index // 2])
            if index > 1:
                grad = multiply_adjoint(chain[index // 2 - 1], grad)
        out_ref[index, 0] = grad[0]
        out_ref[index, 1] = grad[1]
        copies.append(pltpu.make_async_copy(out_ref.at[index], out_hbm.at[index], sem.at[index]))
        copies[-1].start()
    for copy in copies:
        copy.wait()


def from_mask(value, mask, total):
    return lax.ppermute(value, AXES, [(device, device ^ mask) for device in range(total)])


def tree(terms):
    while len(terms) > 1:
        terms = [one + two for one, two in zip(terms[::2], terms[1::2])]
    return terms[0]


def reduce_all(own, other, pair, near, far, total):
    half = own + from_mask(other, pair, total)
    mine = tree([half[0]] + [from_mask(half[place], mask, total) for place, mask in enumerate(near) if place])
    for mask in far:
        mine = mine + from_mask(mine, mask, total)
    half = jnp.stack([mine] + [from_mask(mine, mask, total) for mask in near[1:]])
    return half, from_mask(half, pair, total)


def shards(state, adjoint, gates):
    size = gates.shape[-1]
    count = state.shape[-1]
    na, nb = lax.axis_size("qa"), lax.axis_size("qb")
    total = na * nb
    scaling = float(total * count // size) ** (-0.5)
    rest = count // size
    kept = rest // total
    inner, tail = nb // na, size // nb
    if gates.shape[0] != 8 or inner * kept != size or tail != 8:
        return stepwise(state, adjoint, gates)

    low = 1 << ((nb.bit_length() - 1) // 2)
    near = [a * nb + b for a in range(na) for b in range(0, low, 2)]
    far = [1 << bit for bit in range(low.bit_length() - 1, nb.bit_length() - 1)]
    shape = lambda *dims: jax.ShapeDtypeStruct(dims, jnp.float32)
    flat = (2, rest, size)
    chunks = shape(len(near), 5 * size // len(near), size)
    vmem = pl.BlockSpec(memory_space=pltpu.VMEM)
    hbm = pl.BlockSpec(memory_space=pltpu.HBM)
    buffer = lambda *dims: pltpu.VMEM(dims, jnp.float32)

    def call(kernel, name, out_shape, scratch=(), grant=48 * 2**20, **options):
        return pl.pallas_call(
            kernel,
            out_shape=out_shape,
            scratch_shapes=scratch,
            compiler_params=pltpu.CompilerParams(vmem_limit_bytes=grant),
            name=name,
            **options,
        )

    out, early = call(
        first_kernel,
        "first",
        (shape(total, 4 * kept, size), shape(2, 2 * size, size)),
        [
            buffer(*flat),
            buffer(*flat),
            buffer(*gates.shape),
            buffer(total, 4 * kept, size),
            pltpu.SemaphoreType.DMA((3,)),
            pltpu.SemaphoreType.DMA((rest // size,)),
        ],
        grant=60 * 2**20,
        in_specs=[hbm, hbm, hbm],
        out_specs=[hbm, vmem],
    )(state.reshape(flat), adjoint.reshape(flat), gates)
    got = lax.all_to_all(out, AXES, split_axis=0, concat_axis=0, tiled=True)
    out, own, other = call(
        functools.partial(second_kernel, na, low),
        "second",
        (shape(total, 4 * kept, size), chunks, chunks),
        [buffer(5, 2 * size, size), buffer(total, 4 * kept, size), pltpu.SemaphoreType.DMA((2,))],
        in_specs=[vmem, vmem, vmem],
        out_specs=[hbm, vmem, vmem],
    )(got, gates, early)
    got = lax.all_to_all(out, AXES, split_axis=0, concat_axis=0, tiled=True)
    own, other = reduce_all(own, other, 1, near, far, total)
    state_out, adjoint_out, chain = call(
        functools.partial(third_kernel, na, nb),
        "third",
        (shape(*flat), shape(*flat), shape(3, 2, size, size)),
    )(got, gates)
    grads = call(
        functools.partial(gradient_kernel, scaling, low),
        "gradient",
        shape(*gates.shape),
        [buffer(5, 2 * size, size), buffer(*gates.shape), pltpu.SemaphoreType.DMA((gates.shape[0],))],
        in_specs=[vmem, vmem, vmem, vmem],
        out_specs=hbm,
    )(gates, chain, own, other)
    return state_out.reshape(state.shape), adjoint_out.reshape(adjoint.shape), grads


def solution(mesh):
    in_specs = (P(None, "qa", "qb", None), P(None, "qa", "qb", None), P())
    out_specs = (P(None, "qa", "qb", None), P(None, "qa", "qb", None), P())
    return jax.shard_map(shards, mesh=mesh, in_specs=in_specs, out_specs=out_specs, check_vma=False)
```

```python
import functools

import jax
import jax.numpy as jnp
from jax import lax
from jax.experimental import pallas as pl
from jax.experimental.pallas import tpu as pltpu
from jax.sharding import PartitionSpec as P

AXES = ("qa", "qb")
NN = (((1,), (0,)), ((), ()))
NT = (((1,), (1,)), ((), ()))
TN = (((0,), (0,)), ((), ()))


def contract(left, right, left_dim, right_dim):
    return lax.dot_general(
        left,
        right,
        (((left_dim,), (right_dim,)), ((), ())),
        precision=lax.Precision.HIGHEST,
        preferred_element_type=jnp.float32,
    )


def undo_high(field, gate):
    new_real = contract(gate[0], field[0], 0, 0) + contract(gate[1], field[1], 0, 0)
    new_imag = contract(gate[0], field[1], 0, 0) - contract(gate[1], field[0], 0, 0)
    return jnp.stack([new_real, new_imag])


def undo_low(field, gate):
    new_real = contract(field[0], gate[0], 1, 0) + contract(field[1], gate[1], 1, 0)
    new_imag = contract(field[1], gate[0], 1, 0) - contract(field[0], gate[1], 1, 0)
    return jnp.stack([new_real, new_imag])


def pair_high(adjoint_field, new_field):
    grad_real = contract(adjoint_field[0], new_field[0], 1, 1) + contract(
        adjoint_field[1], new_field[1], 1, 1
    )
    grad_imag = contract(adjoint_field[1], new_field[0], 1, 1) - contract(
        adjoint_field[0], new_field[1], 1, 1
    )
    return jnp.stack([grad_real, grad_imag])


def pair_low(adjoint_field, new_field):
    grad_real = contract(adjoint_field[0], new_field[0], 0, 0) + contract(
        adjoint_field[1], new_field[1], 0, 0
    )
    grad_imag = contract(adjoint_field[1], new_field[0], 0, 0) - contract(
        adjoint_field[0], new_field[1], 0, 0
    )
    return jnp.stack([grad_real, grad_imag])


def stepwise(state, adjoint, gates):
    gate_size = gates.shape[-1]
    local_count = state.shape[-1]
    scaling = float(lax.axis_size("qa") * lax.axis_size("qb") * local_count // gate_size) ** (-0.5)
    state_now = state.reshape(2, local_count)
    adjoint_now = adjoint.reshape(2, local_count)
    collected = []

    def record(term):
        return lax.psum(term, ("qa", "qb"))

    for section in range(gates.shape[0] // 2):
        high_gate = gates[2 * section]
        low_gate = gates[2 * section + 1]
        upright = (2, gate_size, local_count // gate_size)
        state_high = state_now.reshape(upright)
        adjoint_high = adjoint_now.reshape(upright)
        state_new = undo_high(state_high, high_gate)
        collected.append(record(scaling * pair_high(adjoint_high, state_new)))
        adjoint_new = undo_high(adjoint_high, high_gate)
        flat = (2, local_count // gate_size, gate_size)
        state_low = state_new.reshape(flat)
        adjoint_low = adjoint_new.reshape(flat)
        groups = lax.axis_size("qa") if section % 2 == 0 else lax.axis_size("qb")
        state_done = undo_low(state_low, low_gate)
        collected.append(record(scaling * pair_low(adjoint_low, state_done)))
        adjoint_done = undo_low(adjoint_low, low_gate)
        split = (2, groups, local_count // groups)
        outgoing = (state_done.reshape(split), adjoint_done.reshape(split))
        if section % 2 == 0:
            arrived = (
                lax.all_to_all(outgoing[0], "qa", split_axis=1, concat_axis=1, tiled=True),
                lax.all_to_all(outgoing[1], "qa", split_axis=1, concat_axis=1, tiled=True),
            )
        else:
            arrived = (
                lax.all_to_all(outgoing[0], "qb", split_axis=1, concat_axis=1, tiled=True),
                lax.all_to_all(outgoing[1], "qb", split_axis=1, concat_axis=1, tiled=True),
            )
        state_now = arrived[0].reshape(2, local_count)
        adjoint_now = arrived[1].reshape(2, local_count)
    gradients = jnp.stack(collected)
    return (state_now.reshape(state.shape), adjoint_now.reshape(adjoint.shape), gradients)


def split(x):
    high = x.astype(jnp.bfloat16)
    return high, (x - high.astype(jnp.float32)).astype(jnp.bfloat16)


def dot(left, right, dims):
    part = lambda i, j: lax.dot_general(left[i], right[j], dims, preferred_element_type=jnp.float32)
    return (part(0, 1) + part(1, 0)) + part(0, 0)


def each(operation, *arrays):
    return tuple(operation(*parts) for parts in zip(*arrays))


def wide(arrays):
    return jnp.concatenate(arrays, 1)


def tall(arrays):
    return jnp.concatenate(arrays, 0)


def multiply(left, right):
    size = left[0].shape[0]
    both = dot(split(tall(left)), split(wide(right)), NN)
    return (
        both[:size, :size] - both[size:, size:],
        both[:size, size:] + both[size:, :size],
    )


def multiply_adjoint(left, right):
    size = left[0].shape[0]
    both = dot(split(tall((left[0].T, left[1].T))), split(wide(right)), NN)
    return (
        both[:size, :size] + both[size:, size:],
        both[:size, size:] - both[size:, :size],
    )


def undoing(gate):
    real, imag = gate[0].T, gate[1].T
    return split(tall((wide((real, imag)), wide((-imag, real)))))


def paired(both):
    size = both.shape[0] // 2
    return tall((both[:size, :size] + both[size:, size:], both[size:, :size] - both[:size, size:]))


def exchange(parts, width):
    parts = list(parts)
    lanes = parts[0].shape[-1]
    lane = lax.broadcasted_iota(jnp.int32, parts[0].shape, 1)
    step = 1
    while step < len(parts):
        shift = step * width
        lower = (lane // shift) % 2 == 0
        for index in range(len(parts)):
            if index & step == 0:
                one, two = parts[index], parts[index + step]
                parts[index] = jnp.where(lower, one, pltpu.roll(two, shift, 1))
                parts[index + step] = jnp.where(lower, pltpu.roll(one, lanes - shift, 1), two)
        step *= 2
    return parts


def place_of(low):
    along = lax.axis_index("qb")
    within = lax.shift_right_logical(lax.bitwise_and(along, low - 1), 1)
    return lax.bitwise_and(along, 1), lax.axis_index("qa") * (low // 2) + within


def share_out(sums, low, refs, all_ref):
    for index, term in enumerate(sums):
        all_ref[index] = term
    half, within = place_of(low)
    count, rows = refs[0].shape[0], refs[0].shape[1] // len(sums)
    for other, ref in enumerate(refs):
        for mask in range(count):
            chunk = lax.bitwise_xor(half, other) * count + lax.bitwise_xor(within, mask)
            start = pl.multiple_of(chunk * rows, rows)
            for index in range(len(sums)):
                ref[mask, pl.ds(index * rows, rows), :] = all_ref[index, pl.ds(start, rows), :]


def collect(low, refs, all_ref):
    half, within = place_of(low)
    sums, count, rows = all_ref.shape[0], refs[0].shape[0], refs[0].shape[1] // all_ref.shape[0]
    for other, ref in enumerate(refs):
        for mask in range(count):
            chunk = lax.bitwise_xor(half, other) * count + lax.bitwise_xor(within, mask)
            start = pl.multiple_of(chunk * rows, rows)
            for index in range(sums):
                all_ref[index, pl.ds(start, rows), :] = ref[mask, pl.ds(index * rows, rows), :]


def times_gate(both, gate):
    size = both.shape[0] // 2
    term = paired(both)
    return tall(multiply((term[:size], term[size:]), gate))


def rows_low(ref, size):
    mid = ref.shape[1] // size
    return [[split(ref[part, pl.ds(j, size, stride=mid), :]) for part in range(2)] for j in range(mid)]


def rows_high(field):
    return each(
        lambda *a: tall(a), *[each(lambda *b: wide(b), *[row[part] for row in field]) for part in range(2)]
    )


def first_kernel(
    state_hbm, adjoint_hbm, gates_hbm, out_hbm, state_ref, adjoint_ref, gates_ref, out_ref, sem, out_sem
):
    pairs = ((gates_hbm, gates_ref), (state_hbm, state_ref), (adjoint_hbm, adjoint_ref))
    copies = [pltpu.make_async_copy(*pair, sem.at[place]) for place, pair in enumerate(pairs)]
    for copy in copies:
        copy.start()
    size = gates_ref.shape[-1]
    mid = state_ref.shape[1] // size
    total = out_ref.shape[0]
    kept = mid * size // total
    blocks = size // kept
    gate = lambda index: (gates_ref[index, 0], gates_ref[index, 1])

    for copy in copies:
        copy.wait()
    four = multiply(multiply(gate(1), gate(3)), multiply(gate(5), gate(7)))
    undo_low = undoing(four)
    undo_high = undoing(gate(0))
    by_high = [rows_high(rows_low(ref, size)) for ref in (state_ref, adjoint_ref)]
    done = [dot(undo_high, field, NN) for field in by_high]
    copies = []
    for j in range(mid):
        here = slice(j * size, (j + 1) * size)
        rows = tall([wide((field[:size, here], field[size:, here])) for field in done])
        sent = dot(undo_low, split(rows), NT)
        for block in range(blocks):
            for f in range(2):
                for part in range(2):
                    start = part * size + block * kept
                    out_ref[j * blocks + block, pl.ds((f * 2 + part) * kept, kept), :] = sent[
                        start : start + kept, f * size : (f + 1) * size
                    ]
        mine = pl.ds(j * blocks, blocks)
        copies.append(pltpu.make_async_copy(out_ref.at[mine], out_hbm.at[mine], out_sem.at[j]))
        copies[-1].start()
    for copy in copies:
        copy.wait()


def first_sums_kernel(state_ref, adjoint_ref, gates_ref, _, sums_ref):
    size = gates_ref.shape[-1]
    fields = [rows_low(ref, size) for ref in (state_ref, adjoint_ref)]
    by_low = [each(lambda *a: tall(a), *[each(lambda *b: wide(b), *row) for row in field]) for field in fields]
    sums_ref[0] = paired(dot(by_low[1], by_low[0], TN))
    by_high = [rows_high(field) for field in fields]
    sums_ref[1] = times_gate(dot(by_high[1], by_high[0], NT), (gates_ref[0, 0], gates_ref[0, 1]))


def before_gates(na, got_ref, gates_ref):
    size = gates_ref.shape[-1]
    total = got_ref.shape[0]
    nb = total // na
    inner = nb // na
    tail = size // nb
    kept = size // inner
    gate = lambda index: (gates_ref[index, 0], gates_ref[index, 1])

    fields = []
    for f in range(2):
        parts = []
        for part in range(2):
            start = (f * 2 + part) * kept
            rows = [got_ref[pl.ds(a * nb, nb), pl.ds(start, kept), :].reshape(nb * kept, size) for a in range(na)]
            parts.append(tall(exchange(rows, size // na)))
        fields.append(split(wide(parts)))
    before = [fields]
    undo = undoing(gate(2))
    after = []
    for f in range(2):
        done = dot(undo, fields[f], NT)
        after.append(done)
    lists = []
    for h in range(inner):
        pieces = []
        for f in range(2):
            for block in range(na * na):
                cut = after[f][:, block * size : (block + 1) * size]
                pieces.append(cut.reshape(2 * na, inner, tail, size)[:, h].reshape(2 * na * tail, size))
        lists.append(tall(pieces))
    turned = exchange(lists, kept)
    turned = [item.reshape(2, na, na, 2, na, tail, size) for item in turned]

    fields = []
    for f in range(2):
        columns = []
        for top in range(na):
            for a in range(na):
                rows = [
                    turned[b][f, top, B, part, a]
                    for part in range(2)
                    for B in range(na)
                    for b in range(inner)
                ]
                columns.append(tall(rows))
        fields.append(split(wide(columns)))
    before.append(fields)
    undo = undoing(gate(4))
    after = [dot(undo, field, NN) for field in fields]

    span = inner * tail
    fields = []
    for f in range(2):
        columns = []
        for a in range(na):
            for B in range(na):
                rows = []
                for part in range(2):
                    for top in range(na):
                        row = (part * na + B) * span
                        column = (top * na + a) * size
                        rows.append(after[f][row : row + span, column : column + size])
                columns.append(tall(rows))
        fields.append(split(wide(columns)))
    return before + [fields]


def second_kernel(na, got_ref, gates_ref, _, out_hbm, out_ref, sem):
    size = gates_ref.shape[-1]
    total = got_ref.shape[0]
    inner = total // na // na
    tail = size // (total // na)
    kept = size // inner
    fields = before_gates(na, got_ref, gates_ref)[-1]
    undo = undoing((gates_ref[6, 0], gates_ref[6, 1]))
    copies = []
    for f in range(2):
        done = dot(undo, fields[f], NN)
        for part in range(2):
            for a in range(na):
                for B in range(na):
                    column = (a * na + B) * size
                    for top in range(na):
                        for b in range(inner):
                            row = ((part * na + top) * inner + b) * tail
                            out_ref[
                                (B * na + top) * inner + b,
                                pl.ds(((f * 2 + part) * na + a) * tail, tail),
                                :,
                            ] = done[row : row + tail, column : column + size]
        mine = (slice(None), pl.ds(f * 2 * kept, 2 * kept))
        copies.append(pltpu.make_async_copy(out_ref.at[mine], out_hbm.at[mine], sem.at[f]))
        copies[-1].start()
    for copy in copies:
        copy.wait()


def second_sums_kernel(na, low, got_ref, gates_ref, early_ref, _, own_ref, other_ref, all_ref):
    sums = [early_ref[place] for place in range(early_ref.shape[0])]
    for place, fields in enumerate(before_gates(na, got_ref, gates_ref)):
        index = 2 * place + 2
        both = dot(fields[1], fields[0], NT if place else TN)
        sums.append(times_gate(both, (gates_ref[index, 0], gates_ref[index, 1])))
    share_out(sums, low, (own_ref, other_ref), all_ref)


def third_kernel(na, nb, got_ref, gates_ref, state_ref, adjoint_ref, chain_ref):
    total, _, size = got_ref.shape
    rest = state_ref.shape[1]
    mid = rest // size
    inner = nb // na
    tail = size // nb
    kept = size // inner
    blocks = total // mid
    for j in range(mid):
        lists = [
            got_ref[j * blocks + block, pl.ds(0, 4 * kept), :] for block in range(blocks)
        ]
        turned = exchange(lists, kept)
        for h in range(inner):
            for f, ref in enumerate((state_ref, adjoint_ref)):
                for part in range(2):
                    for a in range(na):
                        row = ((f * 2 + part) * na + a) * tail
                        ref[part, pl.ds(((a * inner + h) * tail) * mid + j, tail, stride=mid), :] = turned[h][
                            row : row + tail
                        ]
    gate = lambda index: (gates_ref[index, 0], gates_ref[index, 1])
    two = multiply(gate(1), gate(3))
    three = multiply(two, gate(5))
    four = multiply(two, multiply(gate(5), gate(7)))
    for place, product in enumerate((two, three, four)):
        chain_ref[place, 0] = product[0]
        chain_ref[place, 1] = product[1]


def gradient_kernel(scaling, low, gates_ref, chain_ref, own_ref, other_ref, out_hbm, all_ref, out_ref, sem):
    size = gates_ref.shape[-1]
    gate = lambda index: (gates_ref[index, 0], gates_ref[index, 1])
    collect(low, (own_ref, other_ref), all_ref)
    sums = lambda place: (all_ref[place, :size] * scaling, all_ref[place, size:] * scaling)
    chain = [gate(1)] + [(chain_ref[place, 0], chain_ref[place, 1]) for place in range(3)]
    copies = []
    for index in range(gates_ref.shape[0]):
        if index % 2 == 0:
            grad = sums(1 + index // 2)
        else:
            grad = multiply(sums(0), chain[index // 2])
            if index > 1:
                grad = multiply_adjoint(chain[index // 2 - 1], grad)
        out_ref[index, 0] = grad[0]
        out_ref[index, 1] = grad[1]
        copies.append(pltpu.make_async_copy(out_ref.at[index], out_hbm.at[index], sem.at[index]))
        copies[-1].start()
    for copy in copies:
        copy.wait()


def from_mask(value, mask, total):
    return lax.ppermute(value, AXES, [(device, device ^ mask) for device in range(total)])


def tree(terms):
    while len(terms) > 1:
        terms = [one + two for one, two in zip(terms[::2], terms[1::2])]
    return terms[0]


def reduce_all(own, other, pair, near, far, total):
    half = own + from_mask(other, pair, total)
    mine = tree([half[0]] + [from_mask(half[place], mask, total) for place, mask in enumerate(near) if place])
    for mask in far:
        mine = mine + from_mask(mine, mask, total)
    half = jnp.stack([mine] + [from_mask(mine, mask, total) for mask in near[1:]])
    return half, from_mask(half, pair, total)


def shards(state, adjoint, gates):
    size = gates.shape[-1]
    count = state.shape[-1]
    na, nb = lax.axis_size("qa"), lax.axis_size("qb")
    total = na * nb
    scaling = float(total * count // size) ** (-0.5)
    rest = count // size
    kept = rest // total
    inner, tail = nb // na, size // nb
    if gates.shape[0] != 8 or inner * kept != size or tail != 8:
        return stepwise(state, adjoint, gates)

    low = 1 << ((nb.bit_length() - 1) // 2)
    near = [a * nb + b for a in range(na) for b in range(0, low, 2)]
    far = [1 << bit for bit in range(low.bit_length() - 1, nb.bit_length() - 1)]
    shape = lambda *dims: jax.ShapeDtypeStruct(dims, jnp.float32)
    flat = (2, rest, size)
    chunks = shape(len(near), 5 * size // len(near), size)
    vmem = pl.BlockSpec(memory_space=pltpu.VMEM)
    hbm = pl.BlockSpec(memory_space=pltpu.HBM)
    buffer = lambda *dims: pltpu.VMEM(dims, jnp.float32)

    def call(kernel, name, out_shape, scratch=(), grant=48 * 2**20, **options):
        return pl.pallas_call(
            kernel,
            out_shape=out_shape,
            scratch_shapes=scratch,
            compiler_params=pltpu.CompilerParams(vmem_limit_bytes=grant),
            name=name,
            **options,
        )

    fields = (state.reshape(flat), adjoint.reshape(flat), gates)
    out = call(
        first_kernel,
        "first",
        shape(total, 4 * kept, size),
        [
            buffer(*flat),
            buffer(*flat),
            buffer(*gates.shape),
            buffer(total, 4 * kept, size),
            pltpu.SemaphoreType.DMA((3,)),
            pltpu.SemaphoreType.DMA((rest // size,)),
        ],
        grant=60 * 2**20,
        in_specs=[hbm, hbm, hbm],
        out_specs=hbm,
    )(*fields)
    unread = pl.BlockSpec(memory_space=pl.ANY)
    early = call(
        first_sums_kernel, "first_sums", shape(2, 2 * size, size), in_specs=[vmem, vmem, vmem, unread]
    )(*fields, out)
    got = lax.all_to_all(out, AXES, split_axis=0, concat_axis=0, tiled=True)
    out = call(
        functools.partial(second_kernel, na),
        "second",
        shape(total, 4 * kept, size),
        [buffer(total, 4 * kept, size), pltpu.SemaphoreType.DMA((2,))],
        in_specs=[vmem, vmem, unread],
        out_specs=hbm,
    )(got, gates, early)
    own, other = call(
        functools.partial(second_sums_kernel, na, low),
        "second_sums",
        (chunks, chunks),
        [buffer(5, 2 * size, size)],
        in_specs=[vmem, vmem, vmem, unread],
    )(got, gates, early, out)
    got = lax.all_to_all(out, AXES, split_axis=0, concat_axis=0, tiled=True)
    own, other = reduce_all(own, other, 1, near, far, total)
    state_out, adjoint_out, chain = call(
        functools.partial(third_kernel, na, nb),
        "third",
        (shape(*flat), shape(*flat), shape(3, 2, size, size)),
    )(got, gates)
    grads = call(
        functools.partial(gradient_kernel, scaling, low),
        "gradient",
        shape(*gates.shape),
        [buffer(5, 2 * size, size), buffer(*gates.shape), pltpu.SemaphoreType.DMA((gates.shape[0],))],
        in_specs=[vmem, vmem, vmem, vmem],
        out_specs=hbm,
    )(gates, chain, own, other)
    return state_out.reshape(state.shape), adjoint_out.reshape(adjoint.shape), grads


def solution(mesh):
    in_specs = (P(None, "qa", "qb", None), P(None, "qa", "qb", None), P())
    out_specs = (P(None, "qa", "qb", None), P(None, "qa", "qb", None), P())
    return jax.shard_map(shards, mesh=mesh, in_specs=in_specs, out_specs=out_specs, check_vma=False)
```

```python
import functools

import jax
import jax.numpy as jnp
from jax import lax
from jax.experimental import pallas as pl
from jax.experimental.pallas import tpu as pltpu
from jax.sharding import PartitionSpec as P

AXES = ("qa", "qb")
NN = (((1,), (0,)), ((), ()))
NT = (((1,), (1,)), ((), ()))
TN = (((0,), (0,)), ((), ()))


def contract(left, right, left_dim, right_dim):
    return lax.dot_general(
        left,
        right,
        (((left_dim,), (right_dim,)), ((), ())),
        precision=lax.Precision.HIGHEST,
        preferred_element_type=jnp.float32,
    )


def undo_high(field, gate):
    new_real = contract(gate[0], field[0], 0, 0) + contract(gate[1], field[1], 0, 0)
    new_imag = contract(gate[0], field[1], 0, 0) - contract(gate[1], field[0], 0, 0)
    return jnp.stack([new_real, new_imag])


def undo_low(field, gate):
    new_real = contract(field[0], gate[0], 1, 0) + contract(field[1], gate[1], 1, 0)
    new_imag = contract(field[1], gate[0], 1, 0) - contract(field[0], gate[1], 1, 0)
    return jnp.stack([new_real, new_imag])


def pair_high(adjoint_field, new_field):
    grad_real = contract(adjoint_field[0], new_field[0], 1, 1) + contract(
        adjoint_field[1], new_field[1], 1, 1
    )
    grad_imag = contract(adjoint_field[1], new_field[0], 1, 1) - contract(
        adjoint_field[0], new_field[1], 1, 1
    )
    return jnp.stack([grad_real, grad_imag])


def pair_low(adjoint_field, new_field):
    grad_real = contract(adjoint_field[0], new_field[0], 0, 0) + contract(
        adjoint_field[1], new_field[1], 0, 0
    )
    grad_imag = contract(adjoint_field[1], new_field[0], 0, 0) - contract(
        adjoint_field[0], new_field[1], 0, 0
    )
    return jnp.stack([grad_real, grad_imag])


def stepwise(state, adjoint, gates):
    gate_size = gates.shape[-1]
    local_count = state.shape[-1]
    scaling = float(lax.axis_size("qa") * lax.axis_size("qb") * local_count // gate_size) ** (-0.5)
    state_now = state.reshape(2, local_count)
    adjoint_now = adjoint.reshape(2, local_count)
    collected = []

    def record(term):
        return lax.psum(term, ("qa", "qb"))

    for section in range(gates.shape[0] // 2):
        high_gate = gates[2 * section]
        low_gate = gates[2 * section + 1]
        upright = (2, gate_size, local_count // gate_size)
        state_high = state_now.reshape(upright)
        adjoint_high = adjoint_now.reshape(upright)
        state_new = undo_high(state_high, high_gate)
        collected.append(record(scaling * pair_high(adjoint_high, state_new)))
        adjoint_new = undo_high(adjoint_high, high_gate)
        flat = (2, local_count // gate_size, gate_size)
        state_low = state_new.reshape(flat)
        adjoint_low = adjoint_new.reshape(flat)
        groups = lax.axis_size("qa") if section % 2 == 0 else lax.axis_size("qb")
        state_done = undo_low(state_low, low_gate)
        collected.append(record(scaling * pair_low(adjoint_low, state_done)))
        adjoint_done = undo_low(adjoint_low, low_gate)
        split = (2, groups, local_count // groups)
        outgoing = (state_done.reshape(split), adjoint_done.reshape(split))
        if section % 2 == 0:
            arrived = (
                lax.all_to_all(outgoing[0], "qa", split_axis=1, concat_axis=1, tiled=True),
                lax.all_to_all(outgoing[1], "qa", split_axis=1, concat_axis=1, tiled=True),
            )
        else:
            arrived = (
                lax.all_to_all(outgoing[0], "qb", split_axis=1, concat_axis=1, tiled=True),
                lax.all_to_all(outgoing[1], "qb", split_axis=1, concat_axis=1, tiled=True),
            )
        state_now = arrived[0].reshape(2, local_count)
        adjoint_now = arrived[1].reshape(2, local_count)
    gradients = jnp.stack(collected)
    return (state_now.reshape(state.shape), adjoint_now.reshape(adjoint.shape), gradients)


def split(x):
    high = x.astype(jnp.bfloat16)
    return high, (x - high.astype(jnp.float32)).astype(jnp.bfloat16)


def dot(left, right, dims):
    part = lambda i, j: lax.dot_general(left[i], right[j], dims, preferred_element_type=jnp.float32)
    return (part(0, 1) + part(1, 0)) + part(0, 0)


def each(operation, *arrays):
    return tuple(operation(*parts) for parts in zip(*arrays))


def wide(arrays):
    return jnp.concatenate(arrays, 1)


def tall(arrays):
    return jnp.concatenate(arrays, 0)


def multiply(left, right):
    size = left[0].shape[0]
    both = dot(split(tall(left)), split(wide(right)), NN)
    return (
        both[:size, :size] - both[size:, size:],
        both[:size, size:] + both[size:, :size],
    )


def multiply_adjoint(left, right):
    size = left[0].shape[0]
    both = dot(split(tall((left[0].T, left[1].T))), split(wide(right)), NN)
    return (
        both[:size, :size] + both[size:, size:],
        both[:size, size:] - both[size:, :size],
    )


def undoing(gate):
    real, imag = gate[0].T, gate[1].T
    return split(tall((wide((real, imag)), wide((-imag, real)))))


def paired(both):
    size = both.shape[0] // 2
    return tall((both[:size, :size] + both[size:, size:], both[size:, :size] - both[:size, size:]))


def exchange(parts, width):
    parts = list(parts)
    lanes = parts[0].shape[-1]
    lane = lax.broadcasted_iota(jnp.int32, parts[0].shape, 1)
    step = 1
    while step < len(parts):
        shift = step * width
        lower = (lane // shift) % 2 == 0
        for index in range(len(parts)):
            if index & step == 0:
                one, two = parts[index], parts[index + step]
                parts[index] = jnp.where(lower, one, pltpu.roll(two, shift, 1))
                parts[index + step] = jnp.where(lower, pltpu.roll(one, lanes - shift, 1), two)
        step *= 2
    return parts


def place_of(low):
    along = lax.axis_index("qb")
    within = lax.shift_right_logical(lax.bitwise_and(along, low - 1), 1)
    return lax.bitwise_and(along, 1), lax.axis_index("qa") * (low // 2) + within


def share_out(sums, low, refs, all_ref):
    for index, term in enumerate(sums):
        all_ref[index] = term
    half, within = place_of(low)
    count, rows = refs[0].shape[0], refs[0].shape[1] // len(sums)
    for other, ref in enumerate(refs):
        for mask in range(count):
            chunk = lax.bitwise_xor(half, other) * count + lax.bitwise_xor(within, mask)
            start = pl.multiple_of(chunk * rows, rows)
            for index in range(len(sums)):
                ref[mask, pl.ds(index * rows, rows), :] = all_ref[index, pl.ds(start, rows), :]


def collect(low, refs, all_ref):
    half, within = place_of(low)
    sums, count, rows = all_ref.shape[0], refs[0].shape[0], refs[0].shape[1] // all_ref.shape[0]
    for other, ref in enumerate(refs):
        for mask in range(count):
            chunk = lax.bitwise_xor(half, other) * count + lax.bitwise_xor(within, mask)
            start = pl.multiple_of(chunk * rows, rows)
            for index in range(sums):
                all_ref[index, pl.ds(start, rows), :] = ref[mask, pl.ds(index * rows, rows), :]


def times_gate(both, gate):
    size = both.shape[0] // 2
    term = paired(both)
    return tall(multiply((term[:size], term[size:]), gate))


def rows_low(ref, size):
    mid = ref.shape[1] // size
    return [[split(ref[part, pl.ds(j, size, stride=mid), :]) for part in range(2)] for j in range(mid)]


def rows_high(field):
    return each(
        lambda *a: tall(a), *[each(lambda *b: wide(b), *[row[part] for row in field]) for part in range(2)]
    )


def first_kernel(
    state_hbm, adjoint_hbm, gates_hbm, out_hbm, state_ref, adjoint_ref, gates_ref, out_ref, sem, out_sem
):
    pairs = ((gates_hbm, gates_ref), (state_hbm, state_ref), (adjoint_hbm, adjoint_ref))
    copies = [pltpu.make_async_copy(*pair, sem.at[place]) for place, pair in enumerate(pairs)]
    for copy in copies:
        copy.start()
    size = gates_ref.shape[-1]
    mid = state_ref.shape[1] // size
    total = out_ref.shape[0]
    kept = mid * size // total
    blocks = size // kept
    gate = lambda index: (gates_ref[index, 0], gates_ref[index, 1])

    for copy in copies:
        copy.wait()
    four = multiply(multiply(gate(1), gate(3)), multiply(gate(5), gate(7)))
    undo_low = undoing(four)
    undo_high = undoing(gate(0))
    by_high = [rows_high(rows_low(ref, size)) for ref in (state_ref, adjoint_ref)]
    done = [dot(undo_high, field, NN) for field in by_high]
    copies = []
    for j in range(mid):
        here = slice(j * size, (j + 1) * size)
        rows = tall([wide((field[:size, here], field[size:, here])) for field in done])
        sent = dot(undo_low, split(rows), NT)
        for block in range(blocks):
            for f in range(2):
                for part in range(2):
                    start = part * size + block * kept
                    out_ref[j * blocks + block, pl.ds((f * 2 + part) * kept, kept), :] = sent[
                        start : start + kept, f * size : (f + 1) * size
                    ]
        mine = pl.ds(j * blocks, blocks)
        copies.append(pltpu.make_async_copy(out_ref.at[mine], out_hbm.at[mine], out_sem.at[j]))
        copies[-1].start()
    for copy in copies:
        copy.wait()


def first_sums_kernel(state_ref, adjoint_ref, gates_ref, _, sums_ref):
    size = gates_ref.shape[-1]
    fields = [rows_low(ref, size) for ref in (state_ref, adjoint_ref)]
    by_low = [each(lambda *a: tall(a), *[each(lambda *b: wide(b), *row) for row in field]) for field in fields]
    sums_ref[0] = paired(dot(by_low[1], by_low[0], TN))
    by_high = [rows_high(field) for field in fields]
    sums_ref[1] = times_gate(dot(by_high[1], by_high[0], NT), (gates_ref[0, 0], gates_ref[0, 1]))


def before_gates(na, f, got_ref, gates_ref, undos):
    size = gates_ref.shape[-1]
    total = got_ref.shape[0]
    nb = total // na
    inner = nb // na
    tail = size // nb
    kept = size // inner

    parts = []
    for part in range(2):
        start = (f * 2 + part) * kept
        rows = [got_ref[pl.ds(a * nb, nb), pl.ds(start, kept), :].reshape(nb * kept, size) for a in range(na)]
        parts.append(tall(exchange(rows, size // na)))
    before = [split(wide(parts))]
    after = dot(undos[0], before[0], NT)
    lists = []
    for h in range(inner):
        pieces = []
        for block in range(na * na):
            cut = after[:, block * size : (block + 1) * size]
            pieces.append(cut.reshape(2 * na, inner, tail, size)[:, h].reshape(2 * na * tail, size))
        lists.append(tall(pieces))
    turned = [item.reshape(na, na, 2, na, tail, size) for item in exchange(lists, kept)]

    columns = []
    for top in range(na):
        for a in range(na):
            rows = [
                turned[b][top, B, part, a] for part in range(2) for B in range(na) for b in range(inner)
            ]
            columns.append(tall(rows))
    before.append(split(wide(columns)))
    after = dot(undos[1], before[1], NN)

    span = inner * tail
    columns = []
    for a in range(na):
        for B in range(na):
            rows = []
            for part in range(2):
                for top in range(na):
                    row = (part * na + B) * span
                    column = (top * na + a) * size
                    rows.append(after[row : row + span, column : column + size])
            columns.append(tall(rows))
    before.append(split(wide(columns)))
    return before


def last_gate(na, undo, field, out_ref):
    size = out_ref.shape[2]
    inner = out_ref.shape[0] // na // na
    tail = size // (inner * na)
    done = dot(undo, field, NN)
    for part in range(2):
        for a in range(na):
            for B in range(na):
                column = (a * na + B) * size
                for top in range(na):
                    for b in range(inner):
                        row = ((part * na + top) * inner + b) * tail
                        out_ref[(B * na + top) * inner + b, pl.ds((part * na + a) * tail, tail), :] = done[
                            row : row + tail, column : column + size
                        ]


def undoings(gates_ref):
    return [undoing((gates_ref[index, 0], gates_ref[index, 1])) for index in (2, 4, 6)]


def second_kernel(na, got_ref, gates_ref, _, out_ref):
    undos = undoings(gates_ref)
    last_gate(na, undos[2], before_gates(na, 0, got_ref, gates_ref, undos)[-1], out_ref)


def second_sums_kernel(
    na, low, got_ref, gates_ref, early_ref, _, own_ref, other_ref, out_hbm, all_ref, out_ref, sem
):
    undos = undoings(gates_ref)
    befores = [before_gates(na, f, got_ref, gates_ref, undos) for f in range(2)]
    sums = [early_ref[place] for place in range(early_ref.shape[0])]
    for place, (state, adjoint) in enumerate(zip(*befores)):
        index = 2 * place + 2
        both = dot(adjoint, state, NT if place else TN)
        sums.append(times_gate(both, (gates_ref[index, 0], gates_ref[index, 1])))
    last_gate(na, undos[2], befores[1][-1], out_ref)
    copy = pltpu.make_async_copy(out_ref, out_hbm, sem)
    copy.start()
    share_out(sums, low, (own_ref, other_ref), all_ref)
    copy.wait()


def hold_kernel(held_ref, _, out_ref):
    pass


def third_kernel(na, nb, got_ref, out_ref):
    total, _, size = got_ref.shape
    mid = out_ref.shape[1] // size
    inner = nb // na
    tail = size // nb
    kept = size // inner
    blocks = total // mid
    for j in range(mid):
        lists = [got_ref[j * blocks + block] for block in range(blocks)]
        turned = exchange(lists, kept)
        for h in range(inner):
            for part in range(2):
                for a in range(na):
                    row = (part * na + a) * tail
                    out_ref[part, pl.ds(((a * inner + h) * tail) * mid + j, tail, stride=mid), :] = turned[h][
                        row : row + tail
                    ]


def third_state_kernel(na, nb, got_ref, gates_ref, out_ref, chain_ref):
    third_kernel(na, nb, got_ref, out_ref)
    gate = lambda index: (gates_ref[index, 0], gates_ref[index, 1])
    two = multiply(gate(1), gate(3))
    three = multiply(two, gate(5))
    four = multiply(two, multiply(gate(5), gate(7)))
    for place, product in enumerate((two, three, four)):
        chain_ref[place, 0] = product[0]
        chain_ref[place, 1] = product[1]


def gradient_kernel(scaling, low, gates_ref, chain_ref, own_ref, other_ref, out_hbm, all_ref, out_ref, sem):
    size = gates_ref.shape[-1]
    gate = lambda index: (gates_ref[index, 0], gates_ref[index, 1])
    collect(low, (own_ref, other_ref), all_ref)
    sums = lambda place: (all_ref[place, :size] * scaling, all_ref[place, size:] * scaling)
    chain = [gate(1)] + [(chain_ref[place, 0], chain_ref[place, 1]) for place in range(3)]
    copies = []
    for index in range(gates_ref.shape[0]):
        if index % 2 == 0:
            grad = sums(1 + index // 2)
        else:
            grad = multiply(sums(0), chain[index // 2])
            if index > 1:
                grad = multiply_adjoint(chain[index // 2 - 1], grad)
        out_ref[index, 0] = grad[0]
        out_ref[index, 1] = grad[1]
        copies.append(pltpu.make_async_copy(out_ref.at[index], out_hbm.at[index], sem.at[index]))
        copies[-1].start()
    for copy in copies:
        copy.wait()


def from_mask(value, mask, total):
    return lax.ppermute(value, AXES, [(device, device ^ mask) for device in range(total)])


def tree(terms):
    while len(terms) > 1:
        terms = [one + two for one, two in zip(terms[::2], terms[1::2])]
    return terms[0]


def reduce_there(own, other, pair, near, far, total):
    half = own + from_mask(other, pair, total)
    mine = tree([half[0]] + [from_mask(half[place], mask, total) for place, mask in enumerate(near) if place])
    for mask in far:
        mine = mine + from_mask(mine, mask, total)
    return mine


def reduce_back(mine, pair, near, total):
    half = jnp.stack([mine] + [from_mask(mine, mask, total) for mask in near[1:]])
    return half, from_mask(half, pair, total)


def shards(state, adjoint, gates):
    size = gates.shape[-1]
    count = state.shape[-1]
    na, nb = lax.axis_size("qa"), lax.axis_size("qb")
    total = na * nb
    scaling = float(total * count // size) ** (-0.5)
    rest = count // size
    kept = rest // total
    inner, tail = nb // na, size // nb
    if gates.shape[0] != 8 or inner * kept != size or tail != 8:
        return stepwise(state, adjoint, gates)

    low = 1 << ((nb.bit_length() - 1) // 2)
    near = [a * nb + b for a in range(na) for b in range(0, low, 2)]
    far = [1 << bit for bit in range(low.bit_length() - 1, nb.bit_length() - 1)]
    shape = lambda *dims: jax.ShapeDtypeStruct(dims, jnp.float32)
    flat = (2, rest, size)
    chunks = shape(len(near), 5 * size // len(near), size)
    vmem = pl.BlockSpec(memory_space=pltpu.VMEM)
    hbm = pl.BlockSpec(memory_space=pltpu.HBM)
    buffer = lambda *dims: pltpu.VMEM(dims, jnp.float32)

    def call(kernel, name, out_shape, scratch=(), grant=48 * 2**20, **options):
        return pl.pallas_call(
            kernel,
            out_shape=out_shape,
            scratch_shapes=scratch,
            compiler_params=pltpu.CompilerParams(vmem_limit_bytes=grant),
            name=name,
            **options,
        )

    fields = (state.reshape(flat), adjoint.reshape(flat), gates)
    out = call(
        first_kernel,
        "first",
        shape(total, 4 * kept, size),
        [
            buffer(*flat),
            buffer(*flat),
            buffer(*gates.shape),
            buffer(total, 4 * kept, size),
            pltpu.SemaphoreType.DMA((3,)),
            pltpu.SemaphoreType.DMA((rest // size,)),
        ],
        grant=60 * 2**20,
        in_specs=[hbm, hbm, hbm],
        out_specs=hbm,
    )(*fields)
    unread = pl.BlockSpec(memory_space=pl.ANY)
    early = call(
        first_sums_kernel, "first_sums", shape(2, 2 * size, size), in_specs=[vmem, vmem, vmem, unread]
    )(*fields, out)
    got = lax.all_to_all(out, AXES, split_axis=0, concat_axis=0, tiled=True)
    half = shape(total, 2 * kept, size)
    state_sent = call(
        functools.partial(second_kernel, na), "second", half, in_specs=[vmem, vmem, unread]
    )(got, gates, early)
    state_got = lax.all_to_all(state_sent, AXES, split_axis=0, concat_axis=0, tiled=True)
    own, other, adjoint_sent = call(
        functools.partial(second_sums_kernel, na, low),
        "second_sums",
        (chunks, chunks, half),
        [buffer(5, 2 * size, size), buffer(*half.shape), pltpu.SemaphoreType.DMA],
        in_specs=[vmem, vmem, vmem, unread],
        out_specs=[vmem, vmem, hbm],
    )(got, gates, early, state_sent)
    mine = reduce_there(own, other, 1, near, far, total)
    adjoint_sent = call(
        hold_kernel, "hold", half, in_specs=[hbm, unread], out_specs=hbm, input_output_aliases={0: 0}
    )(adjoint_sent, mine)
    adjoint_got = lax.all_to_all(adjoint_sent, AXES, split_axis=0, concat_axis=0, tiled=True)
    own, other = reduce_back(mine, 1, near, total)
    state_out, chain = call(
        functools.partial(third_state_kernel, na, nb),
        "third_state",
        (shape(*flat), shape(3, 2, size, size)),
    )(state_got, gates)
    adjoint_out = call(functools.partial(third_kernel, na, nb), "third", shape(*flat))(adjoint_got)
    grads = call(
        functools.partial(gradient_kernel, scaling, low),
        "gradient",
        shape(*gates.shape),
        [buffer(5, 2 * size, size), buffer(*gates.shape), pltpu.SemaphoreType.DMA((gates.shape[0],))],
        in_specs=[vmem, vmem, vmem, vmem],
        out_specs=hbm,
    )(gates, chain, own, other)
    return state_out.reshape(state.shape), adjoint_out.reshape(adjoint.shape), grads


def solution(mesh):
    in_specs = (P(None, "qa", "qb", None), P(None, "qa", "qb", None), P())
    out_specs = (P(None, "qa", "qb", None), P(None, "qa", "qb", None), P())
    return jax.shard_map(shards, mesh=mesh, in_specs=in_specs, out_specs=out_specs, check_vma=False)
```

```python
import functools

import jax
import jax.numpy as jnp
from jax import lax
from jax.experimental import pallas as pl
from jax.experimental.pallas import tpu as pltpu
from jax.sharding import PartitionSpec as P

AXES = ("qa", "qb")
NN = (((1,), (0,)), ((), ()))
NT = (((1,), (1,)), ((), ()))
TN = (((0,), (0,)), ((), ()))


def contract(left, right, left_dim, right_dim):
    return lax.dot_general(
        left,
        right,
        (((left_dim,), (right_dim,)), ((), ())),
        precision=lax.Precision.HIGHEST,
        preferred_element_type=jnp.float32,
    )


def undo_high(field, gate):
    new_real = contract(gate[0], field[0], 0, 0) + contract(gate[1], field[1], 0, 0)
    new_imag = contract(gate[0], field[1], 0, 0) - contract(gate[1], field[0], 0, 0)
    return jnp.stack([new_real, new_imag])


def undo_low(field, gate):
    new_real = contract(field[0], gate[0], 1, 0) + contract(field[1], gate[1], 1, 0)
    new_imag = contract(field[1], gate[0], 1, 0) - contract(field[0], gate[1], 1, 0)
    return jnp.stack([new_real, new_imag])


def pair_high(adjoint_field, new_field):
    grad_real = contract(adjoint_field[0], new_field[0], 1, 1) + contract(
        adjoint_field[1], new_field[1], 1, 1
    )
    grad_imag = contract(adjoint_field[1], new_field[0], 1, 1) - contract(
        adjoint_field[0], new_field[1], 1, 1
    )
    return jnp.stack([grad_real, grad_imag])


def pair_low(adjoint_field, new_field):
    grad_real = contract(adjoint_field[0], new_field[0], 0, 0) + contract(
        adjoint_field[1], new_field[1], 0, 0
    )
    grad_imag = contract(adjoint_field[1], new_field[0], 0, 0) - contract(
        adjoint_field[0], new_field[1], 0, 0
    )
    return jnp.stack([grad_real, grad_imag])


def stepwise(state, adjoint, gates):
    gate_size = gates.shape[-1]
    local_count = state.shape[-1]
    scaling = float(lax.axis_size("qa") * lax.axis_size("qb") * local_count // gate_size) ** (-0.5)
    state_now = state.reshape(2, local_count)
    adjoint_now = adjoint.reshape(2, local_count)
    collected = []

    def record(term):
        return lax.psum(term, ("qa", "qb"))

    for section in range(gates.shape[0] // 2):
        high_gate = gates[2 * section]
        low_gate = gates[2 * section + 1]
        upright = (2, gate_size, local_count // gate_size)
        state_high = state_now.reshape(upright)
        adjoint_high = adjoint_now.reshape(upright)
        state_new = undo_high(state_high, high_gate)
        collected.append(record(scaling * pair_high(adjoint_high, state_new)))
        adjoint_new = undo_high(adjoint_high, high_gate)
        flat = (2, local_count // gate_size, gate_size)
        state_low = state_new.reshape(flat)
        adjoint_low = adjoint_new.reshape(flat)
        groups = lax.axis_size("qa") if section % 2 == 0 else lax.axis_size("qb")
        state_done = undo_low(state_low, low_gate)
        collected.append(record(scaling * pair_low(adjoint_low, state_done)))
        adjoint_done = undo_low(adjoint_low, low_gate)
        split = (2, groups, local_count // groups)
        outgoing = (state_done.reshape(split), adjoint_done.reshape(split))
        if section % 2 == 0:
            arrived = (
                lax.all_to_all(outgoing[0], "qa", split_axis=1, concat_axis=1, tiled=True),
                lax.all_to_all(outgoing[1], "qa", split_axis=1, concat_axis=1, tiled=True),
            )
        else:
            arrived = (
                lax.all_to_all(outgoing[0], "qb", split_axis=1, concat_axis=1, tiled=True),
                lax.all_to_all(outgoing[1], "qb", split_axis=1, concat_axis=1, tiled=True),
            )
        state_now = arrived[0].reshape(2, local_count)
        adjoint_now = arrived[1].reshape(2, local_count)
    gradients = jnp.stack(collected)
    return (state_now.reshape(state.shape), adjoint_now.reshape(adjoint.shape), gradients)


def split(x):
    high = x.astype(jnp.bfloat16)
    return high, (x - high.astype(jnp.float32)).astype(jnp.bfloat16)


def dot(left, right, dims):
    part = lambda i, j: lax.dot_general(left[i], right[j], dims, preferred_element_type=jnp.float32)
    return (part(0, 1) + part(1, 0)) + part(0, 0)


def each(operation, *arrays):
    return tuple(operation(*parts) for parts in zip(*arrays))


def wide(arrays):
    return jnp.concatenate(arrays, 1)


def tall(arrays):
    return jnp.concatenate(arrays, 0)


def multiply(left, right):
    size = left[0].shape[0]
    both = dot(split(tall(left)), split(wide(right)), NN)
    return (
        both[:size, :size] - both[size:, size:],
        both[:size, size:] + both[size:, :size],
    )


def multiply_adjoint(left, right):
    size = left[0].shape[0]
    both = dot(split(tall((left[0].T, left[1].T))), split(wide(right)), NN)
    return (
        both[:size, :size] + both[size:, size:],
        both[:size, size:] - both[size:, :size],
    )


def undoing(gate):
    real, imag = gate[0].T, gate[1].T
    return split(tall((wide((real, imag)), wide((-imag, real)))))


def paired(both):
    size = both.shape[0] // 2
    return tall((both[:size, :size] + both[size:, size:], both[size:, :size] - both[:size, size:]))


def exchange(parts, width):
    parts = list(parts)
    lanes = parts[0].shape[-1]
    lane = lax.broadcasted_iota(jnp.int32, parts[0].shape, 1)
    step = 1
    while step < len(parts):
        shift = step * width
        lower = (lane // shift) % 2 == 0
        for index in range(len(parts)):
            if index & step == 0:
                one, two = parts[index], parts[index + step]
                parts[index] = jnp.where(lower, one, pltpu.roll(two, shift, 1))
                parts[index + step] = jnp.where(lower, pltpu.roll(one, lanes - shift, 1), two)
        step *= 2
    return parts


def place_of(low):
    along = lax.axis_index("qb")
    within = lax.shift_right_logical(lax.bitwise_and(along, low - 1), 1)
    return lax.bitwise_and(along, 1), lax.axis_index("qa") * (low // 2) + within


def share_out(sums, low, refs, all_ref):
    for index, term in enumerate(sums):
        all_ref[index] = term
    half, within = place_of(low)
    count, rows = refs[0].shape[0], refs[0].shape[1] // len(sums)
    for other, ref in enumerate(refs):
        for mask in range(count):
            chunk = lax.bitwise_xor(half, other) * count + lax.bitwise_xor(within, mask)
            start = pl.multiple_of(chunk * rows, rows)
            for index in range(len(sums)):
                ref[mask, pl.ds(index * rows, rows), :] = all_ref[index, pl.ds(start, rows), :]


def collect(low, refs, all_ref):
    half, within = place_of(low)
    sums, count, rows = all_ref.shape[0], refs[0].shape[0], refs[0].shape[1] // all_ref.shape[0]
    for other, ref in enumerate(refs):
        for mask in range(count):
            chunk = lax.bitwise_xor(half, other) * count + lax.bitwise_xor(within, mask)
            start = pl.multiple_of(chunk * rows, rows)
            for index in range(sums):
                all_ref[index, pl.ds(start, rows), :] = ref[mask, pl.ds(index * rows, rows), :]


def times_gate(both, gate):
    size = both.shape[0] // 2
    term = paired(both)
    return tall(multiply((term[:size], term[size:]), gate))


def rows_low(ref, size):
    mid = ref.shape[1] // size
    return [[split(ref[part, pl.ds(j, size, stride=mid), :]) for part in range(2)] for j in range(mid)]


def rows_high(field):
    return each(
        lambda *a: tall(a), *[each(lambda *b: wide(b), *[row[part] for row in field]) for part in range(2)]
    )


def first_kernel(
    state_hbm, adjoint_hbm, gates_hbm, out_hbm, state_ref, adjoint_ref, gates_ref, out_ref, sem, out_sem
):
    pairs = ((gates_hbm, gates_ref), (state_hbm, state_ref), (adjoint_hbm, adjoint_ref))
    copies = [pltpu.make_async_copy(*pair, sem.at[place]) for place, pair in enumerate(pairs)]
    for copy in copies:
        copy.start()
    size = gates_ref.shape[-1]
    mid = state_ref.shape[1] // size
    total = out_ref.shape[0]
    kept = mid * size // total
    blocks = size // kept
    gate = lambda index: (gates_ref[index, 0], gates_ref[index, 1])

    for copy in copies:
        copy.wait()
    four = multiply(multiply(gate(1), gate(3)), multiply(gate(5), gate(7)))
    undo_low = undoing(four)
    undo_high = undoing(gate(0))
    by_high = [rows_high(rows_low(ref, size)) for ref in (state_ref, adjoint_ref)]
    done = [dot(undo_high, field, NN) for field in by_high]
    copies = []
    for j in range(mid):
        here = slice(j * size, (j + 1) * size)
        rows = tall([wide((field[:size, here], field[size:, here])) for field in done])
        sent = dot(undo_low, split(rows), NT)
        for block in range(blocks):
            for f in range(2):
                for part in range(2):
                    start = part * size + block * kept
                    out_ref[j * blocks + block, pl.ds((f * 2 + part) * kept, kept), :] = sent[
                        start : start + kept, f * size : (f + 1) * size
                    ]
        mine = pl.ds(j * blocks, blocks)
        copies.append(pltpu.make_async_copy(out_ref.at[mine], out_hbm.at[mine], out_sem.at[j]))
        copies[-1].start()
    for copy in copies:
        copy.wait()


def first_sums_kernel(low, state_ref, adjoint_ref, gates_ref, _, own_ref, other_ref, all_ref):
    size = gates_ref.shape[-1]
    fields = [rows_low(ref, size) for ref in (state_ref, adjoint_ref)]
    by_low = [each(lambda *a: tall(a), *[each(lambda *b: wide(b), *row) for row in field]) for field in fields]
    by_high = [rows_high(field) for field in fields]
    sums = [
        paired(dot(by_low[1], by_low[0], TN)),
        times_gate(dot(by_high[1], by_high[0], NT), (gates_ref[0, 0], gates_ref[0, 1])),
    ]
    share_out(sums, low, (own_ref, other_ref), all_ref)


def before_gates(na, got_ref, gates_ref):
    size = gates_ref.shape[-1]
    total = got_ref.shape[0]
    nb = total // na
    inner = nb // na
    tail = size // nb
    kept = size // inner
    gate = lambda index: (gates_ref[index, 0], gates_ref[index, 1])

    fields = []
    for f in range(2):
        parts = []
        for part in range(2):
            start = (f * 2 + part) * kept
            rows = [got_ref[pl.ds(a * nb, nb), pl.ds(start, kept), :].reshape(nb * kept, size) for a in range(na)]
            parts.append(tall(exchange(rows, size // na)))
        fields.append(split(wide(parts)))
    before = [fields]
    undo = undoing(gate(2))
    after = []
    for f in range(2):
        done = dot(undo, fields[f], NT)
        after.append(done)
    lists = []
    for h in range(inner):
        pieces = []
        for f in range(2):
            for block in range(na * na):
                cut = after[f][:, block * size : (block + 1) * size]
                pieces.append(cut.reshape(2 * na, inner, tail, size)[:, h].reshape(2 * na * tail, size))
        lists.append(tall(pieces))
    turned = exchange(lists, kept)
    turned = [item.reshape(2, na, na, 2, na, tail, size) for item in turned]

    fields = []
    for f in range(2):
        columns = []
        for top in range(na):
            for a in range(na):
                rows = [
                    turned[b][f, top, B, part, a]
                    for part in range(2)
                    for B in range(na)
                    for b in range(inner)
                ]
                columns.append(tall(rows))
        fields.append(split(wide(columns)))
    before.append(fields)
    undo = undoing(gate(4))
    after = [dot(undo, field, NN) for field in fields]

    span = inner * tail
    fields = []
    for f in range(2):
        columns = []
        for a in range(na):
            for B in range(na):
                rows = []
                for part in range(2):
                    for top in range(na):
                        row = (part * na + B) * span
                        column = (top * na + a) * size
                        rows.append(after[f][row : row + span, column : column + size])
                columns.append(tall(rows))
        fields.append(split(wide(columns)))
    return before + [fields]


def second_kernel(na, got_ref, gates_ref, _, out_hbm, out_ref, sem):
    size = gates_ref.shape[-1]
    total = got_ref.shape[0]
    inner = total // na // na
    tail = size // (total // na)
    kept = size // inner
    fields = before_gates(na, got_ref, gates_ref)[-1]
    undo = undoing((gates_ref[6, 0], gates_ref[6, 1]))
    copies = []
    for f in range(2):
        done = dot(undo, fields[f], NN)
        for part in range(2):
            for a in range(na):
                for B in range(na):
                    column = (a * na + B) * size
                    for top in range(na):
                        for b in range(inner):
                            row = ((part * na + top) * inner + b) * tail
                            out_ref[
                                (B * na + top) * inner + b,
                                pl.ds(((f * 2 + part) * na + a) * tail, tail),
                                :,
                            ] = done[row : row + tail, column : column + size]
        mine = (slice(None), pl.ds(f * 2 * kept, 2 * kept))
        copies.append(pltpu.make_async_copy(out_ref.at[mine], out_hbm.at[mine], sem.at[f]))
        copies[-1].start()
    for copy in copies:
        copy.wait()


def second_sums_kernel(na, low, got_ref, gates_ref, _, own_ref, other_ref, all_ref):
    sums = []
    for place, fields in enumerate(before_gates(na, got_ref, gates_ref)):
        index = 2 * place + 2
        both = dot(fields[1], fields[0], NT if place else TN)
        sums.append(times_gate(both, (gates_ref[index, 0], gates_ref[index, 1])))
    share_out(sums, low, (own_ref, other_ref), all_ref)


def third_kernel(na, nb, got_ref, state_ref, adjoint_ref):
    total, _, size = got_ref.shape
    rest = state_ref.shape[1]
    mid = rest // size
    inner = nb // na
    tail = size // nb
    kept = size // inner
    blocks = total // mid
    for j in range(mid):
        lists = [
            got_ref[j * blocks + block, pl.ds(0, 4 * kept), :] for block in range(blocks)
        ]
        turned = exchange(lists, kept)
        for h in range(inner):
            for f, ref in enumerate((state_ref, adjoint_ref)):
                for part in range(2):
                    for a in range(na):
                        row = ((f * 2 + part) * na + a) * tail
                        ref[part, pl.ds(((a * inner + h) * tail) * mid + j, tail, stride=mid), :] = turned[h][
                            row : row + tail
                        ]


def write(grads, out_hbm, out_ref, sem):
    copies = []
    for place, (index, grad) in enumerate(grads):
        out_ref[place, 0] = grad[0]
        out_ref[place, 1] = grad[1]
        copies.append(pltpu.make_async_copy(out_ref.at[place], out_hbm.at[index], sem.at[place]))
        copies[-1].start()
    for copy in copies:
        copy.wait()


def early_kernel(scaling, low, gates_ref, own_ref, other_ref, out_hbm, all_ref, out_ref, sem):
    size = gates_ref.shape[-1]
    gate = lambda index: (gates_ref[index, 0], gates_ref[index, 1])
    collect(low, (own_ref, other_ref), all_ref)
    sums = lambda place: (all_ref[place, :size] * scaling, all_ref[place, size:] * scaling)
    grads = [(0, sums(1))]
    term = sums(0)
    for index in range(1, gates_ref.shape[0], 2):
        grads.append((index, multiply(term, gate(index))))
        term = multiply_adjoint(gate(index), grads[-1][1])
    write(grads, out_hbm, out_ref, sem)


def late_kernel(scaling, low, own_ref, other_ref, _, out_hbm, all_ref, out_ref, sem):
    size = all_ref.shape[-1]
    collect(low, (own_ref, other_ref), all_ref)
    sums = lambda place: (all_ref[place, :size] * scaling, all_ref[place, size:] * scaling)
    write([(2 * place + 2, sums(place)) for place in range(all_ref.shape[0])], out_hbm, out_ref, sem)


def hold_kernel(held_ref, _, out_ref):
    pass


def from_mask(value, mask, total):
    return lax.ppermute(value, AXES, [(device, device ^ mask) for device in range(total)])


def tree(terms):
    while len(terms) > 1:
        terms = [one + two for one, two in zip(terms[::2], terms[1::2])]
    return terms[0]


def reduce_there(own, other, pair, near, far, total):
    half = own + from_mask(other, pair, total)
    mine = [tree([half[0]] + [from_mask(half[place], mask, total) for place, mask in enumerate(near) if place])]
    for mask in far:
        mine.append(mine[-1] + from_mask(mine[-1], mask, total))
    return mine


def reduce_back(mine, pair, near, total):
    half = jnp.stack([mine] + [from_mask(mine, mask, total) for mask in near[1:]])
    return half, from_mask(half, pair, total)


def shards(state, adjoint, gates):
    size = gates.shape[-1]
    count = state.shape[-1]
    na, nb = lax.axis_size("qa"), lax.axis_size("qb")
    total = na * nb
    scaling = float(total * count // size) ** (-0.5)
    rest = count // size
    kept = rest // total
    inner, tail = nb // na, size // nb
    if gates.shape[0] != 8 or inner * kept != size or tail != 8:
        return stepwise(state, adjoint, gates)

    low = 1 << ((nb.bit_length() - 1) // 2)
    near = [a * nb + b for a in range(na) for b in range(0, low, 2)]
    far = [1 << bit for bit in range(low.bit_length() - 1, nb.bit_length() - 1)]
    shape = lambda *dims: jax.ShapeDtypeStruct(dims, jnp.float32)
    flat = (2, rest, size)
    chunks = lambda sums: [shape(len(near), sums * size // len(near), size)] * 2
    vmem = pl.BlockSpec(memory_space=pltpu.VMEM)
    hbm = pl.BlockSpec(memory_space=pltpu.HBM)
    buffer = lambda *dims: pltpu.VMEM(dims, jnp.float32)

    def call(kernel, name, out_shape, scratch=(), grant=48 * 2**20, **options):
        return pl.pallas_call(
            kernel,
            out_shape=out_shape,
            scratch_shapes=scratch,
            compiler_params=pltpu.CompilerParams(vmem_limit_bytes=grant),
            name=name,
            **options,
        )

    fields = (state.reshape(flat), adjoint.reshape(flat), gates)
    out = call(
        first_kernel,
        "first",
        shape(total, 4 * kept, size),
        [
            buffer(*flat),
            buffer(*flat),
            buffer(*gates.shape),
            buffer(total, 4 * kept, size),
            pltpu.SemaphoreType.DMA((3,)),
            pltpu.SemaphoreType.DMA((rest // size,)),
        ],
        grant=60 * 2**20,
        in_specs=[hbm, hbm, hbm],
        out_specs=hbm,
    )(*fields)
    unread = pl.BlockSpec(memory_space=pl.ANY)
    early = call(
        functools.partial(first_sums_kernel, low),
        "first_sums",
        chunks(2),
        [buffer(2, 2 * size, size)],
        in_specs=[vmem, vmem, vmem, unread],
    )(*fields, out)
    got = lax.all_to_all(out, AXES, split_axis=0, concat_axis=0, tiled=True)
    early = reduce_there(*early, 1, near, far, total)
    out = call(
        functools.partial(second_kernel, na),
        "second",
        shape(total, 4 * kept, size),
        [buffer(total, 4 * kept, size), pltpu.SemaphoreType.DMA((2,))],
        in_specs=[vmem, vmem, unread],
        out_specs=hbm,
    )(got, gates, early[-2])
    out = call(
        hold_kernel,
        "hold",
        shape(total, 4 * kept, size),
        in_specs=[hbm, unread],
        out_specs=hbm,
        input_output_aliases={0: 0},
    )(out, early[-1])
    late = call(
        functools.partial(second_sums_kernel, na, low),
        "second_sums",
        chunks(3),
        [buffer(3, 2 * size, size)],
        in_specs=[vmem, vmem, unread],
    )(got, gates, out)
    got = lax.all_to_all(out, AXES, split_axis=0, concat_axis=0, tiled=True)
    early = reduce_back(early[-1], 1, near, total)
    late = reduce_back(reduce_there(*late, 1, near, far, total)[-1], 1, near, total)
    grads = call(
        functools.partial(early_kernel, scaling, low),
        "early",
        shape(*gates.shape),
        [buffer(2, 2 * size, size), buffer(5, 2, size, size), pltpu.SemaphoreType.DMA((5,))],
        in_specs=[vmem, vmem, vmem],
        out_specs=hbm,
    )(gates, *early)
    state_out, adjoint_out = call(
        functools.partial(third_kernel, na, nb), "third", (shape(*flat), shape(*flat))
    )(got)
    grads = call(
        functools.partial(late_kernel, scaling, low),
        "late",
        shape(*gates.shape),
        [buffer(3, 2 * size, size), buffer(3, 2, size, size), pltpu.SemaphoreType.DMA((3,))],
        in_specs=[vmem, vmem, hbm],
        out_specs=hbm,
        input_output_aliases={2: 0},
    )(*late, grads)
    return state_out.reshape(state.shape), adjoint_out.reshape(adjoint.shape), grads


def solution(mesh):
    in_specs = (P(None, "qa", "qb", None), P(None, "qa", "qb", None), P())
    out_specs = (P(None, "qa", "qb", None), P(None, "qa", "qb", None), P())
    return jax.shard_map(shards, mesh=mesh, in_specs=in_specs, out_specs=out_specs, check_vma=False)
```

```python
import functools

import jax
import jax.numpy as jnp
from jax import lax
from jax.experimental import pallas as pl
from jax.experimental.pallas import tpu as pltpu
from jax.sharding import PartitionSpec as P

AXES = ("qa", "qb")
NN = (((1,), (0,)), ((), ()))
NT = (((1,), (1,)), ((), ()))
TN = (((0,), (0,)), ((), ()))


def contract(left, right, left_dim, right_dim):
    return lax.dot_general(
        left,
        right,
        (((left_dim,), (right_dim,)), ((), ())),
        precision=lax.Precision.HIGHEST,
        preferred_element_type=jnp.float32,
    )


def undo_high(field, gate):
    new_real = contract(gate[0], field[0], 0, 0) + contract(gate[1], field[1], 0, 0)
    new_imag = contract(gate[0], field[1], 0, 0) - contract(gate[1], field[0], 0, 0)
    return jnp.stack([new_real, new_imag])


def undo_low(field, gate):
    new_real = contract(field[0], gate[0], 1, 0) + contract(field[1], gate[1], 1, 0)
    new_imag = contract(field[1], gate[0], 1, 0) - contract(field[0], gate[1], 1, 0)
    return jnp.stack([new_real, new_imag])


def pair_high(adjoint_field, new_field):
    grad_real = contract(adjoint_field[0], new_field[0], 1, 1) + contract(
        adjoint_field[1], new_field[1], 1, 1
    )
    grad_imag = contract(adjoint_field[1], new_field[0], 1, 1) - contract(
        adjoint_field[0], new_field[1], 1, 1
    )
    return jnp.stack([grad_real, grad_imag])


def pair_low(adjoint_field, new_field):
    grad_real = contract(adjoint_field[0], new_field[0], 0, 0) + contract(
        adjoint_field[1], new_field[1], 0, 0
    )
    grad_imag = contract(adjoint_field[1], new_field[0], 0, 0) - contract(
        adjoint_field[0], new_field[1], 0, 0
    )
    return jnp.stack([grad_real, grad_imag])


def stepwise(state, adjoint, gates):
    gate_size = gates.shape[-1]
    local_count = state.shape[-1]
    scaling = float(lax.axis_size("qa") * lax.axis_size("qb") * local_count // gate_size) ** (-0.5)
    state_now = state.reshape(2, local_count)
    adjoint_now = adjoint.reshape(2, local_count)
    collected = []

    def record(term):
        return lax.psum(term, ("qa", "qb"))

    for section in range(gates.shape[0] // 2):
        high_gate = gates[2 * section]
        low_gate = gates[2 * section + 1]
        upright = (2, gate_size, local_count // gate_size)
        state_high = state_now.reshape(upright)
        adjoint_high = adjoint_now.reshape(upright)
        state_new = undo_high(state_high, high_gate)
        collected.append(record(scaling * pair_high(adjoint_high, state_new)))
        adjoint_new = undo_high(adjoint_high, high_gate)
        flat = (2, local_count // gate_size, gate_size)
        state_low = state_new.reshape(flat)
        adjoint_low = adjoint_new.reshape(flat)
        groups = lax.axis_size("qa") if section % 2 == 0 else lax.axis_size("qb")
        state_done = undo_low(state_low, low_gate)
        collected.append(record(scaling * pair_low(adjoint_low, state_done)))
        adjoint_done = undo_low(adjoint_low, low_gate)
        split = (2, groups, local_count // groups)
        outgoing = (state_done.reshape(split), adjoint_done.reshape(split))
        if section % 2 == 0:
            arrived = (
                lax.all_to_all(outgoing[0], "qa", split_axis=1, concat_axis=1, tiled=True),
                lax.all_to_all(outgoing[1], "qa", split_axis=1, concat_axis=1, tiled=True),
            )
        else:
            arrived = (
                lax.all_to_all(outgoing[0], "qb", split_axis=1, concat_axis=1, tiled=True),
                lax.all_to_all(outgoing[1], "qb", split_axis=1, concat_axis=1, tiled=True),
            )
        state_now = arrived[0].reshape(2, local_count)
        adjoint_now = arrived[1].reshape(2, local_count)
    gradients = jnp.stack(collected)
    return (state_now.reshape(state.shape), adjoint_now.reshape(adjoint.shape), gradients)


def split(x):
    high = x.astype(jnp.bfloat16)
    return high, (x - high.astype(jnp.float32)).astype(jnp.bfloat16)


def dot(left, right, dims):
    part = lambda i, j: lax.dot_general(left[i], right[j], dims, preferred_element_type=jnp.float32)
    return (part(0, 1) + part(1, 0)) + part(0, 0)


def each(operation, *arrays):
    return tuple(operation(*parts) for parts in zip(*arrays))


def wide(arrays):
    return jnp.concatenate(arrays, 1)


def tall(arrays):
    return jnp.concatenate(arrays, 0)


def multiply(left, right):
    size = left[0].shape[0]
    both = dot(split(tall(left)), split(wide(right)), NN)
    return (
        both[:size, :size] - both[size:, size:],
        both[:size, size:] + both[size:, :size],
    )


def multiply_adjoint(left, right):
    size = left[0].shape[0]
    both = dot(split(tall((left[0].T, left[1].T))), split(wide(right)), NN)
    return (
        both[:size, :size] + both[size:, size:],
        both[:size, size:] - both[size:, :size],
    )


def undoing(gate):
    real, imag = gate[0].T, gate[1].T
    return split(tall((wide((real, imag)), wide((-imag, real)))))


def paired(both):
    size = both.shape[0] // 2
    return tall((both[:size, :size] + both[size:, size:], both[size:, :size] - both[:size, size:]))


def exchange(parts, width):
    parts = list(parts)
    lanes = parts[0].shape[-1]
    lane = lax.broadcasted_iota(jnp.int32, parts[0].shape, 1)
    step = 1
    while step < len(parts):
        shift = step * width
        lower = (lane // shift) % 2 == 0
        for index in range(len(parts)):
            if index & step == 0:
                one, two = parts[index], parts[index + step]
                parts[index] = jnp.where(lower, one, pltpu.roll(two, shift, 1))
                parts[index + step] = jnp.where(lower, pltpu.roll(one, lanes - shift, 1), two)
        step *= 2
    return parts


def place_of(low):
    along = lax.axis_index("qb")
    within = lax.shift_right_logical(lax.bitwise_and(along, low - 1), 1)
    return lax.bitwise_and(along, 1), lax.axis_index("qa") * (low // 2) + within


def share_out(sums, low, refs, all_ref):
    for index, term in enumerate(sums):
        all_ref[index] = term
    half, within = place_of(low)
    count, rows = refs[0].shape[0], refs[0].shape[1] // len(sums)
    for other, ref in enumerate(refs):
        for mask in range(count):
            chunk = lax.bitwise_xor(half, other) * count + lax.bitwise_xor(within, mask)
            start = pl.multiple_of(chunk * rows, rows)
            for index in range(len(sums)):
                ref[mask, pl.ds(index * rows, rows), :] = all_ref[index, pl.ds(start, rows), :]


def collect(low, refs, all_ref):
    half, within = place_of(low)
    sums, count, rows = all_ref.shape[0], refs[0].shape[0], refs[0].shape[1] // all_ref.shape[0]
    for other, ref in enumerate(refs):
        for mask in range(count):
            chunk = lax.bitwise_xor(half, other) * count + lax.bitwise_xor(within, mask)
            start = pl.multiple_of(chunk * rows, rows)
            for index in range(sums):
                all_ref[index, pl.ds(start, rows), :] = ref[mask, pl.ds(index * rows, rows), :]


def times_gate(both, gate):
    size = both.shape[0] // 2
    term = paired(both)
    return tall(multiply((term[:size], term[size:]), gate))


def rows_low(ref, size):
    mid = ref.shape[1] // size
    return [[split(ref[part, pl.ds(j, size, stride=mid), :]) for part in range(2)] for j in range(mid)]


def rows_high(field):
    return each(
        lambda *a: tall(a), *[each(lambda *b: wide(b), *[row[part] for row in field]) for part in range(2)]
    )


def first_kernel(
    state_hbm, adjoint_hbm, gates_hbm, out_hbm, state_ref, adjoint_ref, gates_ref, out_ref, sem, out_sem
):
    pairs = ((gates_hbm, gates_ref), (state_hbm, state_ref), (adjoint_hbm, adjoint_ref))
    copies = [pltpu.make_async_copy(*pair, sem.at[place]) for place, pair in enumerate(pairs)]
    for copy in copies:
        copy.start()
    size = gates_ref.shape[-1]
    mid = state_ref.shape[1] // size
    total = out_ref.shape[0]
    kept = mid * size // total
    blocks = size // kept
    gate = lambda index: (gates_ref[index, 0], gates_ref[index, 1])

    for copy in copies:
        copy.wait()
    four = multiply(multiply(gate(1), gate(3)), multiply(gate(5), gate(7)))
    undo_low = undoing(four)
    undo_high = undoing(gate(0))
    by_high = [rows_high(rows_low(ref, size)) for ref in (state_ref, adjoint_ref)]
    done = [dot(undo_high, field, NN) for field in by_high]
    copies = []
    for j in range(mid):
        here = slice(j * size, (j + 1) * size)
        rows = tall([wide((field[:size, here], field[size:, here])) for field in done])
        sent = dot(undo_low, split(rows), NT)
        for block in range(blocks):
            for f in range(2):
                for part in range(2):
                    start = part * size + block * kept
                    out_ref[j * blocks + block, pl.ds((f * 2 + part) * kept, kept), :] = sent[
                        start : start + kept, f * size : (f + 1) * size
                    ]
        mine = pl.ds(j * blocks, blocks)
        copies.append(pltpu.make_async_copy(out_ref.at[mine], out_hbm.at[mine], out_sem.at[j]))
        copies[-1].start()
    for copy in copies:
        copy.wait()


def first_sums_kernel(low, state_ref, adjoint_ref, gates_ref, _, own_ref, other_ref, all_ref):
    size = gates_ref.shape[-1]
    fields = [rows_low(ref, size) for ref in (state_ref, adjoint_ref)]
    by_low = [each(lambda *a: tall(a), *[each(lambda *b: wide(b), *row) for row in field]) for field in fields]
    by_high = [rows_high(field) for field in fields]
    sums = [
        paired(dot(by_low[1], by_low[0], TN)),
        times_gate(dot(by_high[1], by_high[0], NT), (gates_ref[0, 0], gates_ref[0, 1])),
    ]
    share_out(sums, low, (own_ref, other_ref), all_ref)


def before_gates(na, got_ref, gates_ref):
    size = gates_ref.shape[-1]
    total = got_ref.shape[0]
    nb = total // na
    inner = nb // na
    tail = size // nb
    kept = size // inner
    gate = lambda index: (gates_ref[index, 0], gates_ref[index, 1])

    fields = []
    for f in range(2):
        parts = []
        for part in range(2):
            start = (f * 2 + part) * kept
            rows = [got_ref[pl.ds(a * nb, nb), pl.ds(start, kept), :].reshape(nb * kept, size) for a in range(na)]
            parts.append(tall(exchange(rows, size // na)))
        fields.append(split(wide(parts)))
    before = [fields]
    undo = undoing(gate(2))
    after = []
    for f in range(2):
        done = dot(undo, fields[f], NT)
        after.append(done)
    lists = []
    for h in range(inner):
        pieces = []
        for f in range(2):
            for block in range(na * na):
                cut = after[f][:, block * size : (block + 1) * size]
                pieces.append(cut.reshape(2 * na, inner, tail, size)[:, h].reshape(2 * na * tail, size))
        lists.append(tall(pieces))
    turned = exchange(lists, kept)
    turned = [item.reshape(2, na, na, 2, na, tail, size) for item in turned]

    fields = []
    for f in range(2):
        columns = []
        for top in range(na):
            for a in range(na):
                rows = [
                    turned[b][f, top, B, part, a]
                    for part in range(2)
                    for B in range(na)
                    for b in range(inner)
                ]
                columns.append(tall(rows))
        fields.append(split(wide(columns)))
    before.append(fields)
    undo = undoing(gate(4))
    after = [dot(undo, field, NN) for field in fields]

    span = inner * tail
    fields = []
    for f in range(2):
        columns = []
        for a in range(na):
            for B in range(na):
                rows = []
                for part in range(2):
                    for top in range(na):
                        row = (part * na + B) * span
                        column = (top * na + a) * size
                        rows.append(after[f][row : row + span, column : column + size])
                columns.append(tall(rows))
        fields.append(split(wide(columns)))
    return before + [fields]


def second_kernel(na, got_ref, gates_ref, _, out_hbm, out_ref, sem):
    size = gates_ref.shape[-1]
    total = got_ref.shape[0]
    inner = total // na // na
    tail = size // (total // na)
    kept = size // inner
    fields = before_gates(na, got_ref, gates_ref)[-1]
    undo = undoing((gates_ref[6, 0], gates_ref[6, 1]))
    copies = []
    for f in range(2):
        done = dot(undo, fields[f], NN)
        for part in range(2):
            for a in range(na):
                for B in range(na):
                    column = (a * na + B) * size
                    for top in range(na):
                        for b in range(inner):
                            row = ((part * na + top) * inner + b) * tail
                            out_ref[
                                (B * na + top) * inner + b,
                                pl.ds(((f * 2 + part) * na + a) * tail, tail),
                                :,
                            ] = done[row : row + tail, column : column + size]
        mine = (slice(None), pl.ds(f * 2 * kept, 2 * kept))
        copies.append(pltpu.make_async_copy(out_ref.at[mine], out_hbm.at[mine], sem.at[f]))
        copies[-1].start()
    for copy in copies:
        copy.wait()


def second_sums_kernel(na, low, got_ref, gates_ref, _, own_ref, other_ref, all_ref):
    sums = []
    for place, fields in enumerate(before_gates(na, got_ref, gates_ref)):
        index = 2 * place + 2
        both = dot(fields[1], fields[0], NT if place else TN)
        sums.append(times_gate(both, (gates_ref[index, 0], gates_ref[index, 1])))
    share_out(sums, low, (own_ref, other_ref), all_ref)


def third_kernel(na, nb, got_ref, state_ref, adjoint_ref, token_ref):
    token_ref[...] = jnp.zeros_like(token_ref)
    total, _, size = got_ref.shape
    rest = state_ref.shape[1]
    mid = rest // size
    inner = nb // na
    tail = size // nb
    kept = size // inner
    blocks = total // mid
    for j in range(mid):
        lists = [
            got_ref[j * blocks + block, pl.ds(0, 4 * kept), :] for block in range(blocks)
        ]
        turned = exchange(lists, kept)
        for h in range(inner):
            for f, ref in enumerate((state_ref, adjoint_ref)):
                for part in range(2):
                    for a in range(na):
                        row = ((f * 2 + part) * na + a) * tail
                        ref[part, pl.ds(((a * inner + h) * tail) * mid + j, tail, stride=mid), :] = turned[h][
                            row : row + tail
                        ]


def write(grads, out_hbm, out_ref, sem):
    copies = []
    for place, (index, grad) in enumerate(grads):
        out_ref[place, 0] = grad[0]
        out_ref[place, 1] = grad[1]
        copies.append(pltpu.make_async_copy(out_ref.at[place], out_hbm.at[index], sem.at[place]))
        copies[-1].start()
    for copy in copies:
        copy.wait()


def early_kernel(scaling, low, gates_ref, own_ref, other_ref, out_hbm, token_ref, all_ref, out_ref, sem):
    token_ref[...] = jnp.zeros_like(token_ref)
    size = gates_ref.shape[-1]
    gate = lambda index: (gates_ref[index, 0], gates_ref[index, 1])
    collect(low, (own_ref, other_ref), all_ref)
    sums = lambda place: (all_ref[place, :size] * scaling, all_ref[place, size:] * scaling)
    grads = [(0, sums(1))]
    term = sums(0)
    for index in range(1, gates_ref.shape[0], 2):
        grads.append((index, multiply(term, gate(index))))
        term = multiply_adjoint(gate(index), grads[-1][1])
    write(grads, out_hbm, out_ref, sem)


def late_kernel(scaling, low, own_ref, other_ref, _, out_hbm, all_ref, out_ref, sem):
    size = all_ref.shape[-1]
    collect(low, (own_ref, other_ref), all_ref)
    sums = lambda place: (all_ref[place, :size] * scaling, all_ref[place, size:] * scaling)
    write([(2 * place + 2, sums(place)) for place in range(all_ref.shape[0])], out_hbm, out_ref, sem)


def hold_kernel(held_ref, _, out_ref):
    pass


def from_mask(value, mask, total):
    return lax.ppermute(value, AXES, [(device, device ^ mask) for device in range(total)])


def tree(terms):
    while len(terms) > 1:
        terms = [one + two for one, two in zip(terms[::2], terms[1::2])]
    return terms[0]


def reduce_near(own, other, pair, near, total):
    half = own + from_mask(other, pair, total)
    return tree([half[0]] + [from_mask(half[place], mask, total) for place, mask in enumerate(near) if place])


def reduce_far(mine, far, total):
    for mask in far:
        mine = mine + from_mask(mine, mask, total)
    return mine


def gather_near(mine, near, total):
    return jnp.stack([mine] + [from_mask(mine, mask, total) for mask in near[1:]])


def shards(state, adjoint, gates):
    size = gates.shape[-1]
    count = state.shape[-1]
    na, nb = lax.axis_size("qa"), lax.axis_size("qb")
    total = na * nb
    scaling = float(total * count // size) ** (-0.5)
    rest = count // size
    kept = rest // total
    inner, tail = nb // na, size // nb
    if gates.shape[0] != 8 or inner * kept != size or tail != 8:
        return stepwise(state, adjoint, gates)

    low = 1 << ((nb.bit_length() - 1) // 2)
    near = [a * nb + b for a in range(na) for b in range(0, low, 2)]
    far = [1 << bit for bit in range(low.bit_length() - 1, nb.bit_length() - 1)]
    shape = lambda *dims: jax.ShapeDtypeStruct(dims, jnp.float32)
    flat = (2, rest, size)
    chunks = lambda sums: [shape(len(near), sums * size // len(near), size)] * 2
    vmem = pl.BlockSpec(memory_space=pltpu.VMEM)
    hbm = pl.BlockSpec(memory_space=pltpu.HBM)
    buffer = lambda *dims: pltpu.VMEM(dims, jnp.float32)

    def call(kernel, name, out_shape, scratch=(), grant=48 * 2**20, **options):
        return pl.pallas_call(
            kernel,
            out_shape=out_shape,
            scratch_shapes=scratch,
            compiler_params=pltpu.CompilerParams(vmem_limit_bytes=grant),
            name=name,
            **options,
        )

    unread = pl.BlockSpec(memory_space=pl.ANY)

    def hold(array, operand):
        return call(
            hold_kernel,
            "hold",
            shape(*array.shape),
            in_specs=[unread, unread],
            out_specs=unread,
            input_output_aliases={0: 0},
        )(array, operand)

    fields = (state.reshape(flat), adjoint.reshape(flat), gates)
    out = call(
        first_kernel,
        "first",
        shape(total, 4 * kept, size),
        [
            buffer(*flat),
            buffer(*flat),
            buffer(*gates.shape),
            buffer(total, 4 * kept, size),
            pltpu.SemaphoreType.DMA((3,)),
            pltpu.SemaphoreType.DMA((rest // size,)),
        ],
        grant=60 * 2**20,
        in_specs=[hbm, hbm, hbm],
        out_specs=hbm,
    )(*fields)
    early = call(
        functools.partial(first_sums_kernel, low),
        "first_sums",
        chunks(2),
        [buffer(2, 2 * size, size)],
        in_specs=[vmem, vmem, vmem, unread],
    )(*fields, out)
    got = lax.all_to_all(out, AXES, split_axis=0, concat_axis=0, tiled=True)
    early = reduce_far(reduce_near(*early, 1, near, total), far[:-1], total)
    out = call(
        functools.partial(second_kernel, na),
        "second",
        shape(total, 4 * kept, size),
        [buffer(total, 4 * kept, size), pltpu.SemaphoreType.DMA((2,))],
        in_specs=[vmem, vmem, unread],
        out_specs=hbm,
    )(got, gates, early)
    early = reduce_far(early, far[-1:], total)
    out = hold(out, early)
    late = call(
        functools.partial(second_sums_kernel, na, low),
        "second_sums",
        chunks(3),
        [buffer(3, 2 * size, size)],
        in_specs=[vmem, vmem, unread],
    )(got, gates, out)
    got = lax.all_to_all(out, AXES, split_axis=0, concat_axis=0, tiled=True)
    early = gather_near(early, near, total)
    token = shape(8, size)
    grads, early_made = call(
        functools.partial(early_kernel, scaling, low),
        "early",
        (shape(*gates.shape), token),
        [buffer(2, 2 * size, size), buffer(5, 2, size, size), pltpu.SemaphoreType.DMA((5,))],
        in_specs=[vmem, vmem, vmem],
        out_specs=[hbm, vmem],
    )(gates, early, from_mask(early, 1, total))
    state_out, adjoint_out, fields_made = call(
        functools.partial(third_kernel, na, nb), "third", (shape(*flat), shape(*flat), token)
    )(got)
    late = reduce_far(reduce_near(*late, 1, near, total), far[:-1], total)
    late = reduce_far(hold(late, early_made), far[-1:], total)
    late = hold(gather_near(late, near, total), fields_made)
    grads = call(
        functools.partial(late_kernel, scaling, low),
        "late",
        shape(*gates.shape),
        [buffer(3, 2 * size, size), buffer(3, 2, size, size), pltpu.SemaphoreType.DMA((3,))],
        in_specs=[vmem, vmem, hbm],
        out_specs=hbm,
        input_output_aliases={2: 0},
    )(late, from_mask(late, 1, total), grads)
    return state_out.reshape(state.shape), adjoint_out.reshape(adjoint.shape), grads


def solution(mesh):
    in_specs = (P(None, "qa", "qb", None), P(None, "qa", "qb", None), P())
    out_specs = (P(None, "qa", "qb", None), P(None, "qa", "qb", None), P())
    return jax.shard_map(shards, mesh=mesh, in_specs=in_specs, out_specs=out_specs, check_vma=False)
```

```python
import functools

import jax
import jax.numpy as jnp
from jax import lax
from jax.experimental import pallas as pl
from jax.experimental.pallas import tpu as pltpu
from jax.sharding import PartitionSpec as P

AXES = ("qa", "qb")
NN = (((1,), (0,)), ((), ()))
NT = (((1,), (1,)), ((), ()))
TN = (((0,), (0,)), ((), ()))


def contract(left, right, left_dim, right_dim):
    return lax.dot_general(
        left,
        right,
        (((left_dim,), (right_dim,)), ((), ())),
        precision=lax.Precision.HIGHEST,
        preferred_element_type=jnp.float32,
    )


def undo_high(field, gate):
    new_real = contract(gate[0], field[0], 0, 0) + contract(gate[1], field[1], 0, 0)
    new_imag = contract(gate[0], field[1], 0, 0) - contract(gate[1], field[0], 0, 0)
    return jnp.stack([new_real, new_imag])


def undo_low(field, gate):
    new_real = contract(field[0], gate[0], 1, 0) + contract(field[1], gate[1], 1, 0)
    new_imag = contract(field[1], gate[0], 1, 0) - contract(field[0], gate[1], 1, 0)
    return jnp.stack([new_real, new_imag])


def pair_high(adjoint_field, new_field):
    grad_real = contract(adjoint_field[0], new_field[0], 1, 1) + contract(
        adjoint_field[1], new_field[1], 1, 1
    )
    grad_imag = contract(adjoint_field[1], new_field[0], 1, 1) - contract(
        adjoint_field[0], new_field[1], 1, 1
    )
    return jnp.stack([grad_real, grad_imag])


def pair_low(adjoint_field, new_field):
    grad_real = contract(adjoint_field[0], new_field[0], 0, 0) + contract(
        adjoint_field[1], new_field[1], 0, 0
    )
    grad_imag = contract(adjoint_field[1], new_field[0], 0, 0) - contract(
        adjoint_field[0], new_field[1], 0, 0
    )
    return jnp.stack([grad_real, grad_imag])


def stepwise(state, adjoint, gates):
    gate_size = gates.shape[-1]
    local_count = state.shape[-1]
    scaling = float(lax.axis_size("qa") * lax.axis_size("qb") * local_count // gate_size) ** (-0.5)
    state_now = state.reshape(2, local_count)
    adjoint_now = adjoint.reshape(2, local_count)
    collected = []

    def record(term):
        return lax.psum(term, ("qa", "qb"))

    for section in range(gates.shape[0] // 2):
        high_gate = gates[2 * section]
        low_gate = gates[2 * section + 1]
        upright = (2, gate_size, local_count // gate_size)
        state_high = state_now.reshape(upright)
        adjoint_high = adjoint_now.reshape(upright)
        state_new = undo_high(state_high, high_gate)
        collected.append(record(scaling * pair_high(adjoint_high, state_new)))
        adjoint_new = undo_high(adjoint_high, high_gate)
        flat = (2, local_count // gate_size, gate_size)
        state_low = state_new.reshape(flat)
        adjoint_low = adjoint_new.reshape(flat)
        groups = lax.axis_size("qa") if section % 2 == 0 else lax.axis_size("qb")
        state_done = undo_low(state_low, low_gate)
        collected.append(record(scaling * pair_low(adjoint_low, state_done)))
        adjoint_done = undo_low(adjoint_low, low_gate)
        split = (2, groups, local_count // groups)
        outgoing = (state_done.reshape(split), adjoint_done.reshape(split))
        if section % 2 == 0:
            arrived = (
                lax.all_to_all(outgoing[0], "qa", split_axis=1, concat_axis=1, tiled=True),
                lax.all_to_all(outgoing[1], "qa", split_axis=1, concat_axis=1, tiled=True),
            )
        else:
            arrived = (
                lax.all_to_all(outgoing[0], "qb", split_axis=1, concat_axis=1, tiled=True),
                lax.all_to_all(outgoing[1], "qb", split_axis=1, concat_axis=1, tiled=True),
            )
        state_now = arrived[0].reshape(2, local_count)
        adjoint_now = arrived[1].reshape(2, local_count)
    gradients = jnp.stack(collected)
    return (state_now.reshape(state.shape), adjoint_now.reshape(adjoint.shape), gradients)


def split(x):
    high = x.astype(jnp.bfloat16)
    return high, (x - high.astype(jnp.float32)).astype(jnp.bfloat16)


def dot(left, right, dims):
    part = lambda i, j: lax.dot_general(left[i], right[j], dims, preferred_element_type=jnp.float32)
    return (part(0, 1) + part(1, 0)) + part(0, 0)


def each(operation, *arrays):
    return tuple(operation(*parts) for parts in zip(*arrays))


def wide(arrays):
    return jnp.concatenate(arrays, 1)


def tall(arrays):
    return jnp.concatenate(arrays, 0)


def multiply(left, right):
    size = left[0].shape[0]
    both = dot(split(tall(left)), split(wide(right)), NN)
    return (
        both[:size, :size] - both[size:, size:],
        both[:size, size:] + both[size:, :size],
    )


def multiply_adjoint(left, right):
    size = left[0].shape[0]
    both = dot(split(tall((left[0].T, left[1].T))), split(wide(right)), NN)
    return (
        both[:size, :size] + both[size:, size:],
        both[:size, size:] - both[size:, :size],
    )


def undoing(gate):
    real, imag = gate[0].T, gate[1].T
    return split(tall((wide((real, imag)), wide((-imag, real)))))


def paired(both):
    size = both.shape[0] // 2
    return tall((both[:size, :size] + both[size:, size:], both[size:, :size] - both[:size, size:]))


def exchange(parts, width):
    parts = list(parts)
    lanes = parts[0].shape[-1]
    lane = lax.broadcasted_iota(jnp.int32, parts[0].shape, 1)
    step = 1
    while step < len(parts):
        shift = step * width
        lower = (lane // shift) % 2 == 0
        for index in range(len(parts)):
            if index & step == 0:
                one, two = parts[index], parts[index + step]
                parts[index] = jnp.where(lower, one, pltpu.roll(two, shift, 1))
                parts[index + step] = jnp.where(lower, pltpu.roll(one, lanes - shift, 1), two)
        step *= 2
    return parts


def place_of(low):
    along = lax.axis_index("qb")
    within = lax.shift_right_logical(lax.bitwise_and(along, low - 1), 1)
    return lax.bitwise_and(along, 1), lax.axis_index("qa") * (low // 2) + within


def share_out(sums, low, refs, all_ref):
    for index, term in enumerate(sums):
        all_ref[index] = term
    half, within = place_of(low)
    count, rows = refs[0].shape[0], refs[0].shape[1] // len(sums)
    for other, ref in enumerate(refs):
        for mask in range(count):
            chunk = lax.bitwise_xor(half, other) * count + lax.bitwise_xor(within, mask)
            start = pl.multiple_of(chunk * rows, rows)
            for index in range(len(sums)):
                ref[mask, pl.ds(index * rows, rows), :] = all_ref[index, pl.ds(start, rows), :]


def collect(low, refs, all_ref):
    half, within = place_of(low)
    sums, count, rows = all_ref.shape[0], refs[0].shape[0], refs[0].shape[1] // all_ref.shape[0]
    for other, ref in enumerate(refs):
        for mask in range(count):
            chunk = lax.bitwise_xor(half, other) * count + lax.bitwise_xor(within, mask)
            start = pl.multiple_of(chunk * rows, rows)
            for index in range(sums):
                all_ref[index, pl.ds(start, rows), :] = ref[mask, pl.ds(index * rows, rows), :]


def times_gate(both, gate):
    size = both.shape[0] // 2
    term = paired(both)
    return tall(multiply((term[:size], term[size:]), gate))


def rows_low(ref, size):
    mid = ref.shape[1] // size
    return [[split(ref[part, pl.ds(j, size, stride=mid), :]) for part in range(2)] for j in range(mid)]


def rows_high(field):
    return each(
        lambda *a: tall(a), *[each(lambda *b: wide(b), *[row[part] for row in field]) for part in range(2)]
    )


def first_kernel(
    state_hbm, adjoint_hbm, gates_hbm, out_hbm, state_ref, adjoint_ref, gates_ref, out_ref, sem, out_sem
):
    pairs = ((gates_hbm, gates_ref), (state_hbm, state_ref), (adjoint_hbm, adjoint_ref))
    copies = [pltpu.make_async_copy(*pair, sem.at[place]) for place, pair in enumerate(pairs)]
    for copy in copies:
        copy.start()
    size = gates_ref.shape[-1]
    mid = state_ref.shape[1] // size
    total = out_ref.shape[0]
    kept = mid * size // total
    blocks = size // kept
    gate = lambda index: (gates_ref[index, 0], gates_ref[index, 1])

    for copy in copies:
        copy.wait()
    four = multiply(multiply(gate(1), gate(3)), multiply(gate(5), gate(7)))
    undo_low = undoing(four)
    undo_high = undoing(gate(0))
    by_high = [rows_high(rows_low(ref, size)) for ref in (state_ref, adjoint_ref)]
    done = [dot(undo_high, field, NN) for field in by_high]
    copies = []
    for j in range(mid):
        here = slice(j * size, (j + 1) * size)
        rows = tall([wide((field[:size, here], field[size:, here])) for field in done])
        sent = dot(undo_low, split(rows), NT)
        for block in range(blocks):
            for f in range(2):
                for part in range(2):
                    start = part * size + block * kept
                    out_ref[j * blocks + block, pl.ds((f * 2 + part) * kept, kept), :] = sent[
                        start : start + kept, f * size : (f + 1) * size
                    ]
        mine = pl.ds(j * blocks, blocks)
        copies.append(pltpu.make_async_copy(out_ref.at[mine], out_hbm.at[mine], out_sem.at[j]))
        copies[-1].start()
    for copy in copies:
        copy.wait()


def first_sums_kernel(low, state_ref, adjoint_ref, gates_ref, _, own_ref, other_ref, all_ref):
    size = gates_ref.shape[-1]
    fields = [rows_low(ref, size) for ref in (state_ref, adjoint_ref)]
    by_low = [each(lambda *a: tall(a), *[each(lambda *b: wide(b), *row) for row in field]) for field in fields]
    by_high = [rows_high(field) for field in fields]
    sums = [
        paired(dot(by_low[1], by_low[0], TN)),
        times_gate(dot(by_high[1], by_high[0], NT), (gates_ref[0, 0], gates_ref[0, 1])),
    ]
    share_out(sums, low, (own_ref, other_ref), all_ref)


def before_gates(na, got_ref, gates_ref):
    size = gates_ref.shape[-1]
    total = got_ref.shape[0]
    nb = total // na
    inner = nb // na
    tail = size // nb
    kept = size // inner
    gate = lambda index: (gates_ref[index, 0], gates_ref[index, 1])

    fields = []
    for f in range(2):
        parts = []
        for part in range(2):
            start = (f * 2 + part) * kept
            rows = [got_ref[pl.ds(a * nb, nb), pl.ds(start, kept), :].reshape(nb * kept, size) for a in range(na)]
            parts.append(tall(exchange(rows, size // na)))
        fields.append(split(wide(parts)))
    before = [fields]
    undo = undoing(gate(2))
    after = []
    for f in range(2):
        done = dot(undo, fields[f], NT)
        after.append(done)
    lists = []
    for h in range(inner):
        pieces = []
        for f in range(2):
            for block in range(na * na):
                cut = after[f][:, block * size : (block + 1) * size]
                pieces.append(cut.reshape(2 * na, inner, tail, size)[:, h].reshape(2 * na * tail, size))
        lists.append(tall(pieces))
    turned = exchange(lists, kept)
    turned = [item.reshape(2, na, na, 2, na, tail, size) for item in turned]

    fields = []
    for f in range(2):
        columns = []
        for top in range(na):
            for a in range(na):
                rows = [
                    turned[b][f, top, B, part, a]
                    for part in range(2)
                    for B in range(na)
                    for b in range(inner)
                ]
                columns.append(tall(rows))
        fields.append(split(wide(columns)))
    before.append(fields)
    undo = undoing(gate(4))
    after = [dot(undo, field, NN) for field in fields]

    span = inner * tail
    fields = []
    for f in range(2):
        columns = []
        for a in range(na):
            for B in range(na):
                rows = []
                for part in range(2):
                    for top in range(na):
                        row = (part * na + B) * span
                        column = (top * na + a) * size
                        rows.append(after[f][row : row + span, column : column + size])
                columns.append(tall(rows))
        fields.append(split(wide(columns)))
    return before + [fields]


def second_kernel(na, got_ref, gates_ref, _, out_hbm, out_ref, sem):
    size = gates_ref.shape[-1]
    total = got_ref.shape[0]
    inner = total // na // na
    tail = size // (total // na)
    kept = size // inner
    fields = before_gates(na, got_ref, gates_ref)[-1]
    undo = undoing((gates_ref[6, 0], gates_ref[6, 1]))
    copies = []
    for f in range(2):
        done = dot(undo, fields[f], NN)
        for part in range(2):
            for a in range(na):
                for B in range(na):
                    column = (a * na + B) * size
                    for top in range(na):
                        for b in range(inner):
                            row = ((part * na + top) * inner + b) * tail
                            out_ref[
                                (B * na + top) * inner + b,
                                pl.ds(((f * 2 + part) * na + a) * tail, tail),
                                :,
                            ] = done[row : row + tail, column : column + size]
        mine = (slice(None), pl.ds(f * 2 * kept, 2 * kept))
        copies.append(pltpu.make_async_copy(out_ref.at[mine], out_hbm.at[mine], sem.at[f]))
        copies[-1].start()
    for copy in copies:
        copy.wait()


def second_sums_kernel(na, low, got_ref, gates_ref, _, own_ref, other_ref, all_ref):
    sums = []
    for place, fields in enumerate(before_gates(na, got_ref, gates_ref)):
        index = 2 * place + 2
        both = dot(fields[1], fields[0], NT if place else TN)
        sums.append(times_gate(both, (gates_ref[index, 0], gates_ref[index, 1])))
    share_out(sums, low, (own_ref, other_ref), all_ref)


def third_kernel(na, nb, got_ref, state_ref, adjoint_ref, token_ref):
    token_ref[...] = jnp.zeros_like(token_ref)
    total, _, size = got_ref.shape
    rest = state_ref.shape[1]
    mid = rest // size
    inner = nb // na
    tail = size // nb
    kept = size // inner
    blocks = total // mid
    for j in range(mid):
        lists = [
            got_ref[j * blocks + block, pl.ds(0, 4 * kept), :] for block in range(blocks)
        ]
        turned = exchange(lists, kept)
        for h in range(inner):
            for f, ref in enumerate((state_ref, adjoint_ref)):
                for part in range(2):
                    for a in range(na):
                        row = ((f * 2 + part) * na + a) * tail
                        ref[part, pl.ds(((a * inner + h) * tail) * mid + j, tail, stride=mid), :] = turned[h][
                            row : row + tail
                        ]


def write(grads, out_hbm, out_ref, sem):
    copies = []
    for place, (index, grad) in enumerate(grads):
        out_ref[place, 0] = grad[0]
        out_ref[place, 1] = grad[1]
        copies.append(pltpu.make_async_copy(out_ref.at[place], out_hbm.at[index], sem.at[place]))
        copies[-1].start()
    for copy in copies:
        copy.wait()


def early_kernel(scaling, low, gates_ref, own_ref, other_ref, out_hbm, token_ref, all_ref, out_ref, sem):
    token_ref[...] = jnp.zeros_like(token_ref)
    size = gates_ref.shape[-1]
    gate = lambda index: (gates_ref[index, 0], gates_ref[index, 1])
    collect(low, (own_ref, other_ref), all_ref)
    sums = lambda place: (all_ref[place, :size] * scaling, all_ref[place, size:] * scaling)
    grads = [(0, sums(1))]
    term = sums(0)
    for index in range(1, gates_ref.shape[0], 2):
        grads.append((index, multiply(term, gate(index))))
        term = multiply_adjoint(gate(index), grads[-1][1])
    write(grads, out_hbm, out_ref, sem)


def late_kernel(scaling, low, *refs):
    *refs, _, out_hbm, all_ref, out_ref, sem = refs
    size = all_ref.shape[-1]
    collect_direct(low, refs, all_ref)
    sums = lambda place: (all_ref[place, :size] * scaling, all_ref[place, size:] * scaling)
    write([(2 * place + 2, sums(place)) for place in range(all_ref.shape[0])], out_hbm, out_ref, sem)


def collect_direct(low, refs, all_ref):
    half, within = place_of(low)
    count, rows = len(refs) // 2, refs[0].shape[0] // all_ref.shape[0]
    for place, ref in enumerate(refs):
        chunk = lax.bitwise_xor(half, place // count) * count + lax.bitwise_xor(within, place % count)
        start = pl.multiple_of(chunk * rows, rows)
        for index in range(all_ref.shape[0]):
            all_ref[index, pl.ds(start, rows), :] = ref[pl.ds(index * rows, rows), :]


def hold_kernel(held_ref, _, out_ref):
    pass


def from_mask(value, mask, total):
    return lax.ppermute(value, AXES, [(device, device ^ mask) for device in range(total)])


def tree(terms):
    while len(terms) > 1:
        terms = [one + two for one, two in zip(terms[::2], terms[1::2])]
    return terms[0]


def reduce_near(own, other, pair, near, total):
    half = own + from_mask(other, pair, total)
    return tree([half[0]] + [from_mask(half[place], mask, total) for place, mask in enumerate(near) if place])


def reduce_far(mine, far, total):
    for mask in far:
        mine = mine + from_mask(mine, mask, total)
    return mine


def gather_near(mine, near, total):
    return jnp.stack([mine] + [from_mask(mine, mask, total) for mask in near[1:]])


def shards(state, adjoint, gates):
    size = gates.shape[-1]
    count = state.shape[-1]
    na, nb = lax.axis_size("qa"), lax.axis_size("qb")
    total = na * nb
    scaling = float(total * count // size) ** (-0.5)
    rest = count // size
    kept = rest // total
    inner, tail = nb // na, size // nb
    if gates.shape[0] != 8 or inner * kept != size or tail != 8:
        return stepwise(state, adjoint, gates)

    low = 1 << ((nb.bit_length() - 1) // 2)
    near = [a * nb + b for a in range(na) for b in range(0, low, 2)]
    far = [1 << bit for bit in range(low.bit_length() - 1, nb.bit_length() - 1)]
    shape = lambda *dims: jax.ShapeDtypeStruct(dims, jnp.float32)
    flat = (2, rest, size)
    chunks = lambda sums: [shape(len(near), sums * size // len(near), size)] * 2
    vmem = pl.BlockSpec(memory_space=pltpu.VMEM)
    hbm = pl.BlockSpec(memory_space=pltpu.HBM)
    buffer = lambda *dims: pltpu.VMEM(dims, jnp.float32)

    def call(kernel, name, out_shape, scratch=(), grant=48 * 2**20, **options):
        return pl.pallas_call(
            kernel,
            out_shape=out_shape,
            scratch_shapes=scratch,
            compiler_params=pltpu.CompilerParams(vmem_limit_bytes=grant),
            name=name,
            **options,
        )

    unread = pl.BlockSpec(memory_space=pl.ANY)

    def hold(array, operand):
        return call(
            hold_kernel,
            "hold",
            shape(*array.shape),
            in_specs=[unread, unread],
            out_specs=unread,
            input_output_aliases={0: 0},
        )(array, operand)

    fields = (state.reshape(flat), adjoint.reshape(flat), gates)
    out = call(
        first_kernel,
        "first",
        shape(total, 4 * kept, size),
        [
            buffer(*flat),
            buffer(*flat),
            buffer(*gates.shape),
            buffer(total, 4 * kept, size),
            pltpu.SemaphoreType.DMA((3,)),
            pltpu.SemaphoreType.DMA((rest // size,)),
        ],
        grant=60 * 2**20,
        in_specs=[hbm, hbm, hbm],
        out_specs=hbm,
    )(*fields)
    early = call(
        functools.partial(first_sums_kernel, low),
        "first_sums",
        chunks(2),
        [buffer(2, 2 * size, size)],
        in_specs=[vmem, vmem, vmem, unread],
    )(*fields, out)
    got = lax.all_to_all(out, AXES, split_axis=0, concat_axis=0, tiled=True)
    early = reduce_far(reduce_near(*early, 1, near, total), far[:-1], total)
    out = call(
        functools.partial(second_kernel, na),
        "second",
        shape(total, 4 * kept, size),
        [buffer(total, 4 * kept, size), pltpu.SemaphoreType.DMA((2,))],
        in_specs=[vmem, vmem, unread],
        out_specs=hbm,
    )(got, gates, early)
    early = reduce_far(early, far[-1:], total)
    out = hold(out, early)
    late = call(
        functools.partial(second_sums_kernel, na, low),
        "second_sums",
        chunks(3),
        [buffer(3, 2 * size, size)],
        in_specs=[vmem, vmem, unread],
    )(got, gates, out)
    got = lax.all_to_all(out, AXES, split_axis=0, concat_axis=0, tiled=True)
    early = gather_near(early, near, total)
    token = shape(8, size)
    grads, early_made = call(
        functools.partial(early_kernel, scaling, low),
        "early",
        (shape(*gates.shape), token),
        [buffer(2, 2 * size, size), buffer(5, 2, size, size), pltpu.SemaphoreType.DMA((5,))],
        in_specs=[vmem, vmem, vmem],
        out_specs=[hbm, vmem],
    )(gates, early, from_mask(early, 1, total))
    state_out, adjoint_out, fields_made = call(
        functools.partial(third_kernel, na, nb), "third", (shape(*flat), shape(*flat), token)
    )(got)
    late = reduce_far(reduce_near(*late, 1, near, total), far[:-1], total)
    late = hold(reduce_far(hold(late, early_made), far[-1:], total), fields_made)
    masks = near + [mask ^ 1 for mask in near]
    late = [late] + [from_mask(late, mask, total) for mask in masks[1:]]
    grads = call(
        functools.partial(late_kernel, scaling, low),
        "late",
        shape(*gates.shape),
        [buffer(3, 2 * size, size), buffer(3, 2, size, size), pltpu.SemaphoreType.DMA((3,))],
        in_specs=[vmem] * len(late) + [hbm],
        out_specs=hbm,
        input_output_aliases={len(late): 0},
    )(*late, grads)
    return state_out.reshape(state.shape), adjoint_out.reshape(adjoint.shape), grads


def solution(mesh):
    in_specs = (P(None, "qa", "qb", None), P(None, "qa", "qb", None), P())
    out_specs = (P(None, "qa", "qb", None), P(None, "qa", "qb", None), P())
    return jax.shard_map(shards, mesh=mesh, in_specs=in_specs, out_specs=out_specs, check_vma=False)
```

```python
import functools

import jax
import jax.numpy as jnp
from jax import lax
from jax.experimental import pallas as pl
from jax.experimental.pallas import tpu as pltpu
from jax.sharding import PartitionSpec as P

AXES = ("qa", "qb")
NN = (((1,), (0,)), ((), ()))
NT = (((1,), (1,)), ((), ()))
TN = (((0,), (0,)), ((), ()))


def contract(left, right, left_dim, right_dim):
    return lax.dot_general(
        left,
        right,
        (((left_dim,), (right_dim,)), ((), ())),
        precision=lax.Precision.HIGHEST,
        preferred_element_type=jnp.float32,
    )


def undo_high(field, gate):
    new_real = contract(gate[0], field[0], 0, 0) + contract(gate[1], field[1], 0, 0)
    new_imag = contract(gate[0], field[1], 0, 0) - contract(gate[1], field[0], 0, 0)
    return jnp.stack([new_real, new_imag])


def undo_low(field, gate):
    new_real = contract(field[0], gate[0], 1, 0) + contract(field[1], gate[1], 1, 0)
    new_imag = contract(field[1], gate[0], 1, 0) - contract(field[0], gate[1], 1, 0)
    return jnp.stack([new_real, new_imag])


def pair_high(adjoint_field, new_field):
    grad_real = contract(adjoint_field[0], new_field[0], 1, 1) + contract(
        adjoint_field[1], new_field[1], 1, 1
    )
    grad_imag = contract(adjoint_field[1], new_field[0], 1, 1) - contract(
        adjoint_field[0], new_field[1], 1, 1
    )
    return jnp.stack([grad_real, grad_imag])


def pair_low(adjoint_field, new_field):
    grad_real = contract(adjoint_field[0], new_field[0], 0, 0) + contract(
        adjoint_field[1], new_field[1], 0, 0
    )
    grad_imag = contract(adjoint_field[1], new_field[0], 0, 0) - contract(
        adjoint_field[0], new_field[1], 0, 0
    )
    return jnp.stack([grad_real, grad_imag])


def stepwise(state, adjoint, gates):
    gate_size = gates.shape[-1]
    local_count = state.shape[-1]
    scaling = float(lax.axis_size("qa") * lax.axis_size("qb") * local_count // gate_size) ** (-0.5)
    state_now = state.reshape(2, local_count)
    adjoint_now = adjoint.reshape(2, local_count)
    collected = []

    def record(term):
        return lax.psum(term, ("qa", "qb"))

    for section in range(gates.shape[0] // 2):
        high_gate = gates[2 * section]
        low_gate = gates[2 * section + 1]
        upright = (2, gate_size, local_count // gate_size)
        state_high = state_now.reshape(upright)
        adjoint_high = adjoint_now.reshape(upright)
        state_new = undo_high(state_high, high_gate)
        collected.append(record(scaling * pair_high(adjoint_high, state_new)))
        adjoint_new = undo_high(adjoint_high, high_gate)
        flat = (2, local_count // gate_size, gate_size)
        state_low = state_new.reshape(flat)
        adjoint_low = adjoint_new.reshape(flat)
        groups = lax.axis_size("qa") if section % 2 == 0 else lax.axis_size("qb")
        state_done = undo_low(state_low, low_gate)
        collected.append(record(scaling * pair_low(adjoint_low, state_done)))
        adjoint_done = undo_low(adjoint_low, low_gate)
        split = (2, groups, local_count // groups)
        outgoing = (state_done.reshape(split), adjoint_done.reshape(split))
        if section % 2 == 0:
            arrived = (
                lax.all_to_all(outgoing[0], "qa", split_axis=1, concat_axis=1, tiled=True),
                lax.all_to_all(outgoing[1], "qa", split_axis=1, concat_axis=1, tiled=True),
            )
        else:
            arrived = (
                lax.all_to_all(outgoing[0], "qb", split_axis=1, concat_axis=1, tiled=True),
                lax.all_to_all(outgoing[1], "qb", split_axis=1, concat_axis=1, tiled=True),
            )
        state_now = arrived[0].reshape(2, local_count)
        adjoint_now = arrived[1].reshape(2, local_count)
    gradients = jnp.stack(collected)
    return (state_now.reshape(state.shape), adjoint_now.reshape(adjoint.shape), gradients)


def split(x):
    high = x.astype(jnp.bfloat16)
    return high, (x - high.astype(jnp.float32)).astype(jnp.bfloat16)


def dot(left, right, dims):
    part = lambda i, j: lax.dot_general(left[i], right[j], dims, preferred_element_type=jnp.float32)
    return (part(0, 1) + part(1, 0)) + part(0, 0)


def each(operation, *arrays):
    return tuple(operation(*parts) for parts in zip(*arrays))


def wide(arrays):
    return jnp.concatenate(arrays, 1)


def tall(arrays):
    return jnp.concatenate(arrays, 0)


def multiply(left, right):
    size = left[0].shape[0]
    both = dot(split(tall(left)), split(wide(right)), NN)
    return (
        both[:size, :size] - both[size:, size:],
        both[:size, size:] + both[size:, :size],
    )


def multiply_adjoint(left, right):
    size = left[0].shape[0]
    both = dot(split(tall((left[0].T, left[1].T))), split(wide(right)), NN)
    return (
        both[:size, :size] + both[size:, size:],
        both[:size, size:] - both[size:, :size],
    )


def undoing(gate):
    real, imag = gate[0].T, gate[1].T
    return split(tall((wide((real, imag)), wide((-imag, real)))))


def paired(both):
    size = both.shape[0] // 2
    return tall((both[:size, :size] + both[size:, size:], both[size:, :size] - both[:size, size:]))


def exchange(parts, width):
    parts = list(parts)
    lanes = parts[0].shape[-1]
    lane = lax.broadcasted_iota(jnp.int32, parts[0].shape, 1)
    step = 1
    while step < len(parts):
        shift = step * width
        lower = (lane // shift) % 2 == 0
        for index in range(len(parts)):
            if index & step == 0:
                one, two = parts[index], parts[index + step]
                parts[index] = jnp.where(lower, one, pltpu.roll(two, shift, 1))
                parts[index + step] = jnp.where(lower, pltpu.roll(one, lanes - shift, 1), two)
        step *= 2
    return parts


def place_of(low):
    along = lax.axis_index("qb")
    within = lax.shift_right_logical(lax.bitwise_and(along, low - 1), 1)
    return lax.bitwise_and(along, 1), lax.axis_index("qa") * (low // 2) + within


def share_out(sums, low, refs, all_ref):
    for index, term in enumerate(sums):
        all_ref[index] = term
    half, within = place_of(low)
    count, rows = refs[0].shape[0], refs[0].shape[1] // len(sums)
    for other, ref in enumerate(refs):
        for mask in range(count):
            chunk = lax.bitwise_xor(half, other) * count + lax.bitwise_xor(within, mask)
            start = pl.multiple_of(chunk * rows, rows)
            for index in range(len(sums)):
                ref[mask, pl.ds(index * rows, rows), :] = all_ref[index, pl.ds(start, rows), :]


def collect(low, refs, all_ref):
    half, within = place_of(low)
    sums, count, rows = all_ref.shape[0], refs[0].shape[0], refs[0].shape[1] // all_ref.shape[0]
    for other, ref in enumerate(refs):
        for mask in range(count):
            chunk = lax.bitwise_xor(half, other) * count + lax.bitwise_xor(within, mask)
            start = pl.multiple_of(chunk * rows, rows)
            for index in range(sums):
                all_ref[index, pl.ds(start, rows), :] = ref[mask, pl.ds(index * rows, rows), :]


def times_gate(both, gate):
    size = both.shape[0] // 2
    term = paired(both)
    return tall(multiply((term[:size], term[size:]), gate))


def rows_low(ref, size):
    mid = ref.shape[1] // size
    return [[split(ref[part, pl.ds(j, size, stride=mid), :]) for part in range(2)] for j in range(mid)]


def rows_high(field):
    return each(
        lambda *a: tall(a), *[each(lambda *b: wide(b), *[row[part] for row in field]) for part in range(2)]
    )


def first_kernel(
    state_hbm, adjoint_hbm, gates_hbm, out_hbm, state_ref, adjoint_ref, gates_ref, out_ref, sem, out_sem
):
    pairs = ((gates_hbm, gates_ref), (state_hbm, state_ref), (adjoint_hbm, adjoint_ref))
    copies = [pltpu.make_async_copy(*pair, sem.at[place]) for place, pair in enumerate(pairs)]
    for copy in copies:
        copy.start()
    size = gates_ref.shape[-1]
    mid = state_ref.shape[1] // size
    total = out_ref.shape[0]
    kept = mid * size // total
    blocks = size // kept
    gate = lambda index: (gates_ref[index, 0], gates_ref[index, 1])

    for copy in copies:
        copy.wait()
    four = multiply(multiply(gate(1), gate(3)), multiply(gate(5), gate(7)))
    undo_low = undoing(four)
    undo_high = undoing(gate(0))
    by_high = [rows_high(rows_low(ref, size)) for ref in (state_ref, adjoint_ref)]
    done = [dot(undo_high, field, NN) for field in by_high]
    copies = []
    for j in range(mid):
        here = slice(j * size, (j + 1) * size)
        rows = tall([wide((field[:size, here], field[size:, here])) for field in done])
        sent = dot(undo_low, split(rows), NT)
        for block in range(blocks):
            for f in range(2):
                for part in range(2):
                    start = part * size + block * kept
                    out_ref[j * blocks + block, pl.ds((f * 2 + part) * kept, kept), :] = sent[
                        start : start + kept, f * size : (f + 1) * size
                    ]
        mine = pl.ds(j * blocks, blocks)
        copies.append(pltpu.make_async_copy(out_ref.at[mine], out_hbm.at[mine], out_sem.at[j]))
        copies[-1].start()
    for copy in copies:
        copy.wait()


def first_sums_kernel(low, state_ref, adjoint_ref, gates_ref, _, own_ref, other_ref, all_ref):
    size = gates_ref.shape[-1]
    fields = [rows_low(ref, size) for ref in (state_ref, adjoint_ref)]
    by_low = [each(lambda *a: tall(a), *[each(lambda *b: wide(b), *row) for row in field]) for field in fields]
    by_high = [rows_high(field) for field in fields]
    sums = [
        paired(dot(by_low[1], by_low[0], TN)),
        times_gate(dot(by_high[1], by_high[0], NT), (gates_ref[0, 0], gates_ref[0, 1])),
    ]
    share_out(sums, low, (own_ref, other_ref), all_ref)


def before_gates(na, got_ref, gates_ref):
    size = gates_ref.shape[-1]
    total = got_ref.shape[0]
    nb = total // na
    inner = nb // na
    tail = size // nb
    kept = size // inner
    gate = lambda index: (gates_ref[index, 0], gates_ref[index, 1])

    fields = []
    for f in range(2):
        parts = []
        for part in range(2):
            start = (f * 2 + part) * kept
            rows = [got_ref[pl.ds(a * nb, nb), pl.ds(start, kept), :].reshape(nb * kept, size) for a in range(na)]
            parts.append(tall(exchange(rows, size // na)))
        fields.append(split(wide(parts)))
    before = [fields]
    undo = undoing(gate(2))
    after = []
    for f in range(2):
        done = dot(undo, fields[f], NT)
        after.append(done)
    lists = []
    for h in range(inner):
        pieces = []
        for f in range(2):
            for block in range(na * na):
                cut = after[f][:, block * size : (block + 1) * size]
                pieces.append(cut.reshape(2 * na, inner, tail, size)[:, h].reshape(2 * na * tail, size))
        lists.append(tall(pieces))
    turned = exchange(lists, kept)
    turned = [item.reshape(2, na, na, 2, na, tail, size) for item in turned]

    fields = []
    for f in range(2):
        columns = []
        for top in range(na):
            for a in range(na):
                rows = [
                    turned[b][f, top, B, part, a]
                    for part in range(2)
                    for B in range(na)
                    for b in range(inner)
                ]
                columns.append(tall(rows))
        fields.append(split(wide(columns)))
    before.append(fields)
    undo = undoing(gate(4))
    after = [dot(undo, field, NN) for field in fields]

    span = inner * tail
    fields = []
    for f in range(2):
        columns = []
        for a in range(na):
            for B in range(na):
                rows = []
                for part in range(2):
                    for top in range(na):
                        row = (part * na + B) * span
                        column = (top * na + a) * size
                        rows.append(after[f][row : row + span, column : column + size])
                columns.append(tall(rows))
        fields.append(split(wide(columns)))
    return before + [fields]


def second_kernel(na, got_ref, gates_ref, _, out_hbm, out_ref, sem):
    size = gates_ref.shape[-1]
    total = got_ref.shape[0]
    inner = total // na // na
    tail = size // (total // na)
    kept = size // inner
    fields = before_gates(na, got_ref, gates_ref)[-1]
    undo = undoing((gates_ref[6, 0], gates_ref[6, 1]))
    copies = []
    for f in range(2):
        done = dot(undo, fields[f], NN)
        for part in range(2):
            for a in range(na):
                for B in range(na):
                    column = (a * na + B) * size
                    for top in range(na):
                        for b in range(inner):
                            row = ((part * na + top) * inner + b) * tail
                            out_ref[
                                (B * na + top) * inner + b,
                                pl.ds(((f * 2 + part) * na + a) * tail, tail),
                                :,
                            ] = done[row : row + tail, column : column + size]
        mine = (slice(None), pl.ds(f * 2 * kept, 2 * kept))
        copies.append(pltpu.make_async_copy(out_ref.at[mine], out_hbm.at[mine], sem.at[f]))
        copies[-1].start()
    for copy in copies:
        copy.wait()


def second_sums_kernel(na, low, got_ref, gates_ref, _, own_ref, other_ref, all_ref):
    sums = []
    for place, fields in enumerate(before_gates(na, got_ref, gates_ref)):
        index = 2 * place + 2
        both = dot(fields[1], fields[0], NT if place else TN)
        sums.append(times_gate(both, (gates_ref[index, 0], gates_ref[index, 1])))
    share_out(sums, low, (own_ref, other_ref), all_ref)


def third_kernel(na, nb, got_ref, state_ref, adjoint_ref, token_ref):
    token_ref[...] = jnp.zeros_like(token_ref)
    total, _, size = got_ref.shape
    rest = state_ref.shape[1]
    mid = rest // size
    inner = nb // na
    tail = size // nb
    kept = size // inner
    blocks = total // mid
    for j in range(mid):
        lists = [
            got_ref[j * blocks + block, pl.ds(0, 4 * kept), :] for block in range(blocks)
        ]
        turned = exchange(lists, kept)
        for h in range(inner):
            for f, ref in enumerate((state_ref, adjoint_ref)):
                for part in range(2):
                    for a in range(na):
                        row = ((f * 2 + part) * na + a) * tail
                        ref[part, pl.ds(((a * inner + h) * tail) * mid + j, tail, stride=mid), :] = turned[h][
                            row : row + tail
                        ]


def write(grads, out_hbm, out_ref, sem):
    copies = []
    for place, (index, grad) in enumerate(grads):
        out_ref[place, 0] = grad[0]
        out_ref[place, 1] = grad[1]
        copies.append(pltpu.make_async_copy(out_ref.at[place], out_hbm.at[index], sem.at[place]))
        copies[-1].start()
    for copy in copies:
        copy.wait()


def early_kernel(scaling, low, gates_ref, own_ref, other_ref, out_hbm, token_ref, all_ref, out_ref, sem):
    token_ref[...] = jnp.zeros_like(token_ref)
    size = gates_ref.shape[-1]
    gate = lambda index: (gates_ref[index, 0], gates_ref[index, 1])
    collect(low, (own_ref, other_ref), all_ref)
    sums = lambda place: (all_ref[place, :size] * scaling, all_ref[place, size:] * scaling)
    grads = [(0, sums(1))]
    term = sums(0)
    for index in range(1, gates_ref.shape[0], 2):
        grads.append((index, multiply(term, gate(index))))
        term = multiply_adjoint(gate(index), grads[-1][1])
    write(grads, out_hbm, out_ref, sem)


def late_kernel(scaling, low, own_ref, other_ref, _, __, out_hbm, all_ref, out_ref, sem):
    size = all_ref.shape[-1]
    collect(low, (own_ref, other_ref), all_ref)
    sums = lambda place: (all_ref[place, :size] * scaling, all_ref[place, size:] * scaling)
    write([(2 * place + 2, sums(place)) for place in range(all_ref.shape[0])], out_hbm, out_ref, sem)


def hold_kernel(held_ref, _, out_ref):
    pass


def from_mask(value, mask, total):
    return lax.ppermute(value, AXES, [(device, device ^ mask) for device in range(total)])


def tree(terms):
    while len(terms) > 1:
        terms = [one + two for one, two in zip(terms[::2], terms[1::2])]
    return terms[0]


def reduce_near(own, other, pair, near, total):
    half = own + from_mask(other, pair, total)
    return tree([half[0]] + [from_mask(half[place], mask, total) for place, mask in enumerate(near) if place])


def reduce_far(mine, far, total):
    for mask in far:
        mine = mine + from_mask(mine, mask, total)
    return mine


def gather_near(mine, near, total):
    return jnp.stack([mine] + [from_mask(mine, mask, total) for mask in near[1:]])


def shards(state, adjoint, gates):
    size = gates.shape[-1]
    count = state.shape[-1]
    na, nb = lax.axis_size("qa"), lax.axis_size("qb")
    total = na * nb
    scaling = float(total * count // size) ** (-0.5)
    rest = count // size
    kept = rest // total
    inner, tail = nb // na, size // nb
    if gates.shape[0] != 8 or inner * kept != size or tail != 8:
        return stepwise(state, adjoint, gates)

    low = 1 << ((nb.bit_length() - 1) // 2)
    near = [a * nb + b for a in range(na) for b in range(0, low, 2)]
    far = [1 << bit for bit in range(low.bit_length() - 1, nb.bit_length() - 1)]
    shape = lambda *dims: jax.ShapeDtypeStruct(dims, jnp.float32)
    flat = (2, rest, size)
    chunks = lambda sums: [shape(len(near), sums * size // len(near), size)] * 2
    vmem = pl.BlockSpec(memory_space=pltpu.VMEM)
    hbm = pl.BlockSpec(memory_space=pltpu.HBM)
    buffer = lambda *dims: pltpu.VMEM(dims, jnp.float32)

    def call(kernel, name, out_shape, scratch=(), grant=48 * 2**20, **options):
        return pl.pallas_call(
            kernel,
            out_shape=out_shape,
            scratch_shapes=scratch,
            compiler_params=pltpu.CompilerParams(vmem_limit_bytes=grant),
            name=name,
            **options,
        )

    unread = pl.BlockSpec(memory_space=pl.ANY)

    def hold(array, operand):
        return call(
            hold_kernel,
            "hold",
            shape(*array.shape),
            in_specs=[unread, unread],
            out_specs=unread,
            input_output_aliases={0: 0},
        )(array, operand)

    fields = (state.reshape(flat), adjoint.reshape(flat), gates)
    out = call(
        first_kernel,
        "first",
        shape(total, 4 * kept, size),
        [
            buffer(*flat),
            buffer(*flat),
            buffer(*gates.shape),
            buffer(total, 4 * kept, size),
            pltpu.SemaphoreType.DMA((3,)),
            pltpu.SemaphoreType.DMA((rest // size,)),
        ],
        grant=60 * 2**20,
        in_specs=[hbm, hbm, hbm],
        out_specs=hbm,
    )(*fields)
    early = call(
        functools.partial(first_sums_kernel, low),
        "first_sums",
        chunks(2),
        [buffer(2, 2 * size, size)],
        in_specs=[vmem, vmem, vmem, unread],
    )(*fields, out)
    got = lax.all_to_all(out, AXES, split_axis=0, concat_axis=0, tiled=True)
    early = reduce_far(reduce_near(*early, 1, near, total), far[:-1], total)
    out = call(
        functools.partial(second_kernel, na),
        "second",
        shape(total, 4 * kept, size),
        [buffer(total, 4 * kept, size), pltpu.SemaphoreType.DMA((2,))],
        in_specs=[vmem, vmem, unread],
        out_specs=hbm,
    )(got, gates, early)
    early = reduce_far(early, far[-1:], total)
    out = hold(out, early)
    late = call(
        functools.partial(second_sums_kernel, na, low),
        "second_sums",
        chunks(3),
        [buffer(3, 2 * size, size)],
        in_specs=[vmem, vmem, unread],
    )(got, gates, out)
    got = lax.all_to_all(out, AXES, split_axis=0, concat_axis=0, tiled=True)
    early = gather_near(early, near, total)
    token = shape(8, size)
    grads, early_made = call(
        functools.partial(early_kernel, scaling, low),
        "early",
        (shape(*gates.shape), token),
        [buffer(2, 2 * size, size), buffer(5, 2, size, size), pltpu.SemaphoreType.DMA((5,))],
        in_specs=[vmem, vmem, vmem],
        out_specs=[hbm, vmem],
    )(gates, early, from_mask(early, 1, total))
    state_out, adjoint_out, fields_made = call(
        functools.partial(third_kernel, na, nb), "third", (shape(*flat), shape(*flat), token)
    )(got)
    late = reduce_far(reduce_near(*late, 1, near, total), far[:-1], total)
    late = reduce_far(hold(late, early_made), far[-1:], total)
    late = gather_near(late, near, total)
    grads = call(
        functools.partial(late_kernel, scaling, low),
        "late",
        shape(*gates.shape),
        [buffer(3, 2 * size, size), buffer(3, 2, size, size), pltpu.SemaphoreType.DMA((3,))],
        in_specs=[vmem, vmem, hbm, unread],
        out_specs=hbm,
        input_output_aliases={2: 0},
    )(late, from_mask(late, 1, total), grads, fields_made)
    return state_out.reshape(state.shape), adjoint_out.reshape(adjoint.shape), grads


def solution(mesh):
    in_specs = (P(None, "qa", "qb", None), P(None, "qa", "qb", None), P())
    out_specs = (P(None, "qa", "qb", None), P(None, "qa", "qb", None), P())
    return jax.shard_map(shards, mesh=mesh, in_specs=in_specs, out_specs=out_specs, check_vma=False)
```

```python
import functools

import jax
import jax.numpy as jnp
from jax import lax
from jax.experimental import pallas as pl
from jax.experimental.pallas import tpu as pltpu
from jax.sharding import PartitionSpec as P

AXES = ("qa", "qb")
NN = (((1,), (0,)), ((), ()))
NT = (((1,), (1,)), ((), ()))
TN = (((0,), (0,)), ((), ()))


def contract(left, right, left_dim, right_dim):
    return lax.dot_general(
        left,
        right,
        (((left_dim,), (right_dim,)), ((), ())),
        precision=lax.Precision.HIGHEST,
        preferred_element_type=jnp.float32,
    )


def undo_high(field, gate):
    new_real = contract(gate[0], field[0], 0, 0) + contract(gate[1], field[1], 0, 0)
    new_imag = contract(gate[0], field[1], 0, 0) - contract(gate[1], field[0], 0, 0)
    return jnp.stack([new_real, new_imag])


def undo_low(field, gate):
    new_real = contract(field[0], gate[0], 1, 0) + contract(field[1], gate[1], 1, 0)
    new_imag = contract(field[1], gate[0], 1, 0) - contract(field[0], gate[1], 1, 0)
    return jnp.stack([new_real, new_imag])


def pair_high(adjoint_field, new_field):
    grad_real = contract(adjoint_field[0], new_field[0], 1, 1) + contract(
        adjoint_field[1], new_field[1], 1, 1
    )
    grad_imag = contract(adjoint_field[1], new_field[0], 1, 1) - contract(
        adjoint_field[0], new_field[1], 1, 1
    )
    return jnp.stack([grad_real, grad_imag])


def pair_low(adjoint_field, new_field):
    grad_real = contract(adjoint_field[0], new_field[0], 0, 0) + contract(
        adjoint_field[1], new_field[1], 0, 0
    )
    grad_imag = contract(adjoint_field[1], new_field[0], 0, 0) - contract(
        adjoint_field[0], new_field[1], 0, 0
    )
    return jnp.stack([grad_real, grad_imag])


def stepwise(state, adjoint, gates):
    gate_size = gates.shape[-1]
    local_count = state.shape[-1]
    scaling = float(lax.axis_size("qa") * lax.axis_size("qb") * local_count // gate_size) ** (-0.5)
    state_now = state.reshape(2, local_count)
    adjoint_now = adjoint.reshape(2, local_count)
    collected = []

    def record(term):
        return lax.psum(term, ("qa", "qb"))

    for section in range(gates.shape[0] // 2):
        high_gate = gates[2 * section]
        low_gate = gates[2 * section + 1]
        upright = (2, gate_size, local_count // gate_size)
        state_high = state_now.reshape(upright)
        adjoint_high = adjoint_now.reshape(upright)
        state_new = undo_high(state_high, high_gate)
        collected.append(record(scaling * pair_high(adjoint_high, state_new)))
        adjoint_new = undo_high(adjoint_high, high_gate)
        flat = (2, local_count // gate_size, gate_size)
        state_low = state_new.reshape(flat)
        adjoint_low = adjoint_new.reshape(flat)
        groups = lax.axis_size("qa") if section % 2 == 0 else lax.axis_size("qb")
        state_done = undo_low(state_low, low_gate)
        collected.append(record(scaling * pair_low(adjoint_low, state_done)))
        adjoint_done = undo_low(adjoint_low, low_gate)
        split = (2, groups, local_count // groups)
        outgoing = (state_done.reshape(split), adjoint_done.reshape(split))
        if section % 2 == 0:
            arrived = (
                lax.all_to_all(outgoing[0], "qa", split_axis=1, concat_axis=1, tiled=True),
                lax.all_to_all(outgoing[1], "qa", split_axis=1, concat_axis=1, tiled=True),
            )
        else:
            arrived = (
                lax.all_to_all(outgoing[0], "qb", split_axis=1, concat_axis=1, tiled=True),
                lax.all_to_all(outgoing[1], "qb", split_axis=1, concat_axis=1, tiled=True),
            )
        state_now = arrived[0].reshape(2, local_count)
        adjoint_now = arrived[1].reshape(2, local_count)
    gradients = jnp.stack(collected)
    return (state_now.reshape(state.shape), adjoint_now.reshape(adjoint.shape), gradients)


def split(x):
    high = x.astype(jnp.bfloat16)
    return high, (x - high.astype(jnp.float32)).astype(jnp.bfloat16)


def dot(left, right, dims):
    part = lambda i, j: lax.dot_general(left[i], right[j], dims, preferred_element_type=jnp.float32)
    return (part(0, 1) + part(1, 0)) + part(0, 0)


def each(operation, *arrays):
    return tuple(operation(*parts) for parts in zip(*arrays))


def wide(arrays):
    return jnp.concatenate(arrays, 1)


def tall(arrays):
    return jnp.concatenate(arrays, 0)


def multiply(left, right):
    size = left[0].shape[0]
    both = dot(split(tall(left)), split(wide(right)), NN)
    return (
        both[:size, :size] - both[size:, size:],
        both[:size, size:] + both[size:, :size],
    )


def multiply_adjoint(left, right):
    size = left[0].shape[0]
    both = dot(split(tall((left[0].T, left[1].T))), split(wide(right)), NN)
    return (
        both[:size, :size] + both[size:, size:],
        both[:size, size:] - both[size:, :size],
    )


def undoing(gate):
    real, imag = gate[0].T, gate[1].T
    return split(tall((wide((real, imag)), wide((-imag, real)))))


def paired(both):
    size = both.shape[0] // 2
    return tall((both[:size, :size] + both[size:, size:], both[size:, :size] - both[:size, size:]))


def exchange(parts, width):
    parts = list(parts)
    lanes = parts[0].shape[-1]
    lane = lax.broadcasted_iota(jnp.int32, parts[0].shape, 1)
    step = 1
    while step < len(parts):
        shift = step * width
        lower = (lane // shift) % 2 == 0
        for index in range(len(parts)):
            if index & step == 0:
                one, two = parts[index], parts[index + step]
                parts[index] = jnp.where(lower, one, pltpu.roll(two, shift, 1))
                parts[index + step] = jnp.where(lower, pltpu.roll(one, lanes - shift, 1), two)
        step *= 2
    return parts


def place_of(low):
    along = lax.axis_index("qb")
    within = lax.shift_right_logical(lax.bitwise_and(along, low - 1), 1)
    return lax.bitwise_and(along, 1), lax.axis_index("qa") * (low // 2) + within


def share_out(sums, low, refs, all_ref):
    for index, term in enumerate(sums):
        all_ref[index] = term
    half, within = place_of(low)
    count, rows = refs[0].shape[0], refs[0].shape[1] // len(sums)
    for other, ref in enumerate(refs):
        for mask in range(count):
            chunk = lax.bitwise_xor(half, other) * count + lax.bitwise_xor(within, mask)
            start = pl.multiple_of(chunk * rows, rows)
            for index in range(len(sums)):
                ref[mask, pl.ds(index * rows, rows), :] = all_ref[index, pl.ds(start, rows), :]


def collect(low, refs, all_ref):
    half, within = place_of(low)
    sums, count, rows = all_ref.shape[0], refs[0].shape[0], refs[0].shape[1] // all_ref.shape[0]
    for other, ref in enumerate(refs):
        for mask in range(count):
            chunk = lax.bitwise_xor(half, other) * count + lax.bitwise_xor(within, mask)
            start = pl.multiple_of(chunk * rows, rows)
            for index in range(sums):
                all_ref[index, pl.ds(start, rows), :] = ref[mask, pl.ds(index * rows, rows), :]


def times_gate(both, gate):
    size = both.shape[0] // 2
    term = paired(both)
    return tall(multiply((term[:size], term[size:]), gate))


def rows_low(ref, size):
    mid = ref.shape[1] // size
    return [[split(ref[part, pl.ds(j, size, stride=mid), :]) for part in range(2)] for j in range(mid)]


def rows_high(field):
    return each(
        lambda *a: tall(a), *[each(lambda *b: wide(b), *[row[part] for row in field]) for part in range(2)]
    )


def first_kernel(
    state_hbm, adjoint_hbm, gates_hbm, out_hbm, state_ref, adjoint_ref, gates_ref, out_ref, sem, out_sem
):
    pairs = ((gates_hbm, gates_ref), (state_hbm, state_ref), (adjoint_hbm, adjoint_ref))
    copies = [pltpu.make_async_copy(*pair, sem.at[place]) for place, pair in enumerate(pairs)]
    for copy in copies:
        copy.start()
    size = gates_ref.shape[-1]
    mid = state_ref.shape[1] // size
    total = out_ref.shape[0]
    kept = mid * size // total
    blocks = size // kept
    gate = lambda index: (gates_ref[index, 0], gates_ref[index, 1])

    for copy in copies:
        copy.wait()
    four = multiply(multiply(gate(1), gate(3)), multiply(gate(5), gate(7)))
    undo_low = undoing(four)
    undo_high = undoing(gate(0))
    by_high = [rows_high(rows_low(ref, size)) for ref in (state_ref, adjoint_ref)]
    done = [dot(undo_high, field, NN) for field in by_high]
    copies = []
    for j in range(mid):
        here = slice(j * size, (j + 1) * size)
        rows = tall([wide((field[:size, here], field[size:, here])) for field in done])
        sent = dot(undo_low, split(rows), NT)
        for block in range(blocks):
            for f in range(2):
                for part in range(2):
                    start = part * size + block * kept
                    out_ref[j * blocks + block, pl.ds((f * 2 + part) * kept, kept), :] = sent[
                        start : start + kept, f * size : (f + 1) * size
                    ]
        mine = pl.ds(j * blocks, blocks)
        copies.append(pltpu.make_async_copy(out_ref.at[mine], out_hbm.at[mine], out_sem.at[j]))
        copies[-1].start()
    for copy in copies:
        copy.wait()


def first_sums_kernel(low, state_ref, adjoint_ref, gates_ref, _, own_ref, other_ref, undo_ref, all_ref):
    for place, index in enumerate((2, 4, 6)):
        undo_ref[2 * place], undo_ref[2 * place + 1] = undoing((gates_ref[index, 0], gates_ref[index, 1]))
    size = gates_ref.shape[-1]
    fields = [rows_low(ref, size) for ref in (state_ref, adjoint_ref)]
    by_low = [each(lambda *a: tall(a), *[each(lambda *b: wide(b), *row) for row in field]) for field in fields]
    by_high = [rows_high(field) for field in fields]
    sums = [
        paired(dot(by_low[1], by_low[0], TN)),
        times_gate(dot(by_high[1], by_high[0], NT), (gates_ref[0, 0], gates_ref[0, 1])),
    ]
    share_out(sums, low, (own_ref, other_ref), all_ref)


def before_gates(na, got_ref, undo_ref):
    size = got_ref.shape[-1]
    total = got_ref.shape[0]
    nb = total // na
    inner = nb // na
    tail = size // nb
    kept = size // inner

    fields = []
    for f in range(2):
        parts = []
        for part in range(2):
            start = (f * 2 + part) * kept
            rows = [got_ref[pl.ds(a * nb, nb), pl.ds(start, kept), :].reshape(nb * kept, size) for a in range(na)]
            parts.append(tall(exchange(rows, size // na)))
        fields.append(split(wide(parts)))
    before = [fields]
    undo = undo_ref[0], undo_ref[1]
    after = []
    for f in range(2):
        done = dot(undo, fields[f], NT)
        after.append(done)
    lists = []
    for h in range(inner):
        pieces = []
        for f in range(2):
            for block in range(na * na):
                cut = after[f][:, block * size : (block + 1) * size]
                pieces.append(cut.reshape(2 * na, inner, tail, size)[:, h].reshape(2 * na * tail, size))
        lists.append(tall(pieces))
    turned = exchange(lists, kept)
    turned = [item.reshape(2, na, na, 2, na, tail, size) for item in turned]

    fields = []
    for f in range(2):
        columns = []
        for top in range(na):
            for a in range(na):
                rows = [
                    turned[b][f, top, B, part, a]
                    for part in range(2)
                    for B in range(na)
                    for b in range(inner)
                ]
                columns.append(tall(rows))
        fields.append(split(wide(columns)))
    before.append(fields)
    undo = undo_ref[2], undo_ref[3]
    after = [dot(undo, field, NN) for field in fields]

    span = inner * tail
    fields = []
    for f in range(2):
        columns = []
        for a in range(na):
            for B in range(na):
                rows = []
                for part in range(2):
                    for top in range(na):
                        row = (part * na + B) * span
                        column = (top * na + a) * size
                        rows.append(after[f][row : row + span, column : column + size])
                columns.append(tall(rows))
        fields.append(split(wide(columns)))
    return before + [fields]


def second_kernel(na, got_ref, undo_ref, _, out_hbm, out_ref, sem):
    size = got_ref.shape[-1]
    total = got_ref.shape[0]
    inner = total // na // na
    tail = size // (total // na)
    kept = size // inner
    fields = before_gates(na, got_ref, undo_ref)[-1]
    undo = undo_ref[4], undo_ref[5]
    copies = []
    for f in range(2):
        done = dot(undo, fields[f], NN)
        for part in range(2):
            for a in range(na):
                for B in range(na):
                    column = (a * na + B) * size
                    for top in range(na):
                        for b in range(inner):
                            row = ((part * na + top) * inner + b) * tail
                            out_ref[
                                (B * na + top) * inner + b,
                                pl.ds(((f * 2 + part) * na + a) * tail, tail),
                                :,
                            ] = done[row : row + tail, column : column + size]
        mine = (slice(None), pl.ds(f * 2 * kept, 2 * kept))
        copies.append(pltpu.make_async_copy(out_ref.at[mine], out_hbm.at[mine], sem.at[f]))
        copies[-1].start()
    for copy in copies:
        copy.wait()


def second_sums_kernel(na, low, got_ref, undo_ref, gates_ref, _, own_ref, other_ref, all_ref):
    sums = []
    for place, fields in enumerate(before_gates(na, got_ref, undo_ref)):
        index = 2 * place + 2
        both = dot(fields[1], fields[0], NT if place else TN)
        sums.append(times_gate(both, (gates_ref[index, 0], gates_ref[index, 1])))
    share_out(sums, low, (own_ref, other_ref), all_ref)


def third_kernel(na, nb, got_ref, state_hbm, adjoint_hbm, token_ref, out_ref, sem):
    token_ref[...] = jnp.zeros_like(token_ref)
    total, _, size = got_ref.shape
    mid = out_ref.shape[1] // size
    inner = nb // na
    tail = size // nb
    kept = size // inner
    blocks = total // mid
    copies = []
    for f, hbm in enumerate((state_hbm, adjoint_hbm)):
        for part in range(2):
            piece = f * 2 + part
            for j in range(mid):
                lists = [
                    got_ref[j * blocks + block, pl.ds(piece * na * tail, na * tail), :]
                    for block in range(blocks)
                ]
                turned = exchange(lists, kept)
                for h in range(inner):
                    for a in range(na):
                        place = pl.ds(((a * inner + h) * tail) * mid + j, tail, stride=mid)
                        out_ref[piece, place, :] = turned[h][a * tail : (a + 1) * tail]
            copies.append(pltpu.make_async_copy(out_ref.at[piece], hbm.at[part], sem.at[piece]))
            copies[-1].start()
    for copy in copies:
        copy.wait()


def write(grads, out_hbm, out_ref, sem):
    copies = []
    for place, (index, grad) in enumerate(grads):
        out_ref[place, 0] = grad[0]
        out_ref[place, 1] = grad[1]
        copies.append(pltpu.make_async_copy(out_ref.at[place], out_hbm.at[index], sem.at[place]))
        copies[-1].start()
    for copy in copies:
        copy.wait()


def early_kernel(scaling, low, gates_ref, own_ref, other_ref, out_hbm, token_ref, all_ref, out_ref, sem):
    token_ref[...] = jnp.zeros_like(token_ref)
    size = gates_ref.shape[-1]
    gate = lambda index: (gates_ref[index, 0], gates_ref[index, 1])
    collect(low, (own_ref, other_ref), all_ref)
    sums = lambda place: (all_ref[place, :size] * scaling, all_ref[place, size:] * scaling)
    grads = [(0, sums(1))]
    term = sums(0)
    for index in range(1, gates_ref.shape[0], 2):
        grads.append((index, multiply(term, gate(index))))
        term = multiply_adjoint(gate(index), grads[-1][1])
    write(grads, out_hbm, out_ref, sem)


def late_kernel(scaling, low, own_ref, other_ref, _, __, out_hbm, all_ref, out_ref, sem):
    size = all_ref.shape[-1]
    collect(low, (own_ref, other_ref), all_ref)
    sums = lambda place: (all_ref[place, :size] * scaling, all_ref[place, size:] * scaling)
    write([(2 * place + 2, sums(place)) for place in range(all_ref.shape[0])], out_hbm, out_ref, sem)


def hold_kernel(held_ref, _, out_ref):
    pass


def from_mask(value, mask, total):
    return lax.ppermute(value, AXES, [(device, device ^ mask) for device in range(total)])


def tree(terms):
    while len(terms) > 1:
        terms = [one + two for one, two in zip(terms[::2], terms[1::2])]
    return terms[0]


def reduce_near(own, other, pair, near, total):
    half = own + from_mask(other, pair, total)
    return tree([half[0]] + [from_mask(half[place], mask, total) for place, mask in enumerate(near) if place])


def reduce_far(mine, far, total):
    for mask in far:
        mine = mine + from_mask(mine, mask, total)
    return mine


def gather_near(mine, near, total):
    return jnp.stack([mine] + [from_mask(mine, mask, total) for mask in near[1:]])


def shards(state, adjoint, gates):
    size = gates.shape[-1]
    count = state.shape[-1]
    na, nb = lax.axis_size("qa"), lax.axis_size("qb")
    total = na * nb
    scaling = float(total * count // size) ** (-0.5)
    rest = count // size
    kept = rest // total
    inner, tail = nb // na, size // nb
    if gates.shape[0] != 8 or inner * kept != size or tail != 8:
        return stepwise(state, adjoint, gates)

    low = 1 << ((nb.bit_length() - 1) // 2)
    near = [a * nb + b for a in range(na) for b in range(0, low, 2)]
    far = [1 << bit for bit in range(low.bit_length() - 1, nb.bit_length() - 1)]
    shape = lambda *dims: jax.ShapeDtypeStruct(dims, jnp.float32)
    flat = (2, rest, size)
    chunks = lambda sums: [shape(len(near), sums * size // len(near), size)] * 2
    vmem = pl.BlockSpec(memory_space=pltpu.VMEM)
    hbm = pl.BlockSpec(memory_space=pltpu.HBM)
    buffer = lambda *dims: pltpu.VMEM(dims, jnp.float32)

    def call(kernel, name, out_shape, scratch=(), grant=48 * 2**20, **options):
        return pl.pallas_call(
            kernel,
            out_shape=out_shape,
            scratch_shapes=scratch,
            compiler_params=pltpu.CompilerParams(vmem_limit_bytes=grant),
            name=name,
            **options,
        )

    unread = pl.BlockSpec(memory_space=pl.ANY)

    def hold(array, operand):
        return call(
            hold_kernel,
            "hold",
            shape(*array.shape),
            in_specs=[unread, unread],
            out_specs=unread,
            input_output_aliases={0: 0},
        )(array, operand)

    fields = (state.reshape(flat), adjoint.reshape(flat), gates)
    out = call(
        first_kernel,
        "first",
        shape(total, 4 * kept, size),
        [
            buffer(*flat),
            buffer(*flat),
            buffer(*gates.shape),
            buffer(total, 4 * kept, size),
            pltpu.SemaphoreType.DMA((3,)),
            pltpu.SemaphoreType.DMA((rest // size,)),
        ],
        grant=60 * 2**20,
        in_specs=[hbm, hbm, hbm],
        out_specs=hbm,
    )(*fields)
    *early, undos = call(
        functools.partial(first_sums_kernel, low),
        "first_sums",
        chunks(2) + [jax.ShapeDtypeStruct((6, 2 * size, 2 * size), jnp.bfloat16)],
        [buffer(2, 2 * size, size)],
        in_specs=[vmem, vmem, vmem, unread],
    )(*fields, out)
    got = lax.all_to_all(out, AXES, split_axis=0, concat_axis=0, tiled=True)
    early = reduce_far(reduce_near(*early, 1, near, total), far[:-1], total)
    out = call(
        functools.partial(second_kernel, na),
        "second",
        shape(total, 4 * kept, size),
        [buffer(total, 4 * kept, size), pltpu.SemaphoreType.DMA((2,))],
        in_specs=[vmem, vmem, unread],
        out_specs=hbm,
    )(got, undos, early)
    early = reduce_far(early, far[-1:], total)
    out = hold(out, early)
    late = call(
        functools.partial(second_sums_kernel, na, low),
        "second_sums",
        chunks(3),
        [buffer(3, 2 * size, size)],
        in_specs=[vmem, vmem, vmem, unread],
    )(got, undos, gates, out)
    got = lax.all_to_all(out, AXES, split_axis=0, concat_axis=0, tiled=True)
    early = gather_near(early, near, total)
    token = shape(8, size)
    grads, early_made = call(
        functools.partial(early_kernel, scaling, low),
        "early",
        (shape(*gates.shape), token),
        [buffer(2, 2 * size, size), buffer(5, 2, size, size), pltpu.SemaphoreType.DMA((5,))],
        in_specs=[vmem, vmem, vmem],
        out_specs=[hbm, vmem],
    )(gates, early, from_mask(early, 1, total))
    state_out, adjoint_out, fields_made = call(
        functools.partial(third_kernel, na, nb),
        "third",
        (shape(*flat), shape(*flat), token),
        [buffer(4, rest, size), pltpu.SemaphoreType.DMA((4,))],
        out_specs=[hbm, hbm, vmem],
    )(got)
    late = reduce_far(reduce_near(*late, 1, near, total), far[:-1], total)
    late = reduce_far(hold(late, early_made), far[-1:], total)
    late = gather_near(late, near, total)
    grads = call(
        functools.partial(late_kernel, scaling, low),
        "late",
        shape(*gates.shape),
        [buffer(3, 2 * size, size), buffer(3, 2, size, size), pltpu.SemaphoreType.DMA((3,))],
        in_specs=[vmem, vmem, hbm, unread],
        out_specs=hbm,
        input_output_aliases={2: 0},
    )(late, from_mask(late, 1, total), grads, fields_made)
    return state_out.reshape(state.shape), adjoint_out.reshape(adjoint.shape), grads


def solution(mesh):
    in_specs = (P(None, "qa", "qb", None), P(None, "qa", "qb", None), P())
    out_specs = (P(None, "qa", "qb", None), P(None, "qa", "qb", None), P())
    return jax.shard_map(shards, mesh=mesh, in_specs=in_specs, out_specs=out_specs, check_vma=False)
```

```python
import functools

import jax
import jax.numpy as jnp
from jax import lax
from jax.experimental import pallas as pl
from jax.experimental.pallas import tpu as pltpu
from jax.sharding import PartitionSpec as P

AXES = ("qa", "qb")
NN = (((1,), (0,)), ((), ()))
NT = (((1,), (1,)), ((), ()))
TN = (((0,), (0,)), ((), ()))


def contract(left, right, left_dim, right_dim):
    return lax.dot_general(
        left,
        right,
        (((left_dim,), (right_dim,)), ((), ())),
        precision=lax.Precision.HIGHEST,
        preferred_element_type=jnp.float32,
    )


def undo_high(field, gate):
    new_real = contract(gate[0], field[0], 0, 0) + contract(gate[1], field[1], 0, 0)
    new_imag = contract(gate[0], field[1], 0, 0) - contract(gate[1], field[0], 0, 0)
    return jnp.stack([new_real, new_imag])


def undo_low(field, gate):
    new_real = contract(field[0], gate[0], 1, 0) + contract(field[1], gate[1], 1, 0)
    new_imag = contract(field[1], gate[0], 1, 0) - contract(field[0], gate[1], 1, 0)
    return jnp.stack([new_real, new_imag])


def pair_high(adjoint_field, new_field):
    grad_real = contract(adjoint_field[0], new_field[0], 1, 1) + contract(
        adjoint_field[1], new_field[1], 1, 1
    )
    grad_imag = contract(adjoint_field[1], new_field[0], 1, 1) - contract(
        adjoint_field[0], new_field[1], 1, 1
    )
    return jnp.stack([grad_real, grad_imag])


def pair_low(adjoint_field, new_field):
    grad_real = contract(adjoint_field[0], new_field[0], 0, 0) + contract(
        adjoint_field[1], new_field[1], 0, 0
    )
    grad_imag = contract(adjoint_field[1], new_field[0], 0, 0) - contract(
        adjoint_field[0], new_field[1], 0, 0
    )
    return jnp.stack([grad_real, grad_imag])


def stepwise(state, adjoint, gates):
    gate_size = gates.shape[-1]
    local_count = state.shape[-1]
    scaling = float(lax.axis_size("qa") * lax.axis_size("qb") * local_count // gate_size) ** (-0.5)
    state_now = state.reshape(2, local_count)
    adjoint_now = adjoint.reshape(2, local_count)
    collected = []

    def record(term):
        return lax.psum(term, ("qa", "qb"))

    for section in range(gates.shape[0] // 2):
        high_gate = gates[2 * section]
        low_gate = gates[2 * section + 1]
        upright = (2, gate_size, local_count // gate_size)
        state_high = state_now.reshape(upright)
        adjoint_high = adjoint_now.reshape(upright)
        state_new = undo_high(state_high, high_gate)
        collected.append(record(scaling * pair_high(adjoint_high, state_new)))
        adjoint_new = undo_high(adjoint_high, high_gate)
        flat = (2, local_count // gate_size, gate_size)
        state_low = state_new.reshape(flat)
        adjoint_low = adjoint_new.reshape(flat)
        groups = lax.axis_size("qa") if section % 2 == 0 else lax.axis_size("qb")
        state_done = undo_low(state_low, low_gate)
        collected.append(record(scaling * pair_low(adjoint_low, state_done)))
        adjoint_done = undo_low(adjoint_low, low_gate)
        split = (2, groups, local_count // groups)
        outgoing = (state_done.reshape(split), adjoint_done.reshape(split))
        if section % 2 == 0:
            arrived = (
                lax.all_to_all(outgoing[0], "qa", split_axis=1, concat_axis=1, tiled=True),
                lax.all_to_all(outgoing[1], "qa", split_axis=1, concat_axis=1, tiled=True),
            )
        else:
            arrived = (
                lax.all_to_all(outgoing[0], "qb", split_axis=1, concat_axis=1, tiled=True),
                lax.all_to_all(outgoing[1], "qb", split_axis=1, concat_axis=1, tiled=True),
            )
        state_now = arrived[0].reshape(2, local_count)
        adjoint_now = arrived[1].reshape(2, local_count)
    gradients = jnp.stack(collected)
    return (state_now.reshape(state.shape), adjoint_now.reshape(adjoint.shape), gradients)


def split(x):
    high = x.astype(jnp.bfloat16)
    return high, (x - high.astype(jnp.float32)).astype(jnp.bfloat16)


def dot(left, right, dims):
    part = lambda i, j: lax.dot_general(left[i], right[j], dims, preferred_element_type=jnp.float32)
    return (part(0, 1) + part(1, 0)) + part(0, 0)


def each(operation, *arrays):
    return tuple(operation(*parts) for parts in zip(*arrays))


def wide(arrays):
    return jnp.concatenate(arrays, 1)


def tall(arrays):
    return jnp.concatenate(arrays, 0)


def multiply(left, right):
    size = left[0].shape[0]
    both = dot(split(tall(left)), split(wide(right)), NN)
    return (
        both[:size, :size] - both[size:, size:],
        both[:size, size:] + both[size:, :size],
    )


def multiply_adjoint(left, right):
    size = left[0].shape[0]
    both = dot(split(tall((left[0].T, left[1].T))), split(wide(right)), NN)
    return (
        both[:size, :size] + both[size:, size:],
        both[:size, size:] - both[size:, :size],
    )


def undoing(gate):
    real, imag = gate[0].T, gate[1].T
    return split(tall((wide((real, imag)), wide((-imag, real)))))


def paired(both):
    size = both.shape[0] // 2
    return tall((both[:size, :size] + both[size:, size:], both[size:, :size] - both[:size, size:]))


def exchange(parts, width):
    parts = list(parts)
    lanes = parts[0].shape[-1]
    lane = lax.broadcasted_iota(jnp.int32, parts[0].shape, 1)
    step = 1
    while step < len(parts):
        shift = step * width
        lower = (lane // shift) % 2 == 0
        for index in range(len(parts)):
            if index & step == 0:
                one, two = parts[index], parts[index + step]
                parts[index] = jnp.where(lower, one, pltpu.roll(two, shift, 1))
                parts[index + step] = jnp.where(lower, pltpu.roll(one, lanes - shift, 1), two)
        step *= 2
    return parts


def place_of(low):
    along = lax.axis_index("qb")
    within = lax.shift_right_logical(lax.bitwise_and(along, low - 1), 1)
    return lax.bitwise_and(along, 1), lax.axis_index("qa") * (low // 2) + within


def share_out(sums, low, refs, all_ref):
    for index, term in enumerate(sums):
        all_ref[index] = term
    half, within = place_of(low)
    count, rows = refs[0].shape[0], refs[0].shape[1] // len(sums)
    for other, ref in enumerate(refs):
        for mask in range(count):
            chunk = lax.bitwise_xor(half, other) * count + lax.bitwise_xor(within, mask)
            start = pl.multiple_of(chunk * rows, rows)
            for index in range(len(sums)):
                ref[mask, pl.ds(index * rows, rows), :] = all_ref[index, pl.ds(start, rows), :]


def collect(low, refs, all_ref):
    half, within = place_of(low)
    sums, count, rows = all_ref.shape[0], refs[0].shape[0], refs[0].shape[1] // all_ref.shape[0]
    for other, ref in enumerate(refs):
        for mask in range(count):
            chunk = lax.bitwise_xor(half, other) * count + lax.bitwise_xor(within, mask)
            start = pl.multiple_of(chunk * rows, rows)
            for index in range(sums):
                all_ref[index, pl.ds(start, rows), :] = ref[mask, pl.ds(index * rows, rows), :]


def times_gate(both, gate):
    size = both.shape[0] // 2
    term = paired(both)
    return tall(multiply((term[:size], term[size:]), gate))


def rows_low(ref, size):
    mid = ref.shape[1] // size
    return [[split(ref[part, pl.ds(j, size, stride=mid), :]) for part in range(2)] for j in range(mid)]


def rows_high(field):
    return each(
        lambda *a: tall(a), *[each(lambda *b: wide(b), *[row[part] for row in field]) for part in range(2)]
    )


def first_kernel(
    state_hbm, adjoint_hbm, gates_hbm, out_hbm, state_ref, adjoint_ref, gates_ref, out_ref, sem, out_sem
):
    pairs = ((gates_hbm, gates_ref), (state_hbm, state_ref), (adjoint_hbm, adjoint_ref))
    copies = [pltpu.make_async_copy(*pair, sem.at[place]) for place, pair in enumerate(pairs)]
    for copy in copies:
        copy.start()
    size = gates_ref.shape[-1]
    mid = state_ref.shape[1] // size
    total = out_ref.shape[0]
    kept = mid * size // total
    blocks = size // kept
    gate = lambda index: (gates_ref[index, 0], gates_ref[index, 1])

    for copy in copies:
        copy.wait()
    four = multiply(multiply(gate(1), gate(3)), multiply(gate(5), gate(7)))
    undo_low = undoing(four)
    undo_high = undoing(gate(0))
    by_high = [rows_high(rows_low(ref, size)) for ref in (state_ref, adjoint_ref)]
    done = [dot(undo_high, field, NN) for field in by_high]
    copies = []
    for j in range(mid):
        here = slice(j * size, (j + 1) * size)
        rows = tall([wide((field[:size, here], field[size:, here])) for field in done])
        sent = dot(undo_low, split(rows), NT)
        for block in range(blocks):
            for f in range(2):
                for part in range(2):
                    start = part * size + block * kept
                    out_ref[j * blocks + block, pl.ds((f * 2 + part) * kept, kept), :] = sent[
                        start : start + kept, f * size : (f + 1) * size
                    ]
        mine = pl.ds(j * blocks, blocks)
        copies.append(pltpu.make_async_copy(out_ref.at[mine], out_hbm.at[mine], out_sem.at[j]))
        copies[-1].start()
    for copy in copies:
        copy.wait()


def first_sums_kernel(low, state_ref, adjoint_ref, gates_ref, _, own_ref, other_ref, all_ref):
    size = gates_ref.shape[-1]
    fields = [rows_low(ref, size) for ref in (state_ref, adjoint_ref)]
    by_low = [each(lambda *a: tall(a), *[each(lambda *b: wide(b), *row) for row in field]) for field in fields]
    by_high = [rows_high(field) for field in fields]
    sums = [
        paired(dot(by_low[1], by_low[0], TN)),
        times_gate(dot(by_high[1], by_high[0], NT), (gates_ref[0, 0], gates_ref[0, 1])),
    ]
    share_out(sums, low, (own_ref, other_ref), all_ref)


def before_gates(na, got_ref, gates_ref):
    size = gates_ref.shape[-1]
    total = got_ref.shape[0]
    nb = total // na
    inner = nb // na
    tail = size // nb
    kept = size // inner
    gate = lambda index: (gates_ref[index, 0], gates_ref[index, 1])

    fields = []
    for f in range(2):
        parts = []
        for part in range(2):
            start = (f * 2 + part) * kept
            rows = [got_ref[pl.ds(a * nb, nb), pl.ds(start, kept), :].reshape(nb * kept, size) for a in range(na)]
            parts.append(tall(exchange(rows, size // na)))
        fields.append(split(wide(parts)))
    before = [fields]
    undo = undoing(gate(2))
    after = []
    for f in range(2):
        done = dot(undo, fields[f], NT)
        after.append(done)
    lists = []
    for h in range(inner):
        pieces = []
        for f in range(2):
            for block in range(na * na):
                cut = after[f][:, block * size : (block + 1) * size]
                pieces.append(cut.reshape(2 * na, inner, tail, size)[:, h].reshape(2 * na * tail, size))
        lists.append(tall(pieces))
    turned = exchange(lists, kept)
    turned = [item.reshape(2, na, na, 2, na, tail, size) for item in turned]

    fields = []
    for f in range(2):
        columns = []
        for top in range(na):
            for a in range(na):
                rows = [
                    turned[b][f, top, B, part, a]
                    for part in range(2)
                    for B in range(na)
                    for b in range(inner)
                ]
                columns.append(tall(rows))
        fields.append(split(wide(columns)))
    before.append(fields)
    undo = undoing(gate(4))
    after = [dot(undo, field, NN) for field in fields]

    span = inner * tail
    fields = []
    for f in range(2):
        columns = []
        for a in range(na):
            for B in range(na):
                rows = []
                for part in range(2):
                    for top in range(na):
                        row = (part * na + B) * span
                        column = (top * na + a) * size
                        rows.append(after[f][row : row + span, column : column + size])
                columns.append(tall(rows))
        fields.append(split(wide(columns)))
    return before + [fields]


def second_kernel(na, got_ref, gates_ref, _, out_hbm, out_ref, sem):
    size = gates_ref.shape[-1]
    total = got_ref.shape[0]
    inner = total // na // na
    tail = size // (total // na)
    kept = size // inner
    fields = before_gates(na, got_ref, gates_ref)[-1]
    undo = undoing((gates_ref[6, 0], gates_ref[6, 1]))
    copies = []
    for f in range(2):
        done = dot(undo, fields[f], NN)
        for part in range(2):
            for a in range(na):
                for B in range(na):
                    column = (a * na + B) * size
                    for top in range(na):
                        for b in range(inner):
                            row = ((part * na + top) * inner + b) * tail
                            out_ref[
                                (B * na + top) * inner + b,
                                pl.ds(((f * 2 + part) * na + a) * tail, tail),
                                :,
                            ] = done[row : row + tail, column : column + size]
        mine = (slice(None), pl.ds(f * 2 * kept, 2 * kept))
        copies.append(pltpu.make_async_copy(out_ref.at[mine], out_hbm.at[mine], sem.at[f]))
        copies[-1].start()
    for copy in copies:
        copy.wait()


def second_sums_kernel(na, low, got_ref, gates_ref, _, __, own_ref, other_ref, all_ref):
    sums = []
    for place, fields in enumerate(before_gates(na, got_ref, gates_ref)):
        index = 2 * place + 2
        both = dot(fields[1], fields[0], NT if place else TN)
        sums.append(times_gate(both, (gates_ref[index, 0], gates_ref[index, 1])))
    share_out(sums, low, (own_ref, other_ref), all_ref)


def third_kernel(na, nb, got_ref, state_ref, adjoint_ref, token_ref):
    token_ref[...] = jnp.zeros_like(token_ref)
    total, _, size = got_ref.shape
    rest = state_ref.shape[1]
    mid = rest // size
    inner = nb // na
    tail = size // nb
    kept = size // inner
    blocks = total // mid
    for j in range(mid):
        lists = [
            got_ref[j * blocks + block, pl.ds(0, 4 * kept), :] for block in range(blocks)
        ]
        turned = exchange(lists, kept)
        for h in range(inner):
            for f, ref in enumerate((state_ref, adjoint_ref)):
                for part in range(2):
                    for a in range(na):
                        row = ((f * 2 + part) * na + a) * tail
                        ref[part, pl.ds(((a * inner + h) * tail) * mid + j, tail, stride=mid), :] = turned[h][
                            row : row + tail
                        ]


def write(grads, out_hbm, out_ref, sem):
    copies = []
    for place, (index, grad) in enumerate(grads):
        out_ref[place, 0] = grad[0]
        out_ref[place, 1] = grad[1]
        copies.append(pltpu.make_async_copy(out_ref.at[place], out_hbm.at[index], sem.at[place]))
        copies[-1].start()
    for copy in copies:
        copy.wait()


def early_kernel(scaling, low, gates_ref, own_ref, other_ref, out_hbm, token_ref, all_ref, out_ref, sem):
    token_ref[...] = jnp.zeros_like(token_ref)
    size = gates_ref.shape[-1]
    gate = lambda index: (gates_ref[index, 0], gates_ref[index, 1])
    collect(low, (own_ref, other_ref), all_ref)
    sums = lambda place: (all_ref[place, :size] * scaling, all_ref[place, size:] * scaling)
    grads = [(0, sums(1))]
    term = sums(0)
    for index in range(1, gates_ref.shape[0], 2):
        grads.append((index, multiply(term, gate(index))))
        term = multiply_adjoint(gate(index), grads[-1][1])
    write(grads, out_hbm, out_ref, sem)


def late_kernel(scaling, low, own_ref, other_ref, _, __, out_hbm, all_ref, out_ref, sem):
    size = all_ref.shape[-1]
    collect(low, (own_ref, other_ref), all_ref)
    sums = lambda place: (all_ref[place, :size] * scaling, all_ref[place, size:] * scaling)
    write([(2 * place + 2, sums(place)) for place in range(all_ref.shape[0])], out_hbm, out_ref, sem)


def hold_kernel(held_ref, _, out_ref):
    pass


def from_mask(value, mask, total):
    return lax.ppermute(value, AXES, [(device, device ^ mask) for device in range(total)])


def tree(terms):
    while len(terms) > 1:
        terms = [one + two for one, two in zip(terms[::2], terms[1::2])]
    return terms[0]


def reduce_near(own, other, pair, near, total):
    half = own + from_mask(other, pair, total)
    return tree([half[0]] + [from_mask(half[place], mask, total) for place, mask in enumerate(near) if place])


def reduce_far(mine, far, total):
    for mask in far:
        mine = mine + from_mask(mine, mask, total)
    return mine


def gather_near(mine, near, total):
    return jnp.stack([mine] + [from_mask(mine, mask, total) for mask in near[1:]])


def shards(state, adjoint, gates):
    size = gates.shape[-1]
    count = state.shape[-1]
    na, nb = lax.axis_size("qa"), lax.axis_size("qb")
    total = na * nb
    scaling = float(total * count // size) ** (-0.5)
    rest = count // size
    kept = rest // total
    inner, tail = nb // na, size // nb
    if gates.shape[0] != 8 or inner * kept != size or tail != 8:
        return stepwise(state, adjoint, gates)

    low = 1 << ((nb.bit_length() - 1) // 2)
    near = [a * nb + b for a in range(na) for b in range(0, low, 2)]
    far = [1 << bit for bit in range(low.bit_length() - 1, nb.bit_length() - 1)]
    shape = lambda *dims: jax.ShapeDtypeStruct(dims, jnp.float32)
    flat = (2, rest, size)
    chunks = lambda sums: [shape(len(near), sums * size // len(near), size)] * 2
    vmem = pl.BlockSpec(memory_space=pltpu.VMEM)
    hbm = pl.BlockSpec(memory_space=pltpu.HBM)
    buffer = lambda *dims: pltpu.VMEM(dims, jnp.float32)

    def call(kernel, name, out_shape, scratch=(), grant=48 * 2**20, **options):
        return pl.pallas_call(
            kernel,
            out_shape=out_shape,
            scratch_shapes=scratch,
            compiler_params=pltpu.CompilerParams(vmem_limit_bytes=grant),
            name=name,
            **options,
        )

    unread = pl.BlockSpec(memory_space=pl.ANY)

    def hold(array, operand):
        return call(
            hold_kernel,
            "hold",
            shape(*array.shape),
            in_specs=[unread, unread],
            out_specs=unread,
            input_output_aliases={0: 0},
        )(array, operand)

    fields = (state.reshape(flat), adjoint.reshape(flat), gates)
    out = call(
        first_kernel,
        "first",
        shape(total, 4 * kept, size),
        [
            buffer(*flat),
            buffer(*flat),
            buffer(*gates.shape),
            buffer(total, 4 * kept, size),
            pltpu.SemaphoreType.DMA((3,)),
            pltpu.SemaphoreType.DMA((rest // size,)),
        ],
        grant=60 * 2**20,
        in_specs=[hbm, hbm, hbm],
        out_specs=hbm,
    )(*fields)
    early = call(
        functools.partial(first_sums_kernel, low),
        "first_sums",
        chunks(2),
        [buffer(2, 2 * size, size)],
        in_specs=[vmem, vmem, vmem, unread],
    )(*fields, out)
    got = lax.all_to_all(out, AXES, split_axis=0, concat_axis=0, tiled=True)
    early = reduce_far(reduce_near(*early, 1, near, total), far[:-1], total)
    out = call(
        functools.partial(second_kernel, na),
        "second",
        shape(total, 4 * kept, size),
        [buffer(total, 4 * kept, size), pltpu.SemaphoreType.DMA((2,))],
        in_specs=[vmem, vmem, unread],
        out_specs=hbm,
    )(got, gates, early)
    early = reduce_far(early, far[-1:], total)
    late = call(
        functools.partial(second_sums_kernel, na, low),
        "second_sums",
        chunks(3),
        [buffer(3, 2 * size, size)],
        in_specs=[vmem, vmem, unread, unread],
    )(got, gates, out, early)
    got = lax.all_to_all(out, AXES, split_axis=0, concat_axis=0, tiled=True)
    early = gather_near(early, near, total)
    token = shape(8, size)
    grads, early_made = call(
        functools.partial(early_kernel, scaling, low),
        "early",
        (shape(*gates.shape), token),
        [buffer(2, 2 * size, size), buffer(5, 2, size, size), pltpu.SemaphoreType.DMA((5,))],
        in_specs=[vmem, vmem, vmem],
        out_specs=[hbm, vmem],
    )(gates, early, from_mask(early, 1, total))
    state_out, adjoint_out, fields_made = call(
        functools.partial(third_kernel, na, nb), "third", (shape(*flat), shape(*flat), token)
    )(got)
    late = reduce_far(reduce_near(*late, 1, near, total), far[:-1], total)
    late = reduce_far(hold(late, early_made), far[-1:], total)
    late = gather_near(late, near, total)
    grads = call(
        functools.partial(late_kernel, scaling, low),
        "late",
        shape(*gates.shape),
        [buffer(3, 2 * size, size), buffer(3, 2, size, size), pltpu.SemaphoreType.DMA((3,))],
        in_specs=[vmem, vmem, hbm, unread],
        out_specs=hbm,
        input_output_aliases={2: 0},
    )(late, from_mask(late, 1, total), grads, fields_made)
    return state_out.reshape(state.shape), adjoint_out.reshape(adjoint.shape), grads


def solution(mesh):
    in_specs = (P(None, "qa", "qb", None), P(None, "qa", "qb", None), P())
    out_specs = (P(None, "qa", "qb", None), P(None, "qa", "qb", None), P())
    return jax.shard_map(shards, mesh=mesh, in_specs=in_specs, out_specs=out_specs, check_vma=False)
```
